128 devices in a mesh: sub: 32 (over x, y, core), coarse: 4 (over z).
Axes of the slice: x: 4, y: 4, z: 4, core: 2. Of those that a mesh axis runs over, the one named last changes fastest.
Arguments:
- load: float32 [256, 6, 128, 256], P(('sub', 'coarse')), may hold values from -6 to 6
- schur: float32 [256, 768, 768], P(('sub', 'coarse')), as said below
- schur_inverse: float32 [256, 768, 768], P(('sub', 'coarse')), as said below
- basis: float32 [256, 768, 24], P(('sub', 'coarse')), may hold values from -1.25 to 1.25
- coarse_inverse: float32 [3584, 3584], P('coarse'), as said below
- partner_slot: int32 [256, 6], P(('sub', 'coarse')), may hold values from -1 to 1535, as said below
- edge_map: int32 [256, 6, 128], P(('sub', 'coarse')), may hold values from 0 to 127, as said below
- coarse_number: int32 [256, 6], P(('sub', 'coarse')), may hold values from 0 to 895, as said below
Outputs:
- solution: float32 [256, 6, 128, 256], P(('sub', 'coarse'))
- residual_next: float32 [256, 6, 128, 256], P(('sub', 'coarse'))
- direction_next: float32 [256, 6, 128, 256], P(('sub', 'coarse'))
The draws below stay inside these ranges and needn't reach their ends.
Inputs may be any that keep to these rules, and one draw needn't show every extreme that they name: `partner_slot`: pairs are mutual: if face f of subdomain s names face g of subdomain t, then face g of t names face f of s. Each subdomain has exactly one face paired with a subdomain on the next device along sub+coarse and exactly one paired with a subdomain on the previous device, the first and last devices counting as adjacent; its other faces pair with subdomains on its own device or lie on the outer boundary. `edge_map`: on each paired face the two edge maps are permutations of 0 to 127 and inverse to each other. `coarse_number`: both sides of a paired face carry the same number; every number is used. `schur`: each matrix is symmetric positive definite. `schur_inverse`: each matrix is symmetric positive definite. `coarse_inverse`: symmetric positive definite.
All inputs are finite; a program needn't handle non-finite values.
Results may differ from the reference program's by a relative error of at most 0.00022.
Values sent between devices are 32-bit elements; how exact they have to be, the bound alone decides.
A program may use at most 128 MiB of HBM per device.

```python
import jax
import jax.numpy as jnp
from jax import lax

F = 6
E = 128
NCF = 4
S_DEV = 2
NRHS = 256
NI = 768
NCL = 24
ND = 128
NS = 256
NFACE = 896
NC0 = 3584


def layout(key):
    key_list = jax.random.split(key, 5)
    roles = jax.vmap(lambda sub_key: jax.random.permutation(sub_key, F))(jax.random.split(key_list[0], NS)).astype(jnp.int32)
    first_role = roles[:, 0]
    last_role = roles[:, F - 1]
    swapped = last_role == 1
    roles = roles.at[:, 0].set(jnp.where(swapped, last_role, first_role))
    roles = roles.at[:, F - 1].set(jnp.where(swapped, first_role, last_role))
    sub_ids = jnp.arange(NS, dtype=jnp.int32)
    device = sub_ids // S_DEV
    position = sub_ids % S_DEV
    crossing = jax.vmap(lambda sub_key: jax.random.permutation(sub_key, S_DEV))(jax.random.split(key_list[1], ND)).astype(jnp.int32)
    crossing_back = jnp.argsort(crossing, axis=1).astype(jnp.int32)
    next_device = (device + 1) % ND
    prev_device = (device + ND - 1) % ND
    up_mate = next_device * S_DEV + crossing[device, position]
    down_mate = prev_device * S_DEV + crossing_back[prev_device, position]
    shuffles = jax.vmap(lambda sub_key: jax.random.permutation(sub_key, 4 * S_DEV))(jax.random.split(key_list[2], ND)).astype(jnp.int32)
    item_range = jnp.arange(4 * S_DEV, dtype=jnp.int32)
    flipped = shuffles[:, item_range ^ 1]
    paired = item_range < 4 * S_DEV - 2
    flipped = jnp.where(paired[None, :], flipped, -1)

    def mate_table(shuffle, flip):
        return jnp.zeros(4 * S_DEV, jnp.int32).at[shuffle].set(flip)
    mates = jax.vmap(mate_table)(shuffles, flipped)
    item_ids = position[:, None] * 4 + jnp.arange(4, dtype=jnp.int32)[None, :]
    local_mate = mates[device[:, None], item_ids]
    local_valid = local_mate >= 0
    local_mate = jnp.maximum(local_mate, 0)
    local_sub = device[:, None] * S_DEV + local_mate // 4
    local_role = 2 + local_mate % 4
    mate_sub = jnp.concatenate([down_mate[:, None], up_mate[:, None], local_sub], axis=1)
    mate_role = jnp.concatenate([jnp.ones((NS, 1), jnp.int32), jnp.zeros((NS, 1), jnp.int32), local_role], axis=1)
    valid = jnp.concatenate([jnp.ones((NS, 2), bool), local_valid], axis=1)
    mate_sub = jnp.where(valid, mate_sub, 0)
    by_role = jnp.where(valid, mate_sub * F + roles[mate_sub, mate_role], -1).astype(jnp.int32)
    partner = jnp.zeros((NS, F), jnp.int32).at[sub_ids[:, None], roles].set(by_role)
    own_slot = sub_ids[:, None] * F + jnp.arange(F, dtype=jnp.int32)[None, :]
    leading = (partner < 0) | (own_slot < partner)
    face_rank = (jnp.cumsum(leading.reshape(-1).astype(jnp.int32)) - 1).astype(jnp.int32)
    relabel = jax.random.permutation(key_list[3], NFACE).astype(jnp.int32)
    chosen_slot = jnp.where(leading, own_slot, partner)
    face_id = relabel[face_rank[chosen_slot.reshape(-1)]].reshape(NS, F)
    edge_perms = jax.vmap(lambda sub_key: jax.random.permutation(sub_key, E))(jax.random.split(key_list[4], NFACE)).astype(jnp.int32)
    edge_backs = jnp.argsort(edge_perms, axis=1).astype(jnp.int32)
    edge_table = jnp.where(leading[:, :, None], edge_perms[face_id], edge_backs[face_id])
    return (partner, edge_table, face_id)


def dominant(key, blocks, order, spread):
    places = jnp.arange(order, dtype=jnp.float32)
    distance = jnp.abs(places[:, None] - places[None, :])
    coupling = jnp.exp(distance * (-1.0 / 6.0))

    def one_block(block_index):
        sub_key = jax.random.fold_in(key, block_index)
        key_list = jax.random.split(sub_key, 3)
        raw_entries = jax.random.uniform(key_list[0], (order, order), jnp.float32, -1.0, 1.0)
        symmetric = (raw_entries + raw_entries.T) * (1.25 / order)
        diagonal = jax.random.uniform(key_list[1], (order,), jnp.float32, 2.6, 5.2)
        row_scales = jnp.exp(0.5 * jax.random.uniform(key_list[2], (order,), jnp.float32, 0.0, 1.0) * jnp.log(spread))
        identity = jnp.eye(order, dtype=jnp.float32)
        matrix = symmetric * (1.0 - identity) + identity * diagonal[:, None] + coupling
        return matrix * row_scales[:, None] * row_scales[None, :]
    return lax.map(one_block, jnp.arange(blocks))


def draw_partner_slot(key, part):
    partner, edge_table, face_id = layout(key)
    return partner


def draw_edge_map(key, part):
    partner, edge_table, face_id = layout(key)
    return edge_table


def draw_coarse_number(key, part):
    partner, edge_table, face_id = layout(key)
    return face_id


def draw_schur(key, part):
    key = jax.random.fold_in(key, 11)
    return dominant(key, NS, NI, 2.0)


def draw_schur_inverse(key, part):
    key = jax.random.fold_in(key, 12)
    return dominant(key, NS, NI, 2.0)


def draw_coarse_inverse(key, part):
    key = jax.random.fold_in(key, 13)
    return dominant(key, 1, NC0, 2.0)[0]


def shard_levels(rng, dims, cuts, least, largest):
    factor_of, own = 1.0, jax.random.fold_in(rng, 6)
    for dim, shards_of in cuts:
        heights = jnp.exp(jax.random.uniform(jax.random.fold_in(own, dim), (shards_of,), jnp.float32, least / len(cuts), largest / len(cuts)))
        factor_of = factor_of * jnp.repeat(heights, dims[dim] // shards_of).reshape([-1 if axis == dim else 1 for axis in range(len(dims))])
    return factor_of


def normal_values(own_key, shape, deviation, reach, pieces=(), held_as=jnp.bfloat16):
    entries = jax.random.normal(own_key, shape, jnp.float32) * deviation
    if len(pieces) > 0:
        entries = shard_levels(own_key, shape, pieces, -0.22, 0.18) * entries
    return jnp.clip(entries, min=-reach, max=reach).astype(held_as)


def setup_inputs(seed: int = 0) -> dict:
    streams_of = jax.random.split(jax.random.key(seed), 9)
    return {
        "load": normal_values(streams_of[0], (NS, F, E, NRHS), 1.0, 6.0, ((0, 128),), jnp.float32),
        "schur": draw_schur(jax.random.fold_in(streams_of[8], 71), 0),
        "schur_inverse": draw_schur_inverse(jax.random.fold_in(streams_of[8], 71), 0),
        "basis": normal_values(streams_of[3], (NS, NI, NCL), NCL ** -0.5, 1.25, ((0, 128),), jnp.float32),
        "coarse_inverse": draw_coarse_inverse(jax.random.fold_in(streams_of[8], 71), 0),
        "partner_slot": draw_partner_slot(jax.random.fold_in(streams_of[8], 71), 0),
        "edge_map": draw_edge_map(jax.random.fold_in(streams_of[8], 71), 0),
        "coarse_number": draw_coarse_number(jax.random.fold_in(streams_of[8], 71), 0),
    }


def assemble(local_part, partner_slot, edge_map):
    flat_pool = local_part.reshape(NS * F * E, NRHS)
    flat_index = (jnp.maximum(partner_slot, 0)[:, :, None] * E + edge_map).reshape(-1)
    partner_part = flat_pool[flat_index].reshape(local_part.shape)
    present = (partner_slot >= 0).astype(jnp.float32)[:, :, None, None]
    return local_part + present * partner_part


def inner(left, right, weight):
    return jnp.sum(weight[:, :, None, None] * left * right, axis=(0, 1, 2))


def precondition(vector, weight, schur_inverse, basis, coarse_inverse, coarse_dofs, partner_slot, edge_map):
    scaled = (weight[:, :, None, None] * vector).reshape(NS, NI, NRHS)
    local_part = jnp.einsum("snm,smr->snr", schur_inverse, scaled, precision=lax.Precision.HIGHEST)
    coarse_local = jnp.einsum("snc,snr->scr", basis, scaled, precision=lax.Precision.HIGHEST)
    coarse_load = jnp.zeros((NC0, NRHS), jnp.float32).at[coarse_dofs.reshape(-1)].add(coarse_local.reshape(-1, NRHS))
    solved = jnp.dot(coarse_inverse, coarse_load, precision=lax.Precision.HIGHEST)
    coarse_part = jnp.einsum("snc,scr->snr", basis, solved[coarse_dofs], precision=lax.Precision.HIGHEST)
    combined = (local_part + coarse_part).reshape(NS, F, E, NRHS)
    return assemble(weight[:, :, None, None] * combined, partner_slot, edge_map)


def reference(load, schur, schur_inverse, basis, coarse_inverse, partner_slot, edge_map, coarse_number):
    weight = jnp.where(partner_slot >= 0, 0.5, 1.0).astype(jnp.float32)
    coarse_dofs = (coarse_number[:, :, None] * NCF + jnp.arange(NCF, dtype=jnp.int32)[None, None, :]).reshape(NS, NCL).astype(jnp.int32)
    residual = assemble(load, partner_slot, edge_map)
    direction = precondition(residual, weight, schur_inverse, basis, coarse_inverse, coarse_dofs, partner_slot, edge_map)
    rz_first = inner(residual, direction, weight)
    product = jnp.einsum("snm,smr->snr", schur, direction.reshape(NS, NI, NRHS), precision=lax.Precision.HIGHEST)
    image = assemble(product.reshape(NS, F, E, NRHS), partner_slot, edge_map)
    alpha = rz_first / inner(direction, image, weight)
    solution = alpha * direction
    residual_next = residual - alpha * image
    preconditioned = precondition(residual_next, weight, schur_inverse, basis, coarse_inverse, coarse_dofs, partner_slot, edge_map)
    beta = inner(residual_next, preconditioned, weight) / rz_first
    direction_next = preconditioned + beta * direction
    return solution, residual_next, direction_next
```

```python
import functools

import jax
import jax.numpy as jnp
from jax import lax
from jax.experimental import pallas as pl
from jax.experimental.pallas import tpu as pltpu
from jax.sharding import PartitionSpec as P

MESH = pl.DeviceIdType.MESH
F32 = jnp.float32
BF16 = jnp.bfloat16
FACES = 6
SUBS = 2
SLOTS = FACES * SUBS
NCF = 4
LANES = 128
CG = 8


def split(x):
    hi = x.astype(BF16)
    return hi, (x - hi.astype(F32)).astype(BF16)


def dot(a, b):
    return jnp.dot(a, b, preferred_element_type=F32)


def kernel(
    Q, Z, load, schur, sinv, basis_t, coarse, ps, em, cn,
    out_sol, out_r1, out_dn,
    vld, res, loc, dirn, prod, img, pre,
    hs0, hs1, hs2, hs3, hr0, hr1, hr2, hr3,
    sinv_hi, sinv_lo, schur_hi, schur_lo, c_hi, c_lo, s_stage, c_stage,
    hh, hl, perm, bt_hi, bt_lo, bcol, sp, spt,
    scat, gath, xbuf, xt, yt, xm, xb, y2,
    qb, qr, zb, zr, ob, zs0, zs1, arb, arr, arz0, arz1, cnz,
    in_sem, st_sem, ct_sem, out_sem, q_send, q_recv, h_send, h_recv,
):
    q = lax.axis_index("sub")
    z = lax.axis_index("coarse")
    E = vld.shape[1]
    NR = vld.shape[2]
    ZQ = Z * Q
    NCZ = c_hi.shape[0]
    NC0 = c_hi.shape[1]
    NF = NC0 // NCF
    NFZ = NF // Z
    RR = SLOTS * NCF * CG // LANES
    ndev = Q * Z
    me = q * Z + z
    nxt = lax.rem(me + 1, ndev)
    prv = lax.rem(me + ndev - 1, ndev)
    nxt_id = (nxt // Z, lax.rem(nxt, Z))
    prv_id = (prv // Z, lax.rem(prv, Z))

    def q_peer(k):
        return lax.rem(q + k, Q)

    def z_peer(k):
        return lax.rem(z + k, Z)

    load_copy = pltpu.make_async_copy(load, vld, in_sem)
    load_copy.start()

    def stager(src, rows, stage, sem):
        def copy(i, slot):
            return pltpu.make_async_copy(
                src.at[pl.ds(pl.multiple_of(i * rows, rows), rows), :], stage.at[slot], sem.at[slot]
            )
        return copy

    s_rows = s_stage.shape[1]
    c_rows = c_stage.shape[1]
    sinv_copy = stager(sinv, s_rows, s_stage, st_sem)
    schur_copy = stager(schur, s_rows, s_stage, st_sem)
    c_copy = stager(coarse, c_rows, c_stage, ct_sem)

    def first(copy):
        copy(0, 0).start()
        copy(1, 1).start()

    def convert(copy, stage, n, rows, hi_ref, lo_ref):
        def body(i, carry):
            slot = lax.rem(i, 2)
            copy(i, slot).wait()
            hi, lo = split(stage[slot])
            at = pl.ds(pl.multiple_of(i * rows, rows), rows)
            hi_ref[at, :] = hi
            lo_ref[at, :] = lo

            @pl.when(i + 2 < n)
            def _():
                copy(i + 2, slot).start()
            return carry
        lax.fori_loop(0, n, body, 0)

    first(sinv_copy)
    first(c_copy)

    barrier = pltpu.get_barrier_semaphore()

    def greet(device):
        pl.semaphore_signal(barrier, inc=1, device_id=device, device_id_type=MESH)

    lax.fori_loop(1, Q, lambda k, c: (greet((q_peer(k), z)), c)[1], 0)
    for k in range(1, Z):
        greet((q, z_peer(k)))
    greet(nxt_id)
    greet(prv_id)
    pl.semaphore_wait(barrier, Q + Z)

    lane8 = lax.broadcasted_iota(jnp.int32, (8, LANES), 1)

    def q_start(ph, src, dst, shared=False):
        def body(k, carry):
            p = q_peer(k)
            block = src if shared else src.at[pl.ds(pl.multiple_of(p * 8, 8), 8), :]
            pltpu.make_async_remote_copy(
                src_ref=block,
                dst_ref=dst.at[pl.ds(pl.multiple_of(q * 8, 8), 8), :],
                send_sem=q_send.at[ph], recv_sem=q_recv.at[ph],
                device_id=(p, z), device_id_type=MESH,
            ).start()
            return carry
        lax.fori_loop(1, Q, body, 0)
        mine = pl.ds(pl.multiple_of(q * 8, 8), 8)
        dst[mine, :] = src[...] if shared else src[mine, :]

    def q_wait(ph, dst, sems):
        every = dst.at[pl.ds(0, (Q - 1) * 8), :]
        pltpu.make_async_copy(every, every, sems.at[ph]).wait()

    def z_start(ph, src_of, dst):
        for k in range(1, Z):
            t = z_peer(k)
            pltpu.make_async_remote_copy(
                src_ref=src_of(t), dst_ref=dst,
                send_sem=q_send.at[ph], recv_sem=q_recv.at[ph],
                device_id=(q, t), device_id_type=MESH,
            ).start()

    def z_wait(ph, three, sems):
        pltpu.make_async_copy(three, three, sems.at[ph]).wait()

    row = jnp.zeros((8, LANES), F32)
    for k in range(SLOTS):
        row = jnp.where(lane8 == k, cn[k // FACES, k % FACES].astype(F32), row)
    arb[0] = row
    q_start(0, arb.at[0], arr.at[0], shared=True)

    def rel_of(k):
        p = ps[k // FACES, lax.rem(k, FACES)]
        rel = p - me * SLOTS
        rel = jnp.where(rel < -SLOTS, rel + ndev * SLOTS, rel)
        rel = jnp.where(rel >= 2 * SLOTS, rel - ndev * SLOTS, rel)
        return p, rel

    def weight_of(k):
        return jnp.where(ps[k // FACES, lax.rem(k, FACES)] >= 0, jnp.float32(0.5), jnp.float32(1.0))

    ups, downs = [], []
    for s in range(SUBS):
        up = jnp.int32(0)
        down = jnp.int32(0)
        for f in range(FACES):
            p, rel = rel_of(s * FACES + f)
            here = p >= 0
            up = jnp.where(here & (rel >= SLOTS), s * FACES + f, up)
            down = jnp.where(here & (rel < 0), s * FACES + f, down)
        ups.append(up)
        downs.append(down)

    def halo_start(h, v, send, recv):
        for s in range(SUBS):
            send[s] = v[ups[s]]
            send[SUBS + s] = v[downs[s]]
        for way, device in ((0, nxt_id), (1, prv_id)):
            part = pl.ds(way * SUBS, SUBS)
            pltpu.make_async_remote_copy(
                src_ref=send.at[part], dst_ref=recv.at[part],
                send_sem=h_send.at[h, way], recv_sem=h_recv.at[h, way],
                device_id=device, device_id_type=MESH,
            ).start()

    def halo_wait(h, recv, sems):
        for way in range(2):
            part = recv.at[pl.ds(way * SUBS, SUBS)]
            pltpu.make_async_copy(part, part, sems.at[h, way]).wait()

    def partner(k, v, recv):
        p, rel = rel_of(k)
        local = (rel >= 0) & (rel < SLOTS)
        inside = jnp.clip(rel, 0, SLOTS - 1)
        below = (rel + SLOTS >= FACES).astype(jnp.int32)
        above = SUBS + (rel - SLOTS >= FACES).astype(jnp.int32)
        outside = jnp.clip(jnp.where(rel < 0, below, above), 0, 2 * SUBS - 1)
        val = jnp.where(local, v[inside], recv[outside])
        hi, lo = split(val)
        return dot(perm[k], jnp.concatenate([hi, lo], axis=0))

    load_copy.wait()
    halo_start(0, vld, hs0, hr0)

    rows_e = lax.broadcasted_iota(jnp.int32, (E, E), 0)
    for k in range(SLOTS):
        line = em[k % FACES, pl.ds(k // FACES, 1), :]
        one = jnp.where(rows_e == line, jnp.float32(1.0), jnp.float32(0.0)).T
        one = jnp.where(ps[k // FACES, k % FACES] >= 0, one, jnp.zeros_like(one)).astype(BF16)
        perm[k] = jnp.concatenate([one, one], axis=1)

    NI = FACES * E
    NCL = FACES * NCF
    zrow = jnp.zeros((32 - NCL, NI), F32)
    for s in range(SUBS):
        b = basis_t[s]
        bh = b.astype(BF16).astype(F32)
        bl = b - bh
        bh = jnp.concatenate([bh, zrow], axis=0)
        bl = jnp.concatenate([bl, zrow], axis=0)
        bt_hi[s] = bh.astype(BF16)
        bt_lo[s] = bl.astype(BF16)
        bcol[s] = jnp.concatenate([bh, bh, bl, jnp.zeros_like(bl)], axis=0).T.astype(BF16)

    wide = RR * LANES
    i0 = lax.broadcasted_iota(jnp.int32, (wide, CG * LANES), 0)
    i1 = lax.broadcasted_iota(jnp.int32, (wide, CG * LANES), 1)
    target = (i0 & 7) * LANES + (i0 >> 7) * 16 + ((i0 & 127) >> 3)
    sp[...] = jnp.where(i1 == target, jnp.float32(1.0), jnp.float32(0.0)).astype(BF16)
    j0 = lax.broadcasted_iota(jnp.int32, (CG * LANES, wide), 0)
    j1 = lax.broadcasted_iota(jnp.int32, (CG * LANES, wide), 1)
    back = (j1 & 7) * LANES + (j1 >> 7) * 16 + ((j1 & 127) >> 3)
    spt[...] = jnp.where(j0 == back, jnp.float32(1.0), jnp.float32(0.0)).astype(BF16)

    q_wait(0, arr.at[0], q_recv)
    zmine = pl.ds(pl.multiple_of(z * Q, Q), Q)
    arz0[...] = arr[0, pl.ds(0, Q, stride=8), :]
    cnz[zmine, :] = arz0[...]
    z_start(1, lambda t: arz0, cnz.at[zmine, :])

    convert(sinv_copy, s_stage, SUBS * NI // s_rows, s_rows, sinv_hi, sinv_lo)
    first(schur_copy)

    z_wait(1, cnz.at[pl.ds(0, (Z - 1) * Q), :], q_recv)
    cns = cnz[...]
    cnt = cns.T if ZQ == LANES else jnp.concatenate([cns, jnp.zeros((LANES - ZQ, LANES), F32)], axis=0).T
    face0 = lax.broadcasted_iota(jnp.int32, (NF, ZQ), 0).astype(F32)
    face1 = lax.broadcasted_iota(jnp.int32, (ZQ, NFZ), 1).astype(F32) + (z * NFZ).astype(F32)
    for k in range(SLOTS):
        scat[:, k * ZQ:(k + 1) * ZQ] = jnp.where(
            face0 == cnt[k:k + 1, :ZQ], jnp.float32(1.0), jnp.float32(0.0)
        ).astype(BF16)
        gath[k] = jnp.where(
            cns[:, k:k + 1] == face1, jnp.float32(1.0), jnp.float32(0.0)
        ).astype(BF16)

    xbuf[...] = jnp.zeros_like(xbuf)

    def weigh(r_ref):
        def body(k, carry):
            hi, lo = split(weight_of(k) * r_ref[k])
            at = pl.ds(pl.multiple_of(k * E, E), E)
            hh[at, :] = hi
            hl[at, :] = lo
            return carry
        lax.fori_loop(0, SLOTS, body, 0)

    def local_mul(a_hi, a_lo, out):
        rows = 2 * E
        per = NI // rows

        def body(i, carry):
            at = pl.ds(pl.multiple_of(i * rows, rows), rows)
            sub = pl.ds(pl.multiple_of((i // per) * NI, NI), NI)
            hi = a_hi[at, :]
            top = hh[sub, :]
            acc = dot(hi, top) + dot(hi, hl[sub, :]) + dot(a_lo[at, :], top)
            out[2 * i] = acc[:E]
            out[2 * i + 1] = acc[E:]
            return carry
        lax.fori_loop(0, SUBS * per, body, 0)

    def forward_start(n):
        for s in range(SUBS):
            sub = pl.ds(s * NI, NI)
            top = hh[sub, :]
            x = dot(bt_hi[s], top) + dot(bt_hi[s], hl[sub, :]) + dot(bt_lo[s], top)
            xbuf[s * NCL:(s + 1) * NCL, :] = x[:NCL]
        xt[...] = xbuf[...].T
        acc = jnp.zeros((2 * Q, wide), F32)
        for c in range(CG):
            part = xt[pl.ds(c, Q, stride=CG), :]
            hi = part.astype(BF16).astype(F32)
            both = jnp.concatenate([hi, part - hi], axis=0).astype(BF16)
            acc += dot(both, spt[c * LANES:(c + 1) * LANES, :])
        acc = acc[:Q] + acc[Q:]
        b = qb.at[n]
        for r in range(RR):
            b[pl.ds(r, Q, stride=8), :] = acc[:, r * LANES:(r + 1) * LANES]
        for r in range(RR, 8):
            b[pl.ds(r, Q, stride=8), :] = jnp.zeros((Q, LANES), F32)
        q_start(2 + 4 * n, b, qr.at[n])

    def gather_start(n):
        q_wait(2 + 4 * n, qr.at[n], q_recv)
        for r in range(RR):
            part = qr[n, pl.ds(r, Q, stride=8), :]
            zb[n, r] = part
            zr[n, r, zmine, :] = part
        z_start(3 + 4 * n, lambda t: zb.at[n], zr.at[n, :, zmine, :])

    def coarse_product(n):
        z_wait(3 + 4 * n, zr.at[n, :, pl.ds(0, (Z - 1) * Q), :], q_recv)
        la = lax.broadcasted_iota(jnp.int32, (ZQ, LANES), 1) >> 5
        pieces = []
        for r in range(RR):
            part = zr[n, r]
            for a in range(NCF):
                hi, lo = split(jnp.where(la == a, part, jnp.float32(0.0)))
                pieces.append(jnp.concatenate([hi, lo], axis=1))
        slots = jnp.concatenate(pieces, axis=0)
        fb = NF // 7
        fa = lax.broadcasted_iota(jnp.int32, (fb, LANES), 1)

        def spread(i, carry):
            acc = dot(scat[pl.ds(pl.multiple_of(i * fb, fb), fb), :], slots)
            x = acc[:, :LANES] + acc[:, LANES:]
            x = x + pltpu.roll(x, 64, 1)
            x = x + pltpu.roll(x, 32, 1)
            hi = x.astype(BF16).astype(F32)
            v = jnp.where((fa >> 5) == 0, hi, jnp.where((fa >> 5) == 1, x - hi, jnp.float32(0.0)))
            for j in range(NCF):
                xm[pl.ds(j, fb, stride=NCF), :] = jnp.where(((fa >> 3) & 3) == j, v, jnp.float32(0.0))
            rows = pl.ds(pl.multiple_of(i * fb * NCF, fb * NCF), fb * NCF)
            xb[rows, :] = xm[...].astype(BF16)
            return carry
        lax.fori_loop(0, 7, spread, 0)
        yb = NCZ // 7

        def product(i, carry):
            rows = pl.ds(pl.multiple_of(i * yb, yb), yb)
            y = dot(c_hi[rows, :], xb[...]) + dot(c_lo[rows, :], xb[...])
            for shift in (64, 32, 16, 8):
                y = y + pltpu.roll(y, shift, 1)
            y2[rows, :] = y
            return carry
        lax.fori_loop(0, 7, product, 0)
        fj = (lax.broadcasted_iota(jnp.int32, (NFZ, LANES), 1) >> 3) & 3
        y = jnp.zeros((NFZ, LANES), F32)
        for j in range(NCF):
            y = jnp.where(fj == j, y2[pl.ds(j, NFZ, stride=NCF), :], y)
        hi, lo = split(y)
        both = jnp.concatenate([hi, lo], axis=1)
        for r in range(RR):
            o = jnp.zeros((ZQ, LANES), F32)
            for a in range(NCF):
                g = dot(gath[NCF * r + a], both)
                o = jnp.where(la == a, g[:, :LANES] + g[:, LANES:], o)
            ob[n, r] = o
        zs = (zs0, zs1)[n]
        zs[z] = ob[n, :, zmine, :]
        z_start(
            4 + 4 * n,
            lambda t: ob.at[n, :, pl.ds(pl.multiple_of(t * Q, Q), Q), :],
            zs.at[z],
        )

    def backward_start(n):
        zs = (zs0, zs1)[n]
        z_wait(4 + 4 * n, zs.at[pl.ds(0, Z - 1)], q_recv)
        b = qb.at[2 + n]
        for r in range(RR):
            tot = zs[0, r]
            for t in range(1, Z):
                tot = tot + zs[t, r]
            b[pl.ds(r, Q, stride=8), :] = tot
        for r in range(RR, 8):
            b[pl.ds(r, Q, stride=8), :] = jnp.zeros((Q, LANES), F32)
        q_start(5 + 4 * n, b, qr.at[2 + n])

    def backward_finish(n):
        q_wait(5 + 4 * n, qr.at[2 + n], q_recv)
        acc = jnp.zeros((2 * Q, CG * LANES), F32)
        for r in range(RR):
            part = qr[2 + n, pl.ds(r, Q, stride=8), :]
            hi = part.astype(BF16).astype(F32)
            both = jnp.concatenate([hi, part - hi], axis=0).astype(BF16)
            acc += dot(both, sp[r * LANES:(r + 1) * LANES, :])
        for c in range(CG):
            cols = slice(c * LANES, (c + 1) * LANES)
            yt[pl.ds(c, Q, stride=CG), :] = acc[:Q, cols] + acc[Q:, cols]
        return yt[...].T

    def add_coarse(y):
        pad = jnp.zeros((32 - NCL, NR), F32)
        for s in range(SUBS):
            ys = jnp.concatenate([y[s * NCL:(s + 1) * NCL], pad], axis=0)
            hi = ys.astype(BF16).astype(F32)
            lo = ys - hi
            cols = jnp.concatenate([hi, lo, hi, jnp.zeros_like(hi)], axis=0).astype(BF16)

            def body(f, carry):
                k = s * FACES + f
                at = pl.ds(pl.multiple_of(f * E, E), E)
                loc[k] = weight_of(k) * (loc[k] + dot(bcol[s, at, :], cols))
                return carry
            lax.fori_loop(0, FACES, body, 0)

    def fold(x):
        return x.reshape(E // 8, 8, NR).sum(axis=0)

    nh = max(1, NR // LANES)
    lw = min(NR, LANES)

    def sums_start(n, parts):
        b = arb.at[1 + n]
        b[...] = jnp.zeros((8, LANES), F32)
        for i, part in enumerate(parts):
            line = part.sum(axis=0, keepdims=True)
            for h in range(nh):
                b[pl.ds(i * nh + h, 1), 0:lw] = line[:, h * lw:(h + 1) * lw]
        q_start(10 + 2 * n, b, arr.at[1 + n], shared=True)

    def sums_finish(n, count):
        q_wait(10 + 2 * n, arr.at[1 + n], q_recv)
        tot = arr[1 + n].reshape(Q, 8, LANES).sum(axis=0)
        dst = (arz1.at[0], arz1.at[1])[n]
        arb[3 + n] = tot
        dst[z] = tot
        z_start(11 + 2 * n, lambda t: arb.at[3 + n], dst.at[z])
        z_wait(11 + 2 * n, dst.at[pl.ds(0, Z - 1)], q_recv)
        tot = dst[0]
        for t in range(1, Z):
            tot = tot + dst[t]
        return [
            jnp.concatenate([tot[i * nh + h:i * nh + h + 1, :lw] for h in range(nh)], axis=1)
            for i in range(count)
        ]

    zero8 = jnp.zeros((8, NR), F32)

    halo_wait(0, hr0, h_recv)

    def residual(k, carry):
        res[k] = vld[k] + partner(k, vld, hr0)
        return carry
    lax.fori_loop(0, SLOTS, residual, 0)

    weigh(res)
    forward_start(0)
    local_mul(sinv_hi, sinv_lo, loc)
    gather_start(0)
    convert(c_copy, c_stage, NCZ // c_rows, c_rows, c_hi, c_lo)
    coarse_product(0)
    convert(schur_copy, s_stage, SUBS * NI // s_rows, s_rows, schur_hi, schur_lo)
    backward_start(0)
    add_coarse(backward_finish(0))
    halo_start(1, loc, hs1, hr1)
    halo_wait(1, hr1, h_recv)

    def direction(k, acc):
        d = loc[k] + partner(k, loc, hr1)
        dirn[k] = d
        hi, lo = split(d)
        at = pl.ds(pl.multiple_of(k * E, E), E)
        hh[at, :] = hi
        hl[at, :] = lo
        return acc + fold(weight_of(k) * res[k] * d)
    rz_part = lax.fori_loop(0, SLOTS, direction, zero8)

    local_mul(schur_hi, schur_lo, prod)
    halo_start(2, prod, hs2, hr2)
    halo_wait(2, hr2, h_recv)

    def image(k, acc):
        m = prod[k] + partner(k, prod, hr2)
        img[k] = m
        return acc + fold(weight_of(k) * dirn[k] * m)
    da_part = lax.fori_loop(0, SLOTS, image, zero8)
    sums_start(0, [rz_part, da_part])
    rz, da = sums_finish(0, 2)
    alpha = rz / da

    def step(k, carry):
        vld[k] = alpha * dirn[k]
        res[k] = res[k] - alpha * img[k]
        return carry
    lax.fori_loop(0, SLOTS, step, 0)
    sol_copy = pltpu.make_async_copy(vld, out_sol, out_sem.at[0])
    sol_copy.start()
    r1_copy = pltpu.make_async_copy(res, out_r1, out_sem.at[1])
    r1_copy.start()

    weigh(res)
    forward_start(1)
    local_mul(sinv_hi, sinv_lo, loc)
    gather_start(1)
    coarse_product(1)
    backward_start(1)
    add_coarse(backward_finish(1))
    halo_start(3, loc, hs3, hr3)
    halo_wait(3, hr3, h_recv)

    def second(k, acc):
        d = loc[k] + partner(k, loc, hr3)
        pre[k] = d
        return acc + fold(weight_of(k) * res[k] * d)
    rz1_part = lax.fori_loop(0, SLOTS, second, zero8)
    sums_start(1, [rz1_part])
    (rz1,) = sums_finish(1, 1)
    beta = rz1 / rz

    def last(k, carry):
        pre[k] = pre[k] + beta * dirn[k]
        return carry
    lax.fori_loop(0, SLOTS, last, 0)
    dn_copy = pltpu.make_async_copy(pre, out_dn, out_sem.at[2])
    dn_copy.start()

    q_wait(0, arr.at[0], q_send)
    z_wait(1, cnz.at[pl.ds(0, (Z - 1) * Q), :], q_send)
    for n in range(2):
        q_wait(2 + 4 * n, qr.at[n], q_send)
        z_wait(3 + 4 * n, zr.at[n, :, pl.ds(0, (Z - 1) * Q), :], q_send)
        zs = (zs0, zs1)[n]
        z_wait(4 + 4 * n, zs.at[pl.ds(0, Z - 1)], q_send)
        q_wait(5 + 4 * n, qr.at[2 + n], q_send)
        q_wait(10 + 2 * n, arr.at[1 + n], q_send)
        z_wait(11 + 2 * n, arz1.at[n, pl.ds(0, Z - 1)], q_send)
    for h, recv in enumerate((hr0, hr1, hr2, hr3)):
        halo_wait(h, recv, h_send)
    sol_copy.wait()
    r1_copy.wait()
    dn_copy.wait()


def shards(Q, Z, load, schur, schur_inverse, basis, coarse_inverse, partner_slot, edge_map, coarse_number):
    E, NR = load.shape[2], load.shape[3]
    NI = FACES * E
    NCZ, NC0 = coarse_inverse.shape
    NF = NC0 // NCF
    ZQ = Z * Q
    RR = SLOTS * NCF * CG // LANES
    vec = pltpu.VMEM((SLOTS, E, NR), F32)
    halo = pltpu.VMEM((2 * SUBS, E, NR), F32)
    mat = pltpu.VMEM((SUBS * NI, NI), BF16)
    out = jax.ShapeDtypeStruct((SLOTS, E, NR), F32)
    anywhere = pl.BlockSpec(memory_space=pl.ANY)
    vmem = pl.BlockSpec(memory_space=pltpu.VMEM)
    smem = pl.BlockSpec(memory_space=pltpu.SMEM)
    outs = pl.pallas_call(
        functools.partial(kernel, Q, Z),
        out_shape=(out, out, out),
        in_specs=[anywhere, anywhere, anywhere, vmem, anywhere, smem, vmem, smem],
        out_specs=(anywhere, anywhere, anywhere),
        scratch_shapes=[vec] * 7 + [halo] * 8 + [mat] * 4 + [
            pltpu.VMEM((NCZ, NC0), BF16),
            pltpu.VMEM((NCZ, NC0), BF16),
            pltpu.VMEM((2, 2 * E, NI), F32),
            pltpu.VMEM((2, NCZ // 7, NC0), F32),
            pltpu.VMEM((SUBS * NI, NR), BF16),
            pltpu.VMEM((SUBS * NI, NR), BF16),
            pltpu.VMEM((SLOTS, E, 2 * E), BF16),
            pltpu.VMEM((SUBS, 32, NI), BF16),
            pltpu.VMEM((SUBS, 32, NI), BF16),
            pltpu.VMEM((SUBS, NI, LANES), BF16),
            pltpu.VMEM((RR * LANES, CG * LANES), BF16),
            pltpu.VMEM((CG * LANES, RR * LANES), BF16),
            pltpu.VMEM((NF, SLOTS * ZQ), BF16),
            pltpu.VMEM((SLOTS, ZQ, NF // Z), BF16),
            pltpu.VMEM((LANES, NR), F32),
            pltpu.VMEM((NR, LANES), F32),
            pltpu.VMEM((NR, LANES), F32),
            pltpu.VMEM((NC0 // 7, LANES), F32),
            pltpu.VMEM((NC0, LANES), BF16),
            pltpu.VMEM((NCZ, LANES), F32),
            pltpu.VMEM((4, Q * 8, LANES), F32),
            pltpu.VMEM((4, Q * 8, LANES), F32),
            pltpu.VMEM((2, RR, Q, LANES), F32),
            pltpu.VMEM((2, RR, ZQ, LANES), F32),
            pltpu.VMEM((2, RR, ZQ, LANES), F32),
            pltpu.VMEM((Z, RR, Q, LANES), F32),
            pltpu.VMEM((Z, RR, Q, LANES), F32),
            pltpu.VMEM((5, 8, LANES), F32),
            pltpu.VMEM((3, Q * 8, LANES), F32),
            pltpu.VMEM((Q, LANES), F32),
            pltpu.VMEM((2, Z, 8, LANES), F32),
            pltpu.VMEM((ZQ, LANES), F32),
            pltpu.SemaphoreType.DMA,
            pltpu.SemaphoreType.DMA((2,)),
            pltpu.SemaphoreType.DMA((2,)),
            pltpu.SemaphoreType.DMA((3,)),
            pltpu.SemaphoreType.DMA((14,)),
            pltpu.SemaphoreType.DMA((14,)),
            pltpu.SemaphoreType.DMA((4, 2)),
            pltpu.SemaphoreType.DMA((4, 2)),
        ],
        compiler_params=pltpu.CompilerParams(
            collective_id=0, has_side_effects=True, vmem_limit_bytes=60 * 1024 * 1024
        ),
    )(
        load.reshape(SLOTS, E, NR),
        schur.reshape(SUBS * NI, NI),
        schur_inverse.reshape(SUBS * NI, NI),
        jnp.swapaxes(basis, 1, 2),
        coarse_inverse,
        partner_slot,
        jnp.swapaxes(edge_map, 0, 1),
        coarse_number,
    )
    return tuple(o.reshape(load.shape) for o in outs)


def solution(mesh):
    both = ("sub", "coarse")
    placed = (
        P(both, None, None, None),
        P(both, None, None),
        P(both, None, None),
        P(both, None, None),
        P("coarse", None),
        P(both, None),
        P(both, None, None),
        P(both, None),
    )
    return jax.shard_map(
        functools.partial(shards, mesh.shape["sub"], mesh.shape["coarse"]),
        mesh=mesh,
        in_specs=placed,
        out_specs=(P(both, None, None, None),) * 3,
        check_vma=False,
    )
```

```python
import functools

import jax
import jax.numpy as jnp
from jax import lax
from jax.experimental import pallas as pl
from jax.experimental.pallas import tpu as pltpu
from jax.sharding import PartitionSpec as P

MESH = pl.DeviceIdType.MESH
F32 = jnp.float32
BF16 = jnp.bfloat16
FACES = 6
SUBS = 2
SLOTS = FACES * SUBS
NCF = 4
LANES = 128
CG = 8


def split(x):
    hi = x.astype(BF16)
    return hi, (x - hi.astype(F32)).astype(BF16)


def dot(a, b):
    return jnp.dot(a, b, preferred_element_type=F32)


def kernel(
    Q, Z, load, schur, sinv, basis_t, coarse, ps, em, cn,
    dirn, res, pre, out_ab,
    vld, loc, prod, img,
    hs0, hs1, hs2, hs3, hr0, hr1, hr2, hr3,
    sinv_hi, sinv_lo, schur_hi, schur_lo, c_hi, c_lo, s_stage, c_stage,
    hh, hl, perm, bt_hi, bt_lo, bcol, sp, spt,
    fold4, scat, gath, xbuf, xt, yt, xm, xb, xf0, y2,
    qb, qr, zb, zr, ob, zs0, zs1, arb, arr, arz0, arz1, cnz,
    in_sem, st_sem, ct_sem, q_send, q_recv, h_send, h_recv,
):
    q = lax.axis_index("sub")
    z = lax.axis_index("coarse")
    E = vld.shape[1]
    NR = vld.shape[2]
    ZQ = Z * Q
    NCZ = c_hi.shape[0]
    NC0 = c_hi.shape[1]
    NF = NC0 // NCF
    NFZ = NF // Z
    RR = SLOTS * NCF * CG // LANES
    ndev = Q * Z
    me = q * Z + z
    nxt = lax.rem(me + 1, ndev)
    prv = lax.rem(me + ndev - 1, ndev)
    nxt_id = (nxt // Z, lax.rem(nxt, Z))
    prv_id = (prv // Z, lax.rem(prv, Z))

    def q_peer(k):
        return lax.rem(q + k, Q)

    def z_peer(k):
        return lax.rem(z + k, Z)

    owed = {}

    def owe(key, ref, sem):
        owed[key] = lambda: pltpu.make_async_copy(ref, ref, sem).wait()

    def settle(*key):
        owed.pop(key)()

    load_copy = pltpu.make_async_copy(load, vld, in_sem)
    load_copy.start()

    def stager(src, rows, stage, sem):
        def copy(i, slot):
            return pltpu.make_async_copy(
                src.at[pl.ds(pl.multiple_of(i * rows, rows), rows), :], stage.at[slot], sem.at[slot]
            )
        return copy

    s_rows = s_stage.shape[1]
    c_rows = c_stage.shape[1]
    sinv_copy = stager(sinv, s_rows, s_stage, st_sem)
    schur_copy = stager(schur, s_rows, s_stage, st_sem)
    c_copy = stager(coarse, c_rows, c_stage, ct_sem)

    def first(copy):
        copy(0, 0).start()
        copy(1, 1).start()
        owed[copy] = lambda: (copy(0, 0).wait(), copy(1, 1).wait())

    def convert(copy, stage, n, rows, hi_ref, lo_ref):
        def body(i, carry):
            slot = lax.rem(i, 2)
            copy(i, slot).wait()
            hi, lo = split(stage[slot])
            at = pl.ds(pl.multiple_of(i * rows, rows), rows)
            hi_ref[at, :] = hi
            lo_ref[at, :] = lo

            @pl.when(i + 2 < n)
            def _():
                copy(i + 2, slot).start()
            return carry
        lax.fori_loop(0, n, body, 0)
        owed.pop(copy)

    first(sinv_copy)
    first(c_copy)

    barrier = pltpu.get_barrier_semaphore()

    def greet(device):
        pl.semaphore_signal(barrier, inc=1, device_id=device, device_id_type=MESH)

    lax.fori_loop(1, Q, lambda k, c: (greet((q_peer(k), z)), c)[1], 0)
    for k in range(1, Z):
        greet((q, z_peer(k)))
    greet(nxt_id)
    greet(prv_id)

    lane8 = lax.broadcasted_iota(jnp.int32, (8, LANES), 1)

    def q_start(ph, src, dst, shared=False):
        def body(i, carry):
            p = q_peer(1 + lax.rem(i + Q // 2 - 1, Q - 1))
            block = src if shared else src.at[pl.ds(pl.multiple_of(p * 8, 8), 8), :]
            pltpu.make_async_remote_copy(
                src_ref=block,
                dst_ref=dst.at[pl.ds(pl.multiple_of(q * 8, 8), 8), :],
                send_sem=q_send.at[ph], recv_sem=q_recv.at[ph],
                device_id=(p, z), device_id_type=MESH,
            ).start()
            return carry
        lax.fori_loop(0, Q - 1, body, 0)
        mine = pl.ds(pl.multiple_of(q * 8, 8), 8)
        dst[mine, :] = src[...] if shared else src[mine, :]
        every = dst.at[pl.ds(0, (Q - 1) * 8), :]
        owe((ph, "in"), every, q_recv.at[ph])
        owe((ph, "out"), every, q_send.at[ph])

    def z_start(ph, src_of, dst, three):
        for k in sorted(range(1, Z), key=lambda k: -min(k, Z - k)):
            t = z_peer(k)
            pltpu.make_async_remote_copy(
                src_ref=src_of(t), dst_ref=dst,
                send_sem=q_send.at[ph], recv_sem=q_recv.at[ph],
                device_id=(q, t), device_id_type=MESH,
            ).start()
        owe((ph, "in"), three, q_recv.at[ph])
        owe((ph, "out"), three, q_send.at[ph])

    def rel_of(k):
        p = ps[k // FACES, lax.rem(k, FACES)]
        rel = p - me * SLOTS
        rel = jnp.where(rel < -SLOTS, rel + ndev * SLOTS, rel)
        rel = jnp.where(rel >= 2 * SLOTS, rel - ndev * SLOTS, rel)
        return p, rel

    def weight_of(k):
        return jnp.where(ps[k // FACES, lax.rem(k, FACES)] >= 0, jnp.float32(0.5), jnp.float32(1.0))

    ups, downs = [], []
    for s in range(SUBS):
        up = jnp.int32(0)
        down = jnp.int32(0)
        for f in range(FACES):
            p, rel = rel_of(s * FACES + f)
            here = p >= 0
            up = jnp.where(here & (rel >= SLOTS), s * FACES + f, up)
            down = jnp.where(here & (rel < 0), s * FACES + f, down)
        ups.append(up)
        downs.append(down)

    def halo_start(h, v, send, recv):
        for s in range(SUBS):
            send[s] = v[ups[s]]
            send[SUBS + s] = v[downs[s]]
        for way, device in ((0, nxt_id), (1, prv_id)):
            part = pl.ds(way * SUBS, SUBS)
            pltpu.make_async_remote_copy(
                src_ref=send.at[part], dst_ref=recv.at[part],
                send_sem=h_send.at[h, way], recv_sem=h_recv.at[h, way],
                device_id=device, device_id_type=MESH,
            ).start()
            owe((h, way, "halo in"), recv.at[part], h_recv.at[h, way])
            owe((h, way, "halo out"), recv.at[part], h_send.at[h, way])

    def halo_wait(h):
        settle(h, 0, "halo in")
        settle(h, 1, "halo in")

    def partner(k, v, recv):
        p, rel = rel_of(k)
        local = (rel >= 0) & (rel < SLOTS)
        inside = jnp.clip(rel, 0, SLOTS - 1)
        below = (rel + SLOTS >= FACES).astype(jnp.int32)
        above = SUBS + (rel - SLOTS >= FACES).astype(jnp.int32)
        outside = jnp.clip(jnp.where(rel < 0, below, above), 0, 2 * SUBS - 1)
        val = jnp.where(local, v[inside], recv[outside])
        hi, lo = split(val)
        return dot(perm[k], jnp.concatenate([hi, lo], axis=0))

    rows_e = lax.broadcasted_iota(jnp.int32, (E, E), 0)
    for k in range(SLOTS):
        line = em[k % FACES, pl.ds(k // FACES, 1), :]
        one = jnp.where(rows_e == line, jnp.float32(1.0), jnp.float32(0.0)).T
        one = jnp.where(ps[k // FACES, k % FACES] >= 0, one, jnp.zeros_like(one)).astype(BF16)
        perm[k] = jnp.concatenate([one, one], axis=1)

    NI = FACES * E
    NCL = FACES * NCF
    zrow = jnp.zeros((32 - NCL, NI), F32)
    for s in range(SUBS):
        b = basis_t[s]
        bh = b.astype(BF16).astype(F32)
        bl = b - bh
        bh = jnp.concatenate([bh, zrow], axis=0)
        bl = jnp.concatenate([bl, zrow], axis=0)
        bt_hi[s] = bh.astype(BF16)
        bt_lo[s] = bl.astype(BF16)
        bcol[s] = jnp.concatenate([bh, bh, bl, jnp.zeros_like(bl)], axis=0).T.astype(BF16)

    i0 = lax.broadcasted_iota(jnp.int32, sp.shape, 0)
    i1 = lax.broadcasted_iota(jnp.int32, sp.shape, 1)
    target = (i0 & 7) * LANES + (i0 >> 7) * 16 + ((i0 & 127) >> 3)
    sp[...] = jnp.where(i1 == target, jnp.float32(1.0), jnp.float32(0.0)).astype(BF16)
    wide = RR * LANES
    j0 = lax.broadcasted_iota(jnp.int32, (CG * LANES, wide), 0)
    j1 = lax.broadcasted_iota(jnp.int32, (CG * LANES, wide), 1)
    back = (j1 & 7) * LANES + (j1 >> 7) * 16 + ((j1 & 127) >> 3)
    spt[...] = jnp.where(j0 == back, jnp.float32(1.0), jnp.float32(0.0)).astype(BF16)

    m0 = lax.broadcasted_iota(jnp.int32, fold4.shape, 0)
    m1 = lax.broadcasted_iota(jnp.int32, fold4.shape, 1)
    fold4[...] = jnp.where(
        ((m0 & 7) == (m1 & 7)) & ((m0 >> 8) == ((m1 >> 3) & 3)), jnp.float32(1.0), jnp.float32(0.0)
    ).astype(BF16)
    xbuf[...] = jnp.zeros_like(xbuf)

    convert(sinv_copy, s_stage, SUBS * NI // s_rows, s_rows, sinv_hi, sinv_lo)
    first(schur_copy)
    load_copy.wait()
    pl.semaphore_wait(barrier, Q + Z)
    halo_start(0, vld, hs0, hr0)

    row = jnp.zeros((8, LANES), F32)
    for k in range(SLOTS):
        row = jnp.where(lane8 == k, cn[k // FACES, k % FACES].astype(F32), row)
    arb[0] = row
    q_start(0, arb.at[0], arr.at[0], shared=True)

    convert(c_copy, c_stage, NCZ // c_rows, c_rows, c_hi, c_lo)

    settle(0, "in")
    zmine = pl.ds(pl.multiple_of(z * Q, Q), Q)
    arz0[...] = arr[0, pl.ds(0, Q, stride=8), :]
    cnz[zmine, :] = arz0[...]
    z_start(1, lambda t: arz0, cnz.at[zmine, :], cnz.at[pl.ds(0, (Z - 1) * Q), :])
    convert(schur_copy, s_stage, SUBS * NI // s_rows, s_rows, schur_hi, schur_lo)

    settle(1, "in")
    cns = cnz[...]
    cnt = cns.T if ZQ == LANES else jnp.concatenate([cns, jnp.zeros((LANES - ZQ, LANES), F32)], axis=0).T
    face0 = lax.broadcasted_iota(jnp.int32, (NF, ZQ), 0).astype(F32)
    face1 = lax.broadcasted_iota(jnp.int32, (ZQ, NFZ), 1).astype(F32) + (z * NFZ).astype(F32)
    for k in range(SLOTS):
        scat[:, k * ZQ:(k + 1) * ZQ] = jnp.where(
            face0 == cnt[k:k + 1, :ZQ], jnp.float32(1.0), jnp.float32(0.0)
        ).astype(BF16)
        gath[k] = jnp.where(
            cns[:, k:k + 1] == face1, jnp.float32(1.0), jnp.float32(0.0)
        ).astype(BF16)


    def put(k, x):
        hi, lo = split(x)
        at = pl.ds(pl.multiple_of(k * E, E), E)
        hh[at, :] = hi
        hl[at, :] = lo

    def local_mul(a_hi, a_lo, out):
        rows = 2 * E
        per = NI // rows

        def body(i, carry):
            at = pl.ds(pl.multiple_of(i * rows, rows), rows)
            sub = pl.ds(pl.multiple_of((i // per) * NI, NI), NI)
            hi = a_hi[at, :]
            top = hh[sub, :]
            acc = dot(hi, top) + dot(hi, hl[sub, :]) + dot(a_lo[at, :], top)
            out[2 * i] = acc[:E]
            out[2 * i + 1] = acc[E:]
            return carry
        lax.fori_loop(0, SUBS * per, body, 0)

    def forward_start(n):
        for s in range(SUBS):
            sub = pl.ds(s * NI, NI)
            top = hh[sub, :]
            x = dot(bt_hi[s], top) + dot(bt_hi[s], hl[sub, :]) + dot(bt_lo[s], top)
            xbuf[s * NCL:(s + 1) * NCL, :] = x[:NCL]
        xt[...] = xbuf[...].T
        acc = jnp.zeros((2 * Q, wide), F32)
        for c in range(CG):
            part = xt[pl.ds(c, Q, stride=CG), :]
            hi = part.astype(BF16).astype(F32)
            both = jnp.concatenate([hi, part - hi], axis=0).astype(BF16)
            acc += dot(both, spt[c * LANES:(c + 1) * LANES, :])
        acc = acc[:Q] + acc[Q:]
        b = qb.at[n]
        for r in range(RR):
            b[pl.ds(r, Q, stride=8), :] = acc[:, r * LANES:(r + 1) * LANES]
        for r in range(RR, 8):
            b[pl.ds(r, Q, stride=8), :] = jnp.zeros((Q, LANES), F32)
        q_start(2 + 4 * n, b, qr.at[n])

    def gather_start(n):
        settle(2 + 4 * n, "in")
        for r in range(RR):
            part = qr[n, pl.ds(r, Q, stride=8), :]
            zb[n, r] = part
            zr[n, r, zmine, :] = part
        z_start(
            3 + 4 * n, lambda t: zb.at[n], zr.at[n, :, zmine, :],
            zr.at[n, :, pl.ds(0, (Z - 1) * Q), :],
        )

    def coarse_product(n, step=None):
        settle(3 + 4 * n, "in")
        la = lax.broadcasted_iota(jnp.int32, (ZQ, LANES), 1) >> 5
        pieces = []
        for r in range(RR):
            part = zr[n, r]
            for a in range(NCF):
                hi, lo = split(jnp.where(la == a, part, jnp.float32(0.0)))
                pieces.append(jnp.concatenate([hi, lo], axis=1))
        slots = jnp.concatenate(pieces, axis=0)
        fa = lax.broadcasted_iota(jnp.int32, (NF, LANES), 1)
        acc = dot(scat[...], slots)
        x = acc[:, :LANES] + acc[:, LANES:]
        x = x + pltpu.roll(x, 64, 1)
        x = x + pltpu.roll(x, 32, 1)
        if step is not None:
            x = xf0[...] - step() * x
        xf0[...] = x
        hi = x.astype(BF16).astype(F32)
        v = jnp.where((fa >> 5) == 0, hi, jnp.where((fa >> 5) == 1, x - hi, jnp.float32(0.0)))
        for j in range(NCF):
            xm[pl.ds(j, NF, stride=NCF), :] = jnp.where(((fa >> 3) & 3) == j, v, jnp.float32(0.0))
        xb[...] = xm[...].astype(BF16)
        kc = NC0 // 7
        acc = jnp.zeros((NCZ, LANES), F32)
        for k in range(7):
            cols = slice(k * kc, (k + 1) * kc)
            acc += dot(c_hi[:, cols], xb[cols, :]) + dot(c_lo[:, cols], xb[cols, :])
        y2[...] = acc
        pieces = []
        for j in range(NCF):
            pieces.extend(split(y2[pl.ds(j, NFZ, stride=NCF), :]))
        y = dot(jnp.concatenate(pieces, axis=1), fold4[...])
        hi, lo = split(y)
        both = jnp.concatenate([hi, lo], axis=1)
        for r in range(RR):
            o = jnp.zeros((ZQ, LANES), F32)
            for a in range(NCF):
                g = dot(gath[NCF * r + a], both)
                o = jnp.where(la == a, g[:, :LANES] + g[:, LANES:], o)
            ob[n, r] = o
        mine = xf0[pl.ds(pl.multiple_of(z * NFZ, 8) if NFZ % 8 == 0 else z * NFZ, NFZ), :]
        energy = (mine * y).sum(axis=0, keepdims=True)
        ob[n, RR] = jnp.where(la == 0, energy, jnp.float32(0.0))
        zs = (zs0, zs1)[n]
        zs[z] = ob[n, :, zmine, :]
        z_start(
            4 + 4 * n,
            lambda t: ob.at[n, :, pl.ds(pl.multiple_of(t * Q, Q), Q), :],
            zs.at[z],
            zs.at[pl.ds(0, Z - 1)],
        )

    def backward_start(n):
        zs = (zs0, zs1)[n]
        settle(4 + 4 * n, "in")
        b = qb.at[2 + n]
        for r in range(RR + 1):
            tot = zs[0, r]
            for t in range(1, Z):
                tot = tot + zs[t, r]
            b[pl.ds(r, Q, stride=8), :] = tot
        for r in range(RR + 1, 8):
            b[pl.ds(r, Q, stride=8), :] = jnp.zeros((Q, LANES), F32)
        q_start(5 + 4 * n, b, qr.at[2 + n])

    def backward_finish(n):
        settle(5 + 4 * n, "in")
        acc = jnp.zeros((2 * Q, CG * LANES), F32)
        for r in range(RR + 1):
            part = qr[2 + n, pl.ds(r, Q, stride=8), :]
            hi = part.astype(BF16).astype(F32)
            both = jnp.concatenate([hi, part - hi], axis=0).astype(BF16)
            acc += dot(both, sp[r * LANES:(r + 1) * LANES, :])
        for c in range(CG):
            cols = slice(c * LANES, (c + 1) * LANES)
            yt[pl.ds(c, Q, stride=CG), :] = acc[:Q, cols] + acc[Q:, cols]
        return yt[...].T

    def add_coarse(y):
        pad = jnp.zeros((32 - NCL, NR), F32)
        for s in range(SUBS):
            ys = jnp.concatenate([y[s * NCL:(s + 1) * NCL], pad], axis=0)
            hi = ys.astype(BF16).astype(F32)
            lo = ys - hi
            cols = jnp.concatenate([hi, lo, hi, jnp.zeros_like(hi)], axis=0).astype(BF16)

            def body(f, carry):
                k = s * FACES + f
                at = pl.ds(pl.multiple_of(f * E, E), E)
                loc[k] = weight_of(k) * (loc[k] + dot(bcol[s, at, :], cols))
                return carry
            lax.fori_loop(0, FACES, body, 0)

    def fold(x):
        return x.reshape(E // 8, 8, NR).sum(axis=0)

    nh = max(1, NR // LANES)
    lw = min(NR, LANES)

    def sums_start(n, parts):
        b = arb.at[1 + n]
        b[...] = jnp.zeros((8, LANES), F32)
        for i, part in enumerate(parts):
            line = part.sum(axis=0, keepdims=True)
            for h in range(nh):
                b[pl.ds(i * nh + h, 1), 0:lw] = line[:, h * lw:(h + 1) * lw]
        q_start(10 + 2 * n, b, arr.at[1 + n], shared=True)

    def sums_pass(n):
        settle(10 + 2 * n, "in")
        tot = arr[1 + n].reshape(Q, 8, LANES).sum(axis=0)
        arb[3 + n] = tot
        arz1[n, z] = tot
        z_start(11 + 2 * n, lambda t: arb.at[3 + n], arz1.at[n, z], arz1.at[n, pl.ds(0, Z - 1)])

    def sums_finish(n):
        settle(11 + 2 * n, "in")
        tot = arz1[n, 0]
        for t in range(1, Z):
            tot = tot + arz1[n, t]
        return tot

    def cases(tile, i):
        return jnp.concatenate([tile[i * nh + h:i * nh + h + 1, :lw] for h in range(nh)], axis=1)

    def own_cases(tile):
        row = jnp.where(q * CG >= LANES, tile[nh - 1:nh], tile[0:1])
        row = jnp.broadcast_to(row, (8, LANES))
        row = pltpu.roll(row, lax.rem(2 * LANES - q * CG + LANES, LANES), 1)
        row = jnp.where(lane8 < CG, row, jnp.float32(0.0))
        for shift in (8, 16, 32, 64):
            row = row + pltpu.roll(row, shift, 1)
        return row[0:1]

    zero8 = jnp.zeros((8, NR), F32)

    halo_wait(0)

    def residual(k, carry):
        r = vld[k] + partner(k, vld, hr0)
        res[k] = r
        put(k, weight_of(k) * r)
        return carry
    lax.fori_loop(0, SLOTS, residual, 0)

    forward_start(0)
    local_mul(sinv_hi, sinv_lo, loc)
    gather_start(0)
    coarse_product(0)
    backward_start(0)
    add_coarse(backward_finish(0))
    halo_start(1, loc, hs1, hr1)
    halo_wait(1)

    def direction(k, acc):
        d = loc[k] + partner(k, loc, hr1)
        dirn[k] = d
        put(k, d)
        return acc + fold(weight_of(k) * res[k] * d)
    rz_part = lax.fori_loop(0, SLOTS, direction, zero8)

    local_mul(schur_hi, schur_lo, prod)
    halo_start(2, prod, hs2, hr2)
    halo_wait(2)

    def image(k, acc):
        m = prod[k] + partner(k, prod, hr2)
        img[k] = m
        wm = weight_of(k) * m
        put(k, wm)
        return acc + fold(dirn[k] * wm)
    da_part = lax.fori_loop(0, SLOTS, image, zero8)

    forward_start(1)
    sums_start(0, [rz_part, da_part])
    gather_start(1)
    sums_pass(0)
    tot = sums_finish(0)
    rz = cases(tot, 0)
    alpha = rz / cases(tot, 1)
    coarse_product(1, lambda: own_cases(tot[:nh] / tot[nh:2 * nh]))

    def advance(k, carry):
        r = res[k] - alpha * img[k]
        res[k] = r
        put(k, weight_of(k) * r)
        return carry
    lax.fori_loop(0, SLOTS, advance, 0)

    local_mul(sinv_hi, sinv_lo, loc)
    backward_start(1)

    def energies(k, acc):
        return acc + fold(weight_of(k) * res[k] * loc[k])
    sums_start(1, [lax.fori_loop(0, SLOTS, energies, zero8)])
    y = backward_finish(1)
    coarse_energy = y[SUBS * NCL:SUBS * NCL + NCF].sum(axis=0, keepdims=True)
    add_coarse(y)
    halo_start(3, loc, hs3, hr3)
    sums_pass(1)
    beta = (cases(sums_finish(1), 0) + coarse_energy) / rz
    halo_wait(3)

    def second(k, carry):
        pre[k] = loc[k] + partner(k, loc, hr3)
        return carry
    lax.fori_loop(0, SLOTS, second, 0)
    out_ab[...] = jnp.concatenate([alpha, beta, jnp.zeros((6, NR), F32)], axis=0)

    for wait in list(owed.values()):
        wait()


def shards(Q, Z, load, schur, schur_inverse, basis, coarse_inverse, partner_slot, edge_map, coarse_number):
    E, NR = load.shape[2], load.shape[3]
    NI = FACES * E
    NCZ, NC0 = coarse_inverse.shape
    NF = NC0 // NCF
    ZQ = Z * Q
    RR = SLOTS * NCF * CG // LANES
    vec = pltpu.VMEM((SLOTS, E, NR), F32)
    halo = pltpu.VMEM((2 * SUBS, E, NR), F32)
    mat = pltpu.VMEM((SUBS * NI, NI), BF16)
    out = pltpu.VMEM((SLOTS, E, NR), F32)
    anywhere = pl.BlockSpec(memory_space=pl.ANY)
    vmem = pl.BlockSpec(memory_space=pltpu.VMEM)
    smem = pl.BlockSpec(memory_space=pltpu.SMEM)
    direction, residual, preconditioned, ratios = pl.pallas_call(
        functools.partial(kernel, Q, Z),
        out_shape=(out, out, out, jax.ShapeDtypeStruct((8, NR), F32)),
        in_specs=[anywhere, anywhere, anywhere, vmem, anywhere, smem, vmem, smem],
        out_specs=(vmem, vmem, vmem, vmem),
        scratch_shapes=[vec] * 4 + [halo] * 8 + [mat] * 4 + [
            pltpu.VMEM((NCZ, NC0), BF16),
            pltpu.VMEM((NCZ, NC0), BF16),
            pltpu.VMEM((2, 2 * E, NI), F32),
            pltpu.VMEM((2, NCZ // 7, NC0), F32),
            pltpu.VMEM((SUBS * NI, NR), BF16),
            pltpu.VMEM((SUBS * NI, NR), BF16),
            pltpu.VMEM((SLOTS, E, 2 * E), BF16),
            pltpu.VMEM((SUBS, 32, NI), BF16),
            pltpu.VMEM((SUBS, 32, NI), BF16),
            pltpu.VMEM((SUBS, NI, LANES), BF16),
            pltpu.VMEM(((RR + 1) * LANES, CG * LANES), BF16),
            pltpu.VMEM((CG * LANES, RR * LANES), BF16),
            pltpu.VMEM((2 * NCF * LANES, LANES), BF16),
            pltpu.VMEM((NF, SLOTS * ZQ), BF16),
            pltpu.VMEM((SLOTS, ZQ, NF // Z), BF16),
            pltpu.VMEM((LANES, NR), F32),
            pltpu.VMEM((NR, LANES), F32),
            pltpu.VMEM((NR, LANES), F32),
            pltpu.VMEM((NC0, LANES), F32),
            pltpu.VMEM((NC0, LANES), BF16),
            pltpu.VMEM((NF, LANES), F32),
            pltpu.VMEM((NCZ, LANES), F32),
            pltpu.VMEM((4, Q * 8, LANES), F32),
            pltpu.VMEM((4, Q * 8, LANES), F32),
            pltpu.VMEM((2, RR, Q, LANES), F32),
            pltpu.VMEM((2, RR, ZQ, LANES), F32),
            pltpu.VMEM((2, RR + 1, ZQ, LANES), F32),
            pltpu.VMEM((Z, RR + 1, Q, LANES), F32),
            pltpu.VMEM((Z, RR + 1, Q, LANES), F32),
            pltpu.VMEM((5, 8, LANES), F32),
            pltpu.VMEM((3, Q * 8, LANES), F32),
            pltpu.VMEM((Q, LANES), F32),
            pltpu.VMEM((2, Z, 8, LANES), F32),
            pltpu.VMEM((ZQ, LANES), F32),
            pltpu.SemaphoreType.DMA,
            pltpu.SemaphoreType.DMA((2,)),
            pltpu.SemaphoreType.DMA((2,)),
            pltpu.SemaphoreType.DMA((14,)),
            pltpu.SemaphoreType.DMA((14,)),
            pltpu.SemaphoreType.DMA((4, 2)),
            pltpu.SemaphoreType.DMA((4, 2)),
        ],
        compiler_params=pltpu.CompilerParams(
            collective_id=0, has_side_effects=True, vmem_limit_bytes=56 * 1024 * 1024
        ),
    )(
        load.reshape(SLOTS, E, NR),
        schur.reshape(SUBS * NI, NI),
        schur_inverse.reshape(SUBS * NI, NI),
        jnp.swapaxes(basis, 1, 2),
        coarse_inverse,
        partner_slot,
        jnp.swapaxes(edge_map, 0, 1),
        coarse_number,
    )
    alpha, beta = ratios[0], ratios[1]
    return tuple(
        o.reshape(load.shape)
        for o in (alpha * direction, residual, preconditioned + beta * direction)
    )


def solution(mesh):
    both = ("sub", "coarse")
    placed = (
        P(both, None, None, None),
        P(both, None, None),
        P(both, None, None),
        P(both, None, None),
        P("coarse", None),
        P(both, None),
        P(both, None, None),
        P(both, None),
    )
    return jax.shard_map(
        functools.partial(shards, mesh.shape["sub"], mesh.shape["coarse"]),
        mesh=mesh,
        in_specs=placed,
        out_specs=(P(both, None, None, None),) * 3,
        check_vma=False,
    )
```

```python
import functools

import jax
import jax.numpy as jnp
from jax import lax
from jax.experimental import pallas as pl
from jax.experimental.pallas import tpu as pltpu
from jax.sharding import PartitionSpec as P

MESH = pl.DeviceIdType.MESH
F32 = jnp.float32
BF16 = jnp.bfloat16
FACES = 6
SUBS = 2
SLOTS = FACES * SUBS
NCF = 4
LANES = 128
CG = 8


def split(x):
    hi = x.astype(BF16)
    return hi, (x - hi.astype(F32)).astype(BF16)


def dot(a, b):
    return jnp.dot(a, b, preferred_element_type=F32)


def kernel(
    Q, Z, load, schur, sinv, basis_t, coarse, ps, em, cn,
    dirn, res, img, pre, out_alpha, out_beta,
    vld, loc, prod,
    hs0, hs1, hs2, hs3, hr0, hr1, hr2, hr3,
    sinv_hi, sinv_lo, schur_hi, schur_lo, c_hi, c_lo, s_stage, c_stage,
    hh, hl, perm, bt_hi, bt_lo, bcol, bface, bpart, bs, br, gs, gr, ys, yr, sp, spt,
    fold4, scat, gath, xbuf, xt, yt, xm, xb, xf0, y2,
    qb, qr, zb, zr, ob, zs0, zs1, arb, arr, arz0, arz1, cnz,
    in_sem, st_sem, ct_sem, q_send, q_recv, h_send, h_recv,
):
    q = lax.axis_index("sub")
    z = lax.axis_index("coarse")
    E = vld.shape[1]
    NR = vld.shape[2]
    ZQ = Z * Q
    NCZ = c_hi.shape[0]
    NC0 = c_hi.shape[1]
    NF = NC0 // NCF
    NFZ = NF // Z
    RR = SLOTS * NCF * CG // LANES
    ndev = Q * Z
    me = q * Z + z
    nxt = lax.rem(me + 1, ndev)
    prv = lax.rem(me + ndev - 1, ndev)
    nxt_id = (nxt // Z, lax.rem(nxt, Z))
    prv_id = (prv // Z, lax.rem(prv, Z))

    def q_peer(k):
        return lax.rem(q + k, Q)

    def z_peer(k):
        return lax.rem(z + k, Z)

    owed = {}

    def owe(key, ref, sem):
        owed[key] = lambda: pltpu.make_async_copy(ref, ref, sem).wait()

    def settle(*key):
        owed.pop(key)()

    load_copy = pltpu.make_async_copy(load, vld, in_sem)
    load_copy.start()

    def stager(src, rows, stage, sem):
        def copy(i, slot):
            return pltpu.make_async_copy(
                src.at[pl.ds(pl.multiple_of(i * rows, rows), rows), :], stage.at[slot], sem.at[slot]
            )
        return copy

    s_rows = s_stage.shape[1]
    c_rows = c_stage.shape[1]
    sinv_copy = stager(sinv, s_rows, s_stage, st_sem)
    schur_copy = stager(schur, s_rows, s_stage, st_sem)
    c_copy = stager(coarse, c_rows, c_stage, ct_sem)

    def first(copy):
        copy(0, 0).start()
        copy(1, 1).start()
        owed[copy] = lambda: (copy(0, 0).wait(), copy(1, 1).wait())

    def convert(copy, stage, n, rows, hi_ref, lo_ref):
        def body(i, carry):
            slot = lax.rem(i, 2)
            copy(i, slot).wait()
            hi, lo = split(stage[slot])
            at = pl.ds(pl.multiple_of(i * rows, rows), rows)
            hi_ref[at, :] = hi
            lo_ref[at, :] = lo

            @pl.when(i + 2 < n)
            def _():
                copy(i + 2, slot).start()
            return carry
        lax.fori_loop(0, n, body, 0)
        owed.pop(copy)

    first(sinv_copy)
    first(c_copy)

    barrier = pltpu.get_barrier_semaphore()

    def greet(device):
        pl.semaphore_signal(barrier, inc=1, device_id=device, device_id_type=MESH)

    lax.fori_loop(1, Q, lambda k, c: (greet((q_peer(k), z)), c)[1], 0)
    for k in range(1, Z):
        greet((q, z_peer(k)))
    greet(nxt_id)
    greet(prv_id)

    lane8 = lax.broadcasted_iota(jnp.int32, (8, LANES), 1)

    def q_start(ph, src, dst, shared=False):
        def body(i, carry):
            p = q_peer(1 + lax.rem(i + Q // 2 - 1, Q - 1))
            block = src if shared else src.at[pl.ds(pl.multiple_of(p * 8, 8), 8), :]
            pltpu.make_async_remote_copy(
                src_ref=block,
                dst_ref=dst.at[pl.ds(pl.multiple_of(q * 8, 8), 8), :],
                send_sem=q_send.at[ph], recv_sem=q_recv.at[ph],
                device_id=(p, z), device_id_type=MESH,
            ).start()
            return carry
        lax.fori_loop(0, Q - 1, body, 0)
        mine = pl.ds(pl.multiple_of(q * 8, 8), 8)
        dst[mine, :] = src[...] if shared else src[mine, :]
        every = dst.at[pl.ds(0, (Q - 1) * 8), :]
        owe((ph, "in"), every, q_recv.at[ph])
        owe((ph, "out"), every, q_send.at[ph])

    def z_start(ph, src_of, dst, three):
        for k in sorted(range(1, Z), key=lambda k: -min(k, Z - k)):
            t = z_peer(k)
            pltpu.make_async_remote_copy(
                src_ref=src_of(t), dst_ref=dst,
                send_sem=q_send.at[ph], recv_sem=q_recv.at[ph],
                device_id=(q, t), device_id_type=MESH,
            ).start()
        owe((ph, "in"), three, q_recv.at[ph])
        owe((ph, "out"), three, q_send.at[ph])

    def rel_of(k):
        p = ps[k // FACES, lax.rem(k, FACES)]
        rel = p - me * SLOTS
        rel = jnp.where(rel < -SLOTS, rel + ndev * SLOTS, rel)
        rel = jnp.where(rel >= 2 * SLOTS, rel - ndev * SLOTS, rel)
        return p, rel

    def weight_of(k):
        return jnp.where(ps[k // FACES, lax.rem(k, FACES)] >= 0, jnp.float32(0.5), jnp.float32(1.0))

    ups, downs = [], []
    for s in range(SUBS):
        up = jnp.int32(0)
        down = jnp.int32(0)
        for f in range(FACES):
            p, rel = rel_of(s * FACES + f)
            here = p >= 0
            up = jnp.where(here & (rel >= SLOTS), s * FACES + f, up)
            down = jnp.where(here & (rel < 0), s * FACES + f, down)
        ups.append(up)
        downs.append(down)

    def pair_start(h, send, recv, count):
        for way, device in ((0, nxt_id), (1, prv_id)):
            part = pl.ds(way * count, count)
            pltpu.make_async_remote_copy(
                src_ref=send.at[part], dst_ref=recv.at[part],
                send_sem=h_send.at[h, way], recv_sem=h_recv.at[h, way],
                device_id=device, device_id_type=MESH,
            ).start()
            owe((h, way, "halo in"), recv.at[part], h_recv.at[h, way])
            owe((h, way, "halo out"), recv.at[part], h_send.at[h, way])

    def halo_start(h, v, send, recv):
        for s in range(SUBS):
            send[s] = v[ups[s]]
            send[SUBS + s] = v[downs[s]]
        pair_start(h, send, recv, SUBS)

    def halo_wait(h):
        settle(h, 0, "halo in")
        settle(h, 1, "halo in")

    def place_of(k):
        p, rel = rel_of(k)
        local = (rel >= 0) & (rel < SLOTS)
        inside = jnp.clip(rel, 0, SLOTS - 1)
        below = (rel + SLOTS >= FACES).astype(jnp.int32)
        above = SUBS + (rel - SLOTS >= FACES).astype(jnp.int32)
        return local, inside, jnp.clip(jnp.where(rel < 0, below, above), 0, 2 * SUBS - 1)

    def permute(k, val):
        hi, lo = split(val)
        return dot(perm[k], jnp.concatenate([hi, lo], axis=0))

    def partner(k, v, recv):
        local, inside, outside = place_of(k)
        return permute(k, jnp.where(local, v[inside], recv[outside]))

    def partner_here(k, v):
        local, inside, outside = place_of(k)
        return permute(k, jnp.where(local, v[inside], jnp.float32(0.0)))

    rows_e = lax.broadcasted_iota(jnp.int32, (E, E), 0)
    for k in range(SLOTS):
        line = em[k % FACES, pl.ds(k // FACES, 1), :]
        one = jnp.where(rows_e == line, jnp.float32(1.0), jnp.float32(0.0)).T
        one = jnp.where(ps[k // FACES, k % FACES] >= 0, one, jnp.zeros_like(one)).astype(BF16)
        perm[k] = jnp.concatenate([one, one], axis=1)

    NI = FACES * E
    NCL = FACES * NCF
    convert(sinv_copy, s_stage, SUBS * NI // s_rows, s_rows, sinv_hi, sinv_lo)
    first(schur_copy)
    convert(c_copy, c_stage, NCZ // c_rows, c_rows, c_hi, c_lo)
    load_copy.wait()
    pl.semaphore_wait(barrier, Q + Z)
    halo_start(0, vld, hs0, hr0)

    row = jnp.zeros((8, LANES), F32)
    for k in range(SLOTS):
        row = jnp.where(lane8 == k, cn[k // FACES, k % FACES].astype(F32), row)
    arb[0] = row
    q_start(0, arb.at[0], arr.at[0], shared=True)

    for s in range(SUBS):
        for place, slot in ((s, ups[s]), (SUBS + s, downs[s])):
            face = jnp.zeros((NCL, E), F32)
            for f in range(FACES):
                face = jnp.where(slot == s * FACES + f, basis_t[s, :, f * E:(f + 1) * E], face)
            bs[place] = face
    pair_start(4, bs, br, SUBS)

    zrow = jnp.zeros((32 - NCL, NI), F32)
    for s in range(SUBS):
        b = basis_t[s]
        bh = b.astype(BF16).astype(F32)
        bl = b - bh
        bh = jnp.concatenate([bh, zrow], axis=0)
        bl = jnp.concatenate([bl, zrow], axis=0)
        bt_hi[s] = bh.astype(BF16)
        bt_lo[s] = bl.astype(BF16)
        bcol[s] = jnp.concatenate([bh, bh, bl, jnp.zeros_like(bl)], axis=0).T.astype(BF16)

    i0 = lax.broadcasted_iota(jnp.int32, sp.shape, 0)
    i1 = lax.broadcasted_iota(jnp.int32, sp.shape, 1)
    target = (i0 & 7) * LANES + (i0 >> 7) * 16 + ((i0 & 127) >> 3)
    sp[...] = jnp.where(i1 == target, jnp.float32(1.0), jnp.float32(0.0)).astype(BF16)
    wide = (RR + 1) * LANES
    j0 = lax.broadcasted_iota(jnp.int32, (CG * LANES, wide), 0)
    j1 = lax.broadcasted_iota(jnp.int32, (CG * LANES, wide), 1)
    back = (j1 & 7) * LANES + (j1 >> 7) * 16 + ((j1 & 127) >> 3)
    spt[...] = jnp.where(j0 == back, jnp.float32(1.0), jnp.float32(0.0)).astype(BF16)

    m0 = lax.broadcasted_iota(jnp.int32, fold4.shape, 0)
    m1 = lax.broadcasted_iota(jnp.int32, fold4.shape, 1)
    fold4[...] = jnp.where(
        ((m0 & 7) == (m1 & 7)) & ((m0 >> 8) == ((m1 >> 3) & 3)), jnp.float32(1.0), jnp.float32(0.0)
    ).astype(BF16)
    xbuf[...] = jnp.zeros_like(xbuf)

    settle(0, "in")
    zmine = pl.ds(pl.multiple_of(z * Q, Q), Q)
    arz0[...] = arr[0, pl.ds(0, Q, stride=8), :]
    cnz[zmine, :] = arz0[...]
    z_start(1, lambda t: arz0, cnz.at[zmine, :], cnz.at[pl.ds(0, (Z - 1) * Q), :])

    def number_tables():
        settle(1, "in")
        cns = cnz[...]
        cnt = cns.T if ZQ == LANES else jnp.concatenate([cns, jnp.zeros((LANES - ZQ, LANES), F32)], axis=0).T
        face0 = lax.broadcasted_iota(jnp.int32, (NF, ZQ), 0).astype(F32)
        face1 = lax.broadcasted_iota(jnp.int32, (ZQ, NFZ), 1).astype(F32) + (z * NFZ).astype(F32)
        for k in range(SLOTS):
            scat[:, k * ZQ:(k + 1) * ZQ] = jnp.where(
                face0 == cnt[k:k + 1, :ZQ], jnp.float32(1.0), jnp.float32(0.0)
            ).astype(BF16)
            gath[k] = jnp.where(
                cns[:, k:k + 1] == face1, jnp.float32(1.0), jnp.float32(0.0)
            ).astype(BF16)

    def face_tables():
        settle(4, 0, "halo in")
        settle(4, 1, "halo in")
        pad = jnp.zeros((32 - NCL, E), F32)
        for c in range(2 * SUBS):
            b = jnp.concatenate([br[c], pad], axis=0)
            bh = b.astype(BF16).astype(F32)
            bface[c] = jnp.concatenate([bh, bh, b - bh, jnp.zeros_like(bh)], axis=0).T.astype(BF16)
        for s in range(SUBS):
            for place, slot in ((s, ups[s]), (SUBS + s, downs[s])):
                local, inside, outside = place_of(slot)
                b = jnp.concatenate([br[outside], pad], axis=0)
                bh = b.astype(BF16).astype(F32)
                both = jnp.concatenate([bh, b - bh], axis=0).astype(BF16)
                bpart[place] = lax.dot_general(
                    both, perm[slot][:, :E], (((1,), (1,)), ((), ())), preferred_element_type=F32
                ).astype(BF16)

    def put(k, x):
        hi, lo = split(x)
        at = pl.ds(pl.multiple_of(k * E, E), E)
        hh[at, :] = hi
        hl[at, :] = lo

    def local_mul(a_hi, a_lo, out, scale):
        rows = 2 * E
        per = NI // rows

        def body(i, carry):
            at = pl.ds(pl.multiple_of(i * rows, rows), rows)
            sub = pl.ds(pl.multiple_of((i // per) * NI, NI), NI)
            hi = a_hi[at, :]
            top = hh[sub, :]
            acc = dot(hi, top) + dot(hi, hl[sub, :]) + dot(a_lo[at, :], top)
            out[2 * i] = scale(2 * i) * acc[:E]
            out[2 * i + 1] = scale(2 * i + 1) * acc[E:]
            return carry
        lax.fori_loop(0, SUBS * per, body, 0)

    def coarse_load(s):
        sub = pl.ds(s * NI, NI)
        top = hh[sub, :]
        x = dot(bt_hi[s], top) + dot(bt_hi[s], hl[sub, :]) + dot(bt_lo[s], top)
        return x[:NCL]

    def forward_start(n, loads, sums=()):
        for s in range(SUBS):
            xbuf[s * NCL:(s + 1) * NCL, :] = loads[s]
        for i, part in enumerate(sums):
            xbuf[pl.ds(SUBS * NCL + i, 1), :] = part.sum(axis=0, keepdims=True)
        xt[...] = xbuf[...].T
        acc = jnp.zeros((2 * Q, (RR + 1) * LANES), F32)
        for c in range(CG):
            part = xt[pl.ds(c, Q, stride=CG), :]
            hi = part.astype(BF16).astype(F32)
            both = jnp.concatenate([hi, part - hi], axis=0).astype(BF16)
            acc += dot(both, spt[c * LANES:(c + 1) * LANES, :])
        acc = acc[:Q] + acc[Q:]
        b = qb.at[n]
        for r in range(RR + 1):
            b[pl.ds(r, Q, stride=8), :] = acc[:, r * LANES:(r + 1) * LANES]
        for r in range(RR + 1, 8):
            b[pl.ds(r, Q, stride=8), :] = jnp.zeros((Q, LANES), F32)
        q_start(2 + 4 * n, b, qr.at[n])

    def gather_start(n):
        settle(2 + 4 * n, "in")
        for r in range(RR + 1):
            part = qr[n, pl.ds(r, Q, stride=8), :]
            zb[n, r] = part
            zr[n, r, zmine, :] = part
        z_start(
            3 + 4 * n, lambda t: zb.at[n], zr.at[n, :, zmine, :],
            zr.at[n, :, pl.ds(0, (Z - 1) * Q), :],
        )

    def gather_wait(n):
        settle(3 + 4 * n, "in")

    def own_step(n):
        tot = jnp.broadcast_to(zr[n, RR].sum(axis=0, keepdims=True), (8, LANES))
        below = pltpu.roll(tot, LANES - CG, 1)
        row = jnp.where(lane8 < CG, tot / below, jnp.float32(0.0))
        for shift in (8, 16, 32, 64):
            row = row + pltpu.roll(row, shift, 1)
        return row[0:1]

    def coarse_product(n, step=None):
        la = lax.broadcasted_iota(jnp.int32, (ZQ, LANES), 1) >> 5
        pieces = []
        for r in range(RR):
            part = zr[n, r]
            for a in range(NCF):
                hi, lo = split(jnp.where(la == a, part, jnp.float32(0.0)))
                pieces.append(jnp.concatenate([hi, lo], axis=1))
        slots = jnp.concatenate(pieces, axis=0)
        fa = lax.broadcasted_iota(jnp.int32, (NF, LANES), 1)
        acc = dot(scat[...], slots)
        x = acc[:, :LANES] + acc[:, LANES:]
        x = x + pltpu.roll(x, 64, 1)
        x = x + pltpu.roll(x, 32, 1)
        if step is not None:
            x = xf0[...] - step() * x
        xf0[...] = x
        hi = x.astype(BF16).astype(F32)
        v = jnp.where((fa >> 5) == 0, hi, jnp.where((fa >> 5) == 1, x - hi, jnp.float32(0.0)))
        for j in range(NCF):
            xm[pl.ds(j, NF, stride=NCF), :] = jnp.where(((fa >> 3) & 3) == j, v, jnp.float32(0.0))
        xb[...] = xm[...].astype(BF16)
        kc = NC0 // 7
        acc = jnp.zeros((NCZ, LANES), F32)
        for k in range(7):
            cols = slice(k * kc, (k + 1) * kc)
            acc += dot(c_hi[:, cols], xb[cols, :]) + dot(c_lo[:, cols], xb[cols, :])
        y2[...] = acc
        pieces = []
        for j in range(NCF):
            pieces.extend(split(y2[pl.ds(j, NFZ, stride=NCF), :]))
        y = dot(jnp.concatenate(pieces, axis=1), fold4[...])
        hi, lo = split(y)
        both = jnp.concatenate([hi, lo], axis=1)
        for r in range(RR):
            o = jnp.zeros((ZQ, LANES), F32)
            for a in range(NCF):
                g = dot(gath[NCF * r + a], both)
                o = jnp.where(la == a, g[:, :LANES] + g[:, LANES:], o)
            ob[n, r] = o
        mine = xf0[pl.ds(pl.multiple_of(z * NFZ, 8) if NFZ % 8 == 0 else z * NFZ, NFZ), :]
        energy = (mine * y).sum(axis=0, keepdims=True)
        ob[n, RR] = jnp.where(la == 0, energy, jnp.float32(0.0))
        zs = (zs0, zs1)[n]
        zs[z] = ob[n, :, zmine, :]
        z_start(
            4 + 4 * n,
            lambda t: ob.at[n, :, pl.ds(pl.multiple_of(t * Q, Q), Q), :],
            zs.at[z],
            zs.at[pl.ds(0, Z - 1)],
        )

    def backward_start(n):
        zs = (zs0, zs1)[n]
        settle(4 + 4 * n, "in")
        b = qb.at[2 + n]
        for r in range(RR + 1):
            tot = zs[0, r]
            for t in range(1, Z):
                tot = tot + zs[t, r]
            b[pl.ds(r, Q, stride=8), :] = tot
        for r in range(RR + 1, 8):
            b[pl.ds(r, Q, stride=8), :] = jnp.zeros((Q, LANES), F32)
        q_start(5 + 4 * n, b, qr.at[2 + n])

    def backward_finish(n):
        settle(5 + 4 * n, "in")
        acc = jnp.zeros((2 * Q, CG * LANES), F32)
        for r in range(RR + 1):
            part = qr[2 + n, pl.ds(r, Q, stride=8), :]
            hi = part.astype(BF16).astype(F32)
            both = jnp.concatenate([hi, part - hi], axis=0).astype(BF16)
            acc += dot(both, sp[r * LANES:(r + 1) * LANES, :])
        for c in range(CG):
            cols = slice(c * LANES, (c + 1) * LANES)
            yt[pl.ds(c, Q, stride=CG), :] = acc[:Q, cols] + acc[Q:, cols]
        return yt[...].T

    def columns(ys):
        ys = jnp.concatenate([ys, jnp.zeros((32 - NCL, NR), F32)], axis=0)
        hi = ys.astype(BF16).astype(F32)
        return jnp.concatenate([hi, ys - hi, hi, jnp.zeros_like(hi)], axis=0).astype(BF16)

    def add_coarse(n, y, recv):
        half = SUBS * NCL
        for way in range(2):
            ys[n, way] = y[:half]
        pair_start(6 + n, ys.at[n], yr.at[n], 1)
        for s in range(SUBS):
            cols = columns(y[s * NCL:(s + 1) * NCL])

            def body(f, carry):
                k = s * FACES + f
                at = pl.ds(pl.multiple_of(f * E, E), E)
                loc[k] = loc[k] + weight_of(k) * dot(bcol[s, at, :], cols)
                return carry
            lax.fori_loop(0, FACES, body, 0)
        halo_wait(6 + n)
        halo_wait(1 + 2 * n)
        for c in range(2 * SUBS):
            first_row = (c % SUBS) * NCL
            cols = columns(yr[n, c // SUBS, first_row:first_row + NCL, :])
            recv[c] = recv[c] + 0.5 * dot(bface[c], cols)

    def fold(x):
        return x.reshape(E // 8, 8, NR).sum(axis=0)

    nh = max(1, NR // LANES)
    lw = min(NR, LANES)

    def sums_start(n, parts):
        b = arb.at[1 + n]
        b[...] = jnp.zeros((8, LANES), F32)
        for i, part in enumerate(parts):
            line = part.sum(axis=0, keepdims=True)
            for h in range(nh):
                b[pl.ds(i * nh + h, 1), 0:lw] = line[:, h * lw:(h + 1) * lw]
        q_start(10 + 2 * n, b, arr.at[1 + n], shared=True)

    def sums_pass(n):
        settle(10 + 2 * n, "in")
        tot = arr[1 + n].reshape(Q, 8, LANES).sum(axis=0)
        arb[3 + n] = tot
        arz1[n, z] = tot
        z_start(11 + 2 * n, lambda t: arb.at[3 + n], arz1.at[n, z], arz1.at[n, pl.ds(0, Z - 1)])

    def sums_finish(n):
        settle(11 + 2 * n, "in")
        tot = arz1[n, 0]
        for t in range(1, Z):
            tot = tot + arz1[n, t]
        return tot

    def cases(tile, i):
        return jnp.concatenate([tile[i * nh + h:i * nh + h + 1, :lw] for h in range(nh)], axis=1)

    zero8 = jnp.zeros((8, NR), F32)

    halo_wait(0)

    def residual(k, carry):
        r = vld[k] + partner(k, vld, hr0)
        res[k] = r
        put(k, weight_of(k) * r)
        return carry
    lax.fori_loop(0, SLOTS, residual, 0)

    def unscaled(k):
        return jnp.float32(1.0)

    forward_start(0, [coarse_load(s) for s in range(SUBS)])
    local_mul(sinv_hi, sinv_lo, loc, weight_of)
    gather_start(0)
    number_tables()
    gather_wait(0)
    halo_start(1, loc, hs1, hr1)
    coarse_product(0)
    face_tables()
    convert(schur_copy, s_stage, SUBS * NI // s_rows, s_rows, schur_hi, schur_lo)
    backward_start(0)
    add_coarse(0, backward_finish(0), hr1)

    def direction(k, acc):
        d = loc[k] + partner(k, loc, hr1)
        dirn[k] = d
        put(k, d)
        return acc + fold(weight_of(k) * res[k] * d)
    rz_part = lax.fori_loop(0, SLOTS, direction, zero8)

    local_mul(schur_hi, schur_lo, prod, unscaled)
    for s in range(SUBS):
        for place, slot in ((s, ups[s]), (SUBS + s, downs[s])):
            hi, lo = split(prod[slot])
            b = bpart[place]
            x = dot(b, hi)
            gs[place] = 0.5 * (x[:NCL] + x[32:32 + NCL] + dot(b[:32], lo)[:NCL])
    pair_start(5, gs, gr, SUBS)
    halo_start(2, prod, hs2, hr2)

    def image_here(k, acc):
        m = prod[k]
        put(k, weight_of(k) * (m + partner_here(k, prod)))
        return acc + fold(dirn[k] * m)
    da_part = lax.fori_loop(0, SLOTS, image_here, zero8)

    loads = [coarse_load(s) for s in range(SUBS)]
    halo_wait(5)
    for s in range(SUBS):
        loads[s] = loads[s] + gr[place_of(downs[s])[2]] + gr[place_of(ups[s])[2]]
    forward_start(1, loads, [rz_part, da_part])
    sums_start(0, [rz_part, da_part])
    gather_start(1)
    sums_pass(0)
    gather_wait(1)
    coarse_product(1, lambda: own_step(1))
    tot = sums_finish(0)
    rz = cases(tot, 0)
    alpha = rz / cases(tot, 1)
    halo_wait(2)

    def advance(k, carry):
        m = prod[k] + partner(k, prod, hr2)
        img[k] = m
        r = res[k] - alpha * m
        vld[k] = r
        put(k, weight_of(k) * r)
        return carry
    lax.fori_loop(0, SLOTS, advance, 0)

    local_mul(sinv_hi, sinv_lo, loc, weight_of)
    backward_start(1)
    halo_start(3, loc, hs3, hr3)

    def energies(k, acc):
        return acc + fold(vld[k] * loc[k])
    sums_start(1, [lax.fori_loop(0, SLOTS, energies, zero8)])
    y = backward_finish(1)
    coarse_energy = y[SUBS * NCL:SUBS * NCL + NCF].sum(axis=0, keepdims=True)
    sums_pass(1)
    add_coarse(1, y, hr3)

    def second(k, carry):
        pre[k] = loc[k] + partner(k, loc, hr3)
        return carry
    lax.fori_loop(0, SLOTS, second, 0)
    out_alpha[...] = alpha
    out_beta[...] = (cases(sums_finish(1), 0) + coarse_energy) / rz

    for wait in list(owed.values()):
        wait()


def shards(Q, Z, load, schur, schur_inverse, basis, coarse_inverse, partner_slot, edge_map, coarse_number):
    E, NR = load.shape[2], load.shape[3]
    NI = FACES * E
    NCZ, NC0 = coarse_inverse.shape
    NF = NC0 // NCF
    ZQ = Z * Q
    RR = SLOTS * NCF * CG // LANES
    vec = pltpu.VMEM((SLOTS, E, NR), F32)
    halo = pltpu.VMEM((2 * SUBS, E, NR), F32)
    mat = pltpu.VMEM((SUBS * NI, NI), BF16)
    out = pltpu.VMEM((SLOTS, E, NR), F32)
    ratio = pltpu.VMEM((1, NR), F32)
    NCL = FACES * NCF
    anywhere = pl.BlockSpec(memory_space=pl.ANY)
    vmem = pl.BlockSpec(memory_space=pltpu.VMEM)
    smem = pl.BlockSpec(memory_space=pltpu.SMEM)
    direction, residual, image, preconditioned, alpha, beta = pl.pallas_call(
        functools.partial(kernel, Q, Z),
        out_shape=(out, out, out, out, ratio, ratio),
        in_specs=[anywhere, anywhere, anywhere, vmem, anywhere, smem, vmem, smem],
        out_specs=(vmem,) * 6,
        scratch_shapes=[vec] * 3 + [halo] * 8 + [mat] * 4 + [
            pltpu.VMEM((NCZ, NC0), BF16),
            pltpu.VMEM((NCZ, NC0), BF16),
            pltpu.VMEM((2, 2 * E, NI), F32),
            pltpu.VMEM((2, NCZ // 7, NC0), F32),
            pltpu.VMEM((SUBS * NI, NR), BF16),
            pltpu.VMEM((SUBS * NI, NR), BF16),
            pltpu.VMEM((SLOTS, E, 2 * E), BF16),
            pltpu.VMEM((SUBS, 32, NI), BF16),
            pltpu.VMEM((SUBS, 32, NI), BF16),
            pltpu.VMEM((SUBS, NI, LANES), BF16),
            pltpu.VMEM((2 * SUBS, E, LANES), BF16),
            pltpu.VMEM((2 * SUBS, 64, E), BF16),
            pltpu.VMEM((2 * SUBS, NCL, E), F32),
            pltpu.VMEM((2 * SUBS, NCL, E), F32),
            pltpu.VMEM((2 * SUBS, NCL, NR), F32),
            pltpu.VMEM((2 * SUBS, NCL, NR), F32),
            pltpu.VMEM((2, 2, SUBS * NCL, NR), F32),
            pltpu.VMEM((2, 2, SUBS * NCL, NR), F32),
            pltpu.VMEM(((RR + 1) * LANES, CG * LANES), BF16),
            pltpu.VMEM((CG * LANES, (RR + 1) * LANES), BF16),
            pltpu.VMEM((2 * NCF * LANES, LANES), BF16),
            pltpu.VMEM((NF, SLOTS * ZQ), BF16),
            pltpu.VMEM((SLOTS, ZQ, NF // Z), BF16),
            pltpu.VMEM((LANES, NR), F32),
            pltpu.VMEM((NR, LANES), F32),
            pltpu.VMEM((NR, LANES), F32),
            pltpu.VMEM((NC0, LANES), F32),
            pltpu.VMEM((NC0, LANES), BF16),
            pltpu.VMEM((NF, LANES), F32),
            pltpu.VMEM((NCZ, LANES), F32),
            pltpu.VMEM((4, Q * 8, LANES), F32),
            pltpu.VMEM((4, Q * 8, LANES), F32),
            pltpu.VMEM((2, RR + 1, Q, LANES), F32),
            pltpu.VMEM((2, RR + 1, ZQ, LANES), F32),
            pltpu.VMEM((2, RR + 1, ZQ, LANES), F32),
            pltpu.VMEM((Z, RR + 1, Q, LANES), F32),
            pltpu.VMEM((Z, RR + 1, Q, LANES), F32),
            pltpu.VMEM((5, 8, LANES), F32),
            pltpu.VMEM((3, Q * 8, LANES), F32),
            pltpu.VMEM((Q, LANES), F32),
            pltpu.VMEM((2, Z, 8, LANES), F32),
            pltpu.VMEM((ZQ, LANES), F32),
            pltpu.SemaphoreType.DMA,
            pltpu.SemaphoreType.DMA((2,)),
            pltpu.SemaphoreType.DMA((2,)),
            pltpu.SemaphoreType.DMA((14,)),
            pltpu.SemaphoreType.DMA((14,)),
            pltpu.SemaphoreType.DMA((8, 2)),
            pltpu.SemaphoreType.DMA((8, 2)),
        ],
        compiler_params=pltpu.CompilerParams(
            collective_id=0, has_side_effects=True, vmem_limit_bytes=56 * 1024 * 1024
        ),
    )(
        load.reshape(SLOTS, E, NR),
        schur.reshape(SUBS * NI, NI),
        schur_inverse.reshape(SUBS * NI, NI),
        jnp.swapaxes(basis, 1, 2),
        coarse_inverse,
        partner_slot,
        jnp.swapaxes(edge_map, 0, 1),
        coarse_number,
    )
    return tuple(
        o.reshape(load.shape)
        for o in (alpha * direction, residual - alpha * image, preconditioned + beta * direction)
    )


def solution(mesh):
    both = ("sub", "coarse")
    placed = (
        P(both, None, None, None),
        P(both, None, None),
        P(both, None, None),
        P(both, None, None),
        P("coarse", None),
        P(both, None),
        P(both, None, None),
        P(both, None),
    )
    return jax.shard_map(
        functools.partial(shards, mesh.shape["sub"], mesh.shape["coarse"]),
        mesh=mesh,
        in_specs=placed,
        out_specs=(P(both, None, None, None),) * 3,
        check_vma=False,
    )
```

```python
import functools

import jax
import jax.numpy as jnp
import numpy as np
from jax import lax
from jax.experimental import pallas as pl
from jax.experimental.pallas import tpu as pltpu
from jax.sharding import PartitionSpec as P

MESH = pl.DeviceIdType.MESH
F32 = jnp.float32
BF16 = jnp.bfloat16
FACES = 6
SUBS = 2
SLOTS = FACES * SUBS
NCF = 4
LANES = 128
CG = 8


def split(x):
    hi = x.astype(BF16)
    return hi, (x - hi.astype(F32)).astype(BF16)


def dot(a, b):
    return jnp.dot(a, b, preferred_element_type=F32)


def kernel(
    Q, Z, load, schur, sinv, basis_t, coarse, ps, em, cn, sp_in, spt_in, fold4_in,
    dirn, res, img, pre, out_alpha, out_beta,
    vld, loc, prod,
    hs0, hs1, hs2, hs3, hr0, hr1, hr2, hr3,
    sinv_hi, sinv_lo, schur_hi, schur_lo, c_hi, c_lo, s_stage, c_stage,
    hh, hl, perm, bt_hi, bt_lo, bcol, bface, bpart, bs, br, gs, gr, ys, yr, sp, spt,
    fold4, scat, gath, xbuf, xt, yt, xm, xb, xf0, y2,
    qb, qr, zb, zr, ob, zs0, zs1, arb, arr, arz0, arz1, cnz,
    in_sem, tab_sem, st_sem, ct_sem, q_send, q_recv, h_send, h_recv,
):
    q = lax.axis_index("sub")
    z = lax.axis_index("coarse")
    E = vld.shape[1]
    NR = vld.shape[2]
    ZQ = Z * Q
    NCZ = c_hi.shape[0]
    NC0 = c_hi.shape[1]
    NF = NC0 // NCF
    NFZ = NF // Z
    RR = SLOTS * NCF * CG // LANES
    ndev = Q * Z
    me = q * Z + z
    nxt = lax.rem(me + 1, ndev)
    prv = lax.rem(me + ndev - 1, ndev)
    nxt_id = (nxt // Z, lax.rem(nxt, Z))
    prv_id = (prv // Z, lax.rem(prv, Z))

    def q_peer(k):
        return lax.rem(q + k, Q)

    def z_peer(k):
        return lax.rem(z + k, Z)

    owed = {}

    def owe(key, ref, sem):
        owed[key] = lambda: pltpu.make_async_copy(ref, ref, sem).wait()

    def settle(*key):
        owed.pop(key)()

    load_copy = pltpu.make_async_copy(load, vld, in_sem)
    load_copy.start()

    def stager(src, rows, stage, sem):
        def copy(i, slot):
            return pltpu.make_async_copy(
                src.at[pl.ds(pl.multiple_of(i * rows, rows), rows), :], stage.at[slot], sem.at[slot]
            )
        return copy

    s_rows = s_stage.shape[1]
    c_rows = c_stage.shape[1]
    sinv_copy = stager(sinv, s_rows, s_stage, st_sem)
    schur_copy = stager(schur, s_rows, s_stage, st_sem)
    c_copy = stager(coarse, c_rows, c_stage, ct_sem)

    def first(copy):
        copy(0, 0).start()
        copy(1, 1).start()
        owed[copy] = lambda: (copy(0, 0).wait(), copy(1, 1).wait())

    def convert(copy, stage, n, rows, hi_ref, lo_ref):
        def body(i, carry):
            slot = lax.rem(i, 2)
            copy(i, slot).wait()
            hi, lo = split(stage[slot])
            at = pl.ds(pl.multiple_of(i * rows, rows), rows)
            hi_ref[at, :] = hi
            lo_ref[at, :] = lo

            @pl.when(i + 2 < n)
            def _():
                copy(i + 2, slot).start()
            return carry
        lax.fori_loop(0, n, body, 0)
        owed.pop(copy)

    first(sinv_copy)
    first(c_copy)
    tables = [
        pltpu.make_async_copy(src, dst, tab_sem.at[i])
        for i, (src, dst) in enumerate(((sp_in, sp), (spt_in, spt), (fold4_in, fold4)))
    ]
    for copy in tables:
        copy.start()

    barrier = pltpu.get_barrier_semaphore()

    def greet(device):
        pl.semaphore_signal(barrier, inc=1, device_id=device, device_id_type=MESH)

    lax.fori_loop(1, Q, lambda k, c: (greet((q_peer(k), z)), c)[1], 0)
    for k in range(1, Z):
        greet((q, z_peer(k)))
    greet(nxt_id)
    greet(prv_id)

    lane8 = lax.broadcasted_iota(jnp.int32, (8, LANES), 1)

    def q_start(ph, src, dst, shared=False):
        def body(i, carry):
            p = q_peer(1 + lax.rem(i + Q // 2 - 1, Q - 1))
            block = src if shared else src.at[pl.ds(pl.multiple_of(p * 8, 8), 8), :]
            pltpu.make_async_remote_copy(
                src_ref=block,
                dst_ref=dst.at[pl.ds(pl.multiple_of(q * 8, 8), 8), :],
                send_sem=q_send.at[ph], recv_sem=q_recv.at[ph],
                device_id=(p, z), device_id_type=MESH,
            ).start()
            return carry
        lax.fori_loop(0, Q - 1, body, 0)
        mine = pl.ds(pl.multiple_of(q * 8, 8), 8)
        dst[mine, :] = src[...] if shared else src[mine, :]
        every = dst.at[pl.ds(0, (Q - 1) * 8), :]
        owe((ph, "in"), every, q_recv.at[ph])
        owe((ph, "out"), every, q_send.at[ph])

    def z_start(ph, src_of, dst, three):
        for k in sorted(range(1, Z), key=lambda k: -min(k, Z - k)):
            t = z_peer(k)
            pltpu.make_async_remote_copy(
                src_ref=src_of(t), dst_ref=dst,
                send_sem=q_send.at[ph], recv_sem=q_recv.at[ph],
                device_id=(q, t), device_id_type=MESH,
            ).start()
        owe((ph, "in"), three, q_recv.at[ph])
        owe((ph, "out"), three, q_send.at[ph])

    def rel_of(k):
        p = ps[k // FACES, lax.rem(k, FACES)]
        rel = p - me * SLOTS
        rel = jnp.where(rel < -SLOTS, rel + ndev * SLOTS, rel)
        rel = jnp.where(rel >= 2 * SLOTS, rel - ndev * SLOTS, rel)
        return p, rel

    def weight_of(k):
        return jnp.where(ps[k // FACES, lax.rem(k, FACES)] >= 0, jnp.float32(0.5), jnp.float32(1.0))

    ups, downs = [], []
    for s in range(SUBS):
        up = jnp.int32(0)
        down = jnp.int32(0)
        for f in range(FACES):
            p, rel = rel_of(s * FACES + f)
            here = p >= 0
            up = jnp.where(here & (rel >= SLOTS), s * FACES + f, up)
            down = jnp.where(here & (rel < 0), s * FACES + f, down)
        ups.append(up)
        downs.append(down)

    def pair_start(h, send, recv, count):
        for way, device in ((0, nxt_id), (1, prv_id)):
            part = pl.ds(way * count, count)
            pltpu.make_async_remote_copy(
                src_ref=send.at[part], dst_ref=recv.at[part],
                send_sem=h_send.at[h, way], recv_sem=h_recv.at[h, way],
                device_id=device, device_id_type=MESH,
            ).start()
            owe((h, way, "halo in"), recv.at[part], h_recv.at[h, way])
            owe((h, way, "halo out"), recv.at[part], h_send.at[h, way])

    def halo_start(h, v, send, recv):
        for s in range(SUBS):
            send[s] = v[ups[s]]
            send[SUBS + s] = v[downs[s]]
        pair_start(h, send, recv, SUBS)

    def half_start(h, s, v, send, recv):
        for way, slot, device in ((0, ups[s], nxt_id), (1, downs[s], prv_id)):
            place = way * SUBS + s
            send[place] = v[slot]
            part = pl.ds(place, 1)
            pltpu.make_async_remote_copy(
                src_ref=send.at[part], dst_ref=recv.at[part],
                send_sem=h_send.at[h, way], recv_sem=h_recv.at[h, way],
                device_id=device, device_id_type=MESH,
            ).start()
            owe((h, way, "halo in"), recv.at[part], h_recv.at[h, way])
            owe((h, way, "halo out"), recv.at[part], h_send.at[h, way])

    def halo_wait(h):
        settle(h, 0, "halo in")
        settle(h, 1, "halo in")

    def place_of(k):
        p, rel = rel_of(k)
        local = (rel >= 0) & (rel < SLOTS)
        inside = jnp.clip(rel, 0, SLOTS - 1)
        below = (rel + SLOTS >= FACES).astype(jnp.int32)
        above = SUBS + (rel - SLOTS >= FACES).astype(jnp.int32)
        return local, inside, jnp.clip(jnp.where(rel < 0, below, above), 0, 2 * SUBS - 1)

    def permute(k, val):
        hi, lo = split(val)
        return dot(perm[k], jnp.concatenate([hi, lo], axis=0))

    def partner(k, v, recv):
        local, inside, outside = place_of(k)
        return permute(k, jnp.where(local, v[inside], recv[outside]))

    def partner_here(k, v):
        local, inside, outside = place_of(k)
        return permute(k, jnp.where(local, v[inside], jnp.float32(0.0)))

    rows_e = lax.broadcasted_iota(jnp.int32, (E, E), 0)
    for k in range(SLOTS):
        line = em[k % FACES, pl.ds(k // FACES, 1), :]
        one = jnp.where(rows_e == line, jnp.float32(1.0), jnp.float32(0.0)).T
        one = jnp.where(ps[k // FACES, k % FACES] >= 0, one, jnp.zeros_like(one)).astype(BF16)
        perm[k] = jnp.concatenate([one, one], axis=1)

    NI = FACES * E
    NCL = FACES * NCF
    convert(sinv_copy, s_stage, SUBS * NI // s_rows, s_rows, sinv_hi, sinv_lo)
    first(schur_copy)
    load_copy.wait()
    pl.semaphore_wait(barrier, Q + Z)
    halo_start(0, vld, hs0, hr0)

    row = jnp.zeros((8, LANES), F32)
    for k in range(SLOTS):
        row = jnp.where(lane8 == k, cn[k // FACES, k % FACES].astype(F32), row)
    arb[0] = row
    q_start(0, arb.at[0], arr.at[0], shared=True)

    for s in range(SUBS):
        for place, slot in ((s, ups[s]), (SUBS + s, downs[s])):
            face = jnp.zeros((NCL, E), F32)
            for f in range(FACES):
                face = jnp.where(slot == s * FACES + f, basis_t[s, :, f * E:(f + 1) * E], face)
            bs[place] = face
    pair_start(4, bs, br, SUBS)

    zrow = jnp.zeros((32 - NCL, NI), F32)
    for s in range(SUBS):
        b = basis_t[s]
        bh = b.astype(BF16).astype(F32)
        bl = b - bh
        bh = jnp.concatenate([bh, zrow], axis=0)
        bl = jnp.concatenate([bl, zrow], axis=0)
        bt_hi[s] = bh.astype(BF16)
        bt_lo[s] = bl.astype(BF16)
        bcol[s] = jnp.concatenate([bh, bh, bl, jnp.zeros_like(bl)], axis=0).T.astype(BF16)

    xbuf[...] = jnp.zeros_like(xbuf)

    convert(c_copy, c_stage, NCZ // c_rows, c_rows, c_hi, c_lo)
    for copy in tables:
        copy.wait()

    settle(0, "in")
    zmine = pl.ds(pl.multiple_of(z * Q, Q), Q)
    arz0[...] = arr[0, pl.ds(0, Q, stride=8), :]
    cnz[zmine, :] = arz0[...]
    z_start(1, lambda t: arz0, cnz.at[zmine, :], cnz.at[pl.ds(0, (Z - 1) * Q), :])

    def number_tables():
        settle(1, "in")
        cns = cnz[...]
        cnt = cns.T if ZQ == LANES else jnp.concatenate([cns, jnp.zeros((LANES - ZQ, LANES), F32)], axis=0).T
        face0 = lax.broadcasted_iota(jnp.int32, (NF, ZQ), 0).astype(F32)
        face1 = lax.broadcasted_iota(jnp.int32, (ZQ, NFZ), 1).astype(F32) + (z * NFZ).astype(F32)
        for k in range(SLOTS):
            scat[:, k * ZQ:(k + 1) * ZQ] = jnp.where(
                face0 == cnt[k:k + 1, :ZQ], jnp.float32(1.0), jnp.float32(0.0)
            ).astype(BF16)
            gath[k] = jnp.where(
                cns[:, k:k + 1] == face1, jnp.float32(1.0), jnp.float32(0.0)
            ).astype(BF16)

    def face_tables():
        settle(4, 0, "halo in")
        settle(4, 1, "halo in")
        pad = jnp.zeros((32 - NCL, E), F32)
        for c in range(2 * SUBS):
            b = jnp.concatenate([br[c], pad], axis=0)
            bh = b.astype(BF16).astype(F32)
            bface[c] = jnp.concatenate([bh, bh, b - bh, jnp.zeros_like(bh)], axis=0).T.astype(BF16)
        for s in range(SUBS):
            for place, slot in ((s, ups[s]), (SUBS + s, downs[s])):
                local, inside, outside = place_of(slot)
                b = jnp.concatenate([br[outside], pad], axis=0)
                bh = b.astype(BF16).astype(F32)
                both = jnp.concatenate([bh, b - bh], axis=0).astype(BF16)
                bpart[place] = lax.dot_general(
                    both, perm[slot][:, :E], (((1,), (1,)), ((), ())), preferred_element_type=F32
                ).astype(BF16)

    def put(k, x):
        hi, lo = split(x)
        at = pl.ds(pl.multiple_of(k * E, E), E)
        hh[at, :] = hi
        hl[at, :] = lo

    def local_mul(a_hi, a_lo, out, scale, subs=range(SUBS)):
        rows = 2 * E
        per = NI // rows

        def body(i, carry):
            at = pl.ds(pl.multiple_of(i * rows, rows), rows)
            sub = pl.ds(pl.multiple_of((i // per) * NI, NI), NI)
            hi = a_hi[at, :]
            top = hh[sub, :]
            acc = dot(hi, top) + dot(hi, hl[sub, :]) + dot(a_lo[at, :], top)
            out[2 * i] = scale(2 * i) * acc[:E]
            out[2 * i + 1] = scale(2 * i + 1) * acc[E:]
            return carry
        lax.fori_loop(subs[0] * per, (subs[-1] + 1) * per, body, 0)

    def coarse_load(s):
        sub = pl.ds(s * NI, NI)
        top = hh[sub, :]
        x = dot(bt_hi[s], top) + dot(bt_hi[s], hl[sub, :]) + dot(bt_lo[s], top)
        return x[:NCL]

    def forward_start(n, loads, sums=()):
        for s in range(SUBS):
            xbuf[s * NCL:(s + 1) * NCL, :] = loads[s]
        for i, part in enumerate(sums):
            xbuf[pl.ds(SUBS * NCL + i, 1), :] = part.sum(axis=0, keepdims=True)
        xt[...] = xbuf[...].T
        acc = jnp.zeros((2 * Q, (RR + 1) * LANES), F32)
        for c in range(CG):
            part = xt[pl.ds(c, Q, stride=CG), :]
            hi = part.astype(BF16).astype(F32)
            both = jnp.concatenate([hi, part - hi], axis=0).astype(BF16)
            acc += dot(both, spt[c * LANES:(c + 1) * LANES, :])
        acc = acc[:Q] + acc[Q:]
        b = qb.at[n]
        for r in range(RR + 1):
            b[pl.ds(r, Q, stride=8), :] = acc[:, r * LANES:(r + 1) * LANES]
        for r in range(RR + 1, 8):
            b[pl.ds(r, Q, stride=8), :] = jnp.zeros((Q, LANES), F32)
        q_start(2 + 4 * n, b, qr.at[n])

    def gather_start(n):
        settle(2 + 4 * n, "in")
        for r in range(RR + 1):
            part = qr[n, pl.ds(r, Q, stride=8), :]
            zb[n, r] = part
            zr[n, r, zmine, :] = part
        z_start(
            3 + 4 * n, lambda t: zb.at[n], zr.at[n, :, zmine, :],
            zr.at[n, :, pl.ds(0, (Z - 1) * Q), :],
        )

    def gather_wait(n):
        settle(3 + 4 * n, "in")

    def own_step(n):
        tot = jnp.broadcast_to(zr[n, RR].sum(axis=0, keepdims=True), (8, LANES))
        below = pltpu.roll(tot, LANES - CG, 1)
        row = jnp.where(lane8 < CG, tot / below, jnp.float32(0.0))
        for shift in (8, 16, 32, 64):
            row = row + pltpu.roll(row, shift, 1)
        return row[0:1]

    def coarse_product(n, step=None):
        la = lax.broadcasted_iota(jnp.int32, (ZQ, LANES), 1) >> 5
        pieces = []
        for r in range(RR):
            part = zr[n, r]
            for a in range(NCF):
                hi, lo = split(jnp.where(la == a, part, jnp.float32(0.0)))
                pieces.append(jnp.concatenate([hi, lo], axis=1))
        slots = jnp.concatenate(pieces, axis=0)
        fa = lax.broadcasted_iota(jnp.int32, (NF, LANES), 1)
        acc = dot(scat[...], slots)
        x = acc[:, :LANES] + acc[:, LANES:]
        x = x + pltpu.roll(x, 64, 1)
        x = x + pltpu.roll(x, 32, 1)
        if step is not None:
            x = xf0[...] - step() * x
        xf0[...] = x
        hi = x.astype(BF16).astype(F32)
        v = jnp.where((fa >> 5) == 0, hi, jnp.where((fa >> 5) == 1, x - hi, jnp.float32(0.0)))
        for j in range(NCF):
            xm[pl.ds(j, NF, stride=NCF), :] = jnp.where(((fa >> 3) & 3) == j, v, jnp.float32(0.0))
        xb[...] = xm[...].astype(BF16)
        kc = NC0 // 7
        acc = jnp.zeros((NCZ, LANES), F32)
        for k in range(7):
            cols = slice(k * kc, (k + 1) * kc)
            acc += dot(c_hi[:, cols], xb[cols, :]) + dot(c_lo[:, cols], xb[cols, :])
        y2[...] = acc
        pieces = []
        for j in range(NCF):
            pieces.extend(split(y2[pl.ds(j, NFZ, stride=NCF), :]))
        y = dot(jnp.concatenate(pieces, axis=1), fold4[...])
        hi, lo = split(y)
        both = jnp.concatenate([hi, lo], axis=1)
        for r in range(RR):
            o = jnp.zeros((ZQ, LANES), F32)
            for a in range(NCF):
                g = dot(gath[NCF * r + a], both)
                o = jnp.where(la == a, g[:, :LANES] + g[:, LANES:], o)
            ob[n, r] = o
        mine = xf0[pl.ds(pl.multiple_of(z * NFZ, 8) if NFZ % 8 == 0 else z * NFZ, NFZ), :]
        energy = (mine * y).sum(axis=0, keepdims=True)
        ob[n, RR] = jnp.where(la == 0, energy, jnp.float32(0.0))
        zs = (zs0, zs1)[n]
        zs[z] = ob[n, :, zmine, :]
        z_start(
            4 + 4 * n,
            lambda t: ob.at[n, :, pl.ds(pl.multiple_of(t * Q, Q), Q), :],
            zs.at[z],
            zs.at[pl.ds(0, Z - 1)],
        )

    def backward_start(n):
        zs = (zs0, zs1)[n]
        settle(4 + 4 * n, "in")
        b = qb.at[2 + n]
        for r in range(RR + 1):
            tot = zs[0, r]
            for t in range(1, Z):
                tot = tot + zs[t, r]
            b[pl.ds(r, Q, stride=8), :] = tot
        for r in range(RR + 1, 8):
            b[pl.ds(r, Q, stride=8), :] = jnp.zeros((Q, LANES), F32)
        q_start(5 + 4 * n, b, qr.at[2 + n])

    def backward_finish(n):
        settle(5 + 4 * n, "in")
        acc = jnp.zeros((2 * Q, CG * LANES), F32)
        for r in range(RR + 1):
            part = qr[2 + n, pl.ds(r, Q, stride=8), :]
            hi = part.astype(BF16).astype(F32)
            both = jnp.concatenate([hi, part - hi], axis=0).astype(BF16)
            acc += dot(both, sp[r * LANES:(r + 1) * LANES, :])
        for c in range(CG):
            cols = slice(c * LANES, (c + 1) * LANES)
            yt[pl.ds(c, Q, stride=CG), :] = acc[:Q, cols] + acc[Q:, cols]
        return yt[...].T

    def columns(ys):
        ys = jnp.concatenate([ys, jnp.zeros((32 - NCL, NR), F32)], axis=0)
        hi = ys.astype(BF16).astype(F32)
        return jnp.concatenate([hi, ys - hi, hi, jnp.zeros_like(hi)], axis=0).astype(BF16)

    def share_coarse(n, y):
        for way in range(2):
            ys[n, way] = y[:SUBS * NCL]
        pair_start(6 + n, ys.at[n], yr.at[n], 1)

    def add_coarse(n, y, recv):
        for s in range(SUBS):
            cols = columns(y[s * NCL:(s + 1) * NCL])

            def body(f, carry):
                k = s * FACES + f
                at = pl.ds(pl.multiple_of(f * E, E), E)
                loc[k] = loc[k] + weight_of(k) * dot(bcol[s, at, :], cols)
                return carry
            lax.fori_loop(0, FACES, body, 0)
        halo_wait(6 + n)
        halo_wait(1 + 2 * n)
        halo_wait(8 + n)
        for c in range(2 * SUBS):
            first_row = (c % SUBS) * NCL
            cols = columns(yr[n, c // SUBS, first_row:first_row + NCL, :])
            recv[c] = recv[c] + 0.5 * dot(bface[c], cols)

    def fold(x):
        return x.reshape(E // 8, 8, NR).sum(axis=0)

    nh = max(1, NR // LANES)
    lw = min(NR, LANES)

    def sums_start(n, parts):
        b = arb.at[1 + n]
        b[...] = jnp.zeros((8, LANES), F32)
        for i, part in enumerate(parts):
            line = part.sum(axis=0, keepdims=True)
            for h in range(nh):
                b[pl.ds(i * nh + h, 1), 0:lw] = line[:, h * lw:(h + 1) * lw]
        q_start(10 + 2 * n, b, arr.at[1 + n], shared=True)

    def sums_pass(n):
        settle(10 + 2 * n, "in")
        tot = arr[1 + n].reshape(Q, 8, LANES).sum(axis=0)
        arb[3 + n] = tot
        arz1[n, z] = tot
        z_start(11 + 2 * n, lambda t: arb.at[3 + n], arz1.at[n, z], arz1.at[n, pl.ds(0, Z - 1)])

    def sums_finish(n):
        settle(11 + 2 * n, "in")
        tot = arz1[n, 0]
        for t in range(1, Z):
            tot = tot + arz1[n, t]
        return tot

    def cases(tile, i):
        return jnp.concatenate([tile[i * nh + h:i * nh + h + 1, :lw] for h in range(nh)], axis=1)

    zero8 = jnp.zeros((8, NR), F32)

    halo_wait(0)

    def residual(k, carry):
        r = vld[k] + partner(k, vld, hr0)
        res[k] = r
        put(k, weight_of(k) * r)
        return carry
    lax.fori_loop(0, SLOTS, residual, 0)

    def unscaled(k):
        return jnp.float32(1.0)

    forward_start(0, [coarse_load(s) for s in range(SUBS)])
    local_mul(sinv_hi, sinv_lo, loc, weight_of, (0,))
    half_start(1, 0, loc, hs1, hr1)
    local_mul(sinv_hi, sinv_lo, loc, weight_of, (1,))
    gather_start(0)
    number_tables()
    gather_wait(0)
    half_start(8, 1, loc, hs1, hr1)
    coarse_product(0)
    face_tables()
    convert(schur_copy, s_stage, SUBS * NI // s_rows, s_rows, schur_hi, schur_lo)
    backward_start(0)
    y = backward_finish(0)
    share_coarse(0, y)
    add_coarse(0, y, hr1)

    def direction(k, acc):
        d = loc[k] + partner(k, loc, hr1)
        dirn[k] = d
        put(k, d)
        return acc + fold(weight_of(k) * res[k] * d)
    rz_part = lax.fori_loop(0, SLOTS, direction, zero8)

    local_mul(schur_hi, schur_lo, prod, unscaled)
    for s in range(SUBS):
        for place, slot in ((s, ups[s]), (SUBS + s, downs[s])):
            hi, lo = split(prod[slot])
            b = bpart[place]
            x = dot(b, hi)
            gs[place] = 0.5 * (x[:NCL] + x[32:32 + NCL] + dot(b[:32], lo)[:NCL])
    pair_start(5, gs, gr, SUBS)
    halo_start(2, prod, hs2, hr2)

    def image_here(k, acc):
        m = prod[k]
        put(k, weight_of(k) * (m + partner_here(k, prod)))
        return acc + fold(dirn[k] * m)
    da_part = lax.fori_loop(0, SLOTS, image_here, zero8)

    loads = [coarse_load(s) for s in range(SUBS)]
    halo_wait(5)
    for s in range(SUBS):
        loads[s] = loads[s] + gr[place_of(downs[s])[2]] + gr[place_of(ups[s])[2]]
    forward_start(1, loads, [rz_part, da_part])
    sums_start(0, [rz_part, da_part])
    gather_start(1)
    sums_pass(0)
    gather_wait(1)
    coarse_product(1, lambda: own_step(1))
    tot = sums_finish(0)
    rz = cases(tot, 0)
    alpha = rz / cases(tot, 1)
    halo_wait(2)

    def advance(k, carry):
        m = prod[k] + partner(k, prod, hr2)
        img[k] = m
        r = res[k] - alpha * m
        vld[k] = r
        put(k, weight_of(k) * r)
        return carry
    lax.fori_loop(0, SLOTS, advance, 0)

    local_mul(sinv_hi, sinv_lo, loc, weight_of, (0,))
    half_start(3, 0, loc, hs3, hr3)
    local_mul(sinv_hi, sinv_lo, loc, weight_of, (1,))
    backward_start(1)
    half_start(9, 1, loc, hs3, hr3)

    def energies(k, acc):
        return acc + fold(vld[k] * loc[k])
    sums_start(1, [lax.fori_loop(0, SLOTS, energies, zero8)])
    y = backward_finish(1)
    share_coarse(1, y)
    coarse_energy = y[SUBS * NCL:SUBS * NCL + NCF].sum(axis=0, keepdims=True)
    sums_pass(1)
    add_coarse(1, y, hr3)

    def second(k, carry):
        pre[k] = loc[k] + partner(k, loc, hr3)
        return carry
    lax.fori_loop(0, SLOTS, second, 0)
    out_alpha[...] = alpha
    out_beta[...] = (cases(sums_finish(1), 0) + coarse_energy) / rz

    for wait in list(owed.values()):
        wait()


def one_hot_tables():
    rows = (SLOTS * NCF * CG // LANES + 1) * LANES
    i0 = np.arange(rows)[:, None]
    i1 = np.arange(CG * LANES)[None, :]
    table = i1 == (i0 % CG) * LANES + (i0 // LANES) * (LANES // CG) + i0 % LANES // CG
    m0 = np.arange(2 * NCF * LANES)[:, None]
    m1 = np.arange(LANES)[None, :]
    fold = (m0 % CG == m1 % CG) & (m0 // (2 * LANES) == m1 // CG % NCF)
    return [jnp.asarray(t.astype(np.float32), BF16) for t in (table, table.T, fold)]


def shards(Q, Z, load, schur, schur_inverse, basis, coarse_inverse, partner_slot, edge_map, coarse_number):
    E, NR = load.shape[2], load.shape[3]
    NI = FACES * E
    NCZ, NC0 = coarse_inverse.shape
    NF = NC0 // NCF
    ZQ = Z * Q
    RR = SLOTS * NCF * CG // LANES
    vec = pltpu.VMEM((SLOTS, E, NR), F32)
    halo = pltpu.VMEM((2 * SUBS, E, NR), F32)
    mat = pltpu.VMEM((SUBS * NI, NI), BF16)
    out = pltpu.VMEM((SLOTS, E, NR), F32)
    ratio = pltpu.VMEM((1, NR), F32)
    NCL = FACES * NCF
    anywhere = pl.BlockSpec(memory_space=pl.ANY)
    vmem = pl.BlockSpec(memory_space=pltpu.VMEM)
    smem = pl.BlockSpec(memory_space=pltpu.SMEM)
    direction, residual, image, preconditioned, alpha, beta = pl.pallas_call(
        functools.partial(kernel, Q, Z),
        out_shape=(out, out, out, out, ratio, ratio),
        in_specs=[anywhere, anywhere, anywhere, vmem, anywhere, smem, vmem, smem] + [anywhere] * 3,
        out_specs=(vmem,) * 6,
        scratch_shapes=[vec] * 3 + [halo] * 8 + [mat] * 4 + [
            pltpu.VMEM((NCZ, NC0), BF16),
            pltpu.VMEM((NCZ, NC0), BF16),
            pltpu.VMEM((2, 2 * E, NI), F32),
            pltpu.VMEM((2, NCZ // 7, NC0), F32),
            pltpu.VMEM((SUBS * NI, NR), BF16),
            pltpu.VMEM((SUBS * NI, NR), BF16),
            pltpu.VMEM((SLOTS, E, 2 * E), BF16),
            pltpu.VMEM((SUBS, 32, NI), BF16),
            pltpu.VMEM((SUBS, 32, NI), BF16),
            pltpu.VMEM((SUBS, NI, LANES), BF16),
            pltpu.VMEM((2 * SUBS, E, LANES), BF16),
            pltpu.VMEM((2 * SUBS, 64, E), BF16),
            pltpu.VMEM((2 * SUBS, NCL, E), F32),
            pltpu.VMEM((2 * SUBS, NCL, E), F32),
            pltpu.VMEM((2 * SUBS, NCL, NR), F32),
            pltpu.VMEM((2 * SUBS, NCL, NR), F32),
            pltpu.VMEM((2, 2, SUBS * NCL, NR), F32),
            pltpu.VMEM((2, 2, SUBS * NCL, NR), F32),
            pltpu.VMEM(((RR + 1) * LANES, CG * LANES), BF16),
            pltpu.VMEM((CG * LANES, (RR + 1) * LANES), BF16),
            pltpu.VMEM((2 * NCF * LANES, LANES), BF16),
            pltpu.VMEM((NF, SLOTS * ZQ), BF16),
            pltpu.VMEM((SLOTS, ZQ, NF // Z), BF16),
            pltpu.VMEM((LANES, NR), F32),
            pltpu.VMEM((NR, LANES), F32),
            pltpu.VMEM((NR, LANES), F32),
            pltpu.VMEM((NC0, LANES), F32),
            pltpu.VMEM((NC0, LANES), BF16),
            pltpu.VMEM((NF, LANES), F32),
            pltpu.VMEM((NCZ, LANES), F32),
            pltpu.VMEM((4, Q * 8, LANES), F32),
            pltpu.VMEM((4, Q * 8, LANES), F32),
            pltpu.VMEM((2, RR + 1, Q, LANES), F32),
            pltpu.VMEM((2, RR + 1, ZQ, LANES), F32),
            pltpu.VMEM((2, RR + 1, ZQ, LANES), F32),
            pltpu.VMEM((Z, RR + 1, Q, LANES), F32),
            pltpu.VMEM((Z, RR + 1, Q, LANES), F32),
            pltpu.VMEM((5, 8, LANES), F32),
            pltpu.VMEM((3, Q * 8, LANES), F32),
            pltpu.VMEM((Q, LANES), F32),
            pltpu.VMEM((2, Z, 8, LANES), F32),
            pltpu.VMEM((ZQ, LANES), F32),
            pltpu.SemaphoreType.DMA,
            pltpu.SemaphoreType.DMA((3,)),
            pltpu.SemaphoreType.DMA((2,)),
            pltpu.SemaphoreType.DMA((2,)),
            pltpu.SemaphoreType.DMA((14,)),
            pltpu.SemaphoreType.DMA((14,)),
            pltpu.SemaphoreType.DMA((10, 2)),
            pltpu.SemaphoreType.DMA((10, 2)),
        ],
        compiler_params=pltpu.CompilerParams(
            collective_id=0, has_side_effects=True, vmem_limit_bytes=56 * 1024 * 1024
        ),
    )(
        load.reshape(SLOTS, E, NR),
        schur.reshape(SUBS * NI, NI),
        schur_inverse.reshape(SUBS * NI, NI),
        jnp.swapaxes(basis, 1, 2),
        coarse_inverse,
        partner_slot,
        jnp.swapaxes(edge_map, 0, 1),
        coarse_number,
        *one_hot_tables(),
    )
    return tuple(
        o.reshape(load.shape)
        for o in (alpha * direction, residual - alpha * image, preconditioned + beta * direction)
    )


def solution(mesh):
    both = ("sub", "coarse")
    placed = (
        P(both, None, None, None),
        P(both, None, None),
        P(both, None, None),
        P(both, None, None),
        P("coarse", None),
        P(both, None),
        P(both, None, None),
        P(both, None),
    )
    return jax.shard_map(
        functools.partial(shards, mesh.shape["sub"], mesh.shape["coarse"]),
        mesh=mesh,
        in_specs=placed,
        out_specs=(P(both, None, None, None),) * 3,
        check_vma=False,
    )
```

```python
import functools

import jax
import jax.numpy as jnp
import numpy as np
from jax import lax
from jax.experimental import pallas as pl
from jax.experimental.pallas import tpu as pltpu
from jax.sharding import PartitionSpec as P

MESH = pl.DeviceIdType.MESH
F32 = jnp.float32
BF16 = jnp.bfloat16
FACES = 6
SUBS = 2
SLOTS = FACES * SUBS
NCF = 4
LANES = 128
STEP = 4
USED = 4
CG = 8


def split(x):
    hi = x.astype(BF16)
    return hi, (x - hi.astype(F32)).astype(BF16)


def dot(a, b):
    return jnp.dot(a, b, preferred_element_type=F32)


def kernel(
    Q, Z, load, schur, sinv, basis_t, coarse, ps, em, cn, sp_in, spt_in, fold4_in,
    dirn, res, img, pre, out_alpha, out_beta,
    vld, loc, prod,
    hs0, hs1, hs2, hs3, hr0, hr1, hr2, hr3,
    sinv_hi, sinv_lo, schur_hi, schur_lo, c_hi, c_lo, s_stage, c_stage,
    hh, hl, perm, bt_hi, bt_lo, bcol, bface, bpart, bs, br, gs, gr, ys, yr, sp, spt,
    fold4, scat, gath, xbuf, xt, yt, xm, xb, xf0, y2,
    qb, qr, zb, zr, ob, zs0, zs1, arb, arr, arz0, arz1, cnz,
    in_sem, tab_sem, st_sem, ct_sem, q_send, q_recv, h_send, h_recv,
):
    q = lax.axis_index("sub")
    z = lax.axis_index("coarse")
    E = vld.shape[1]
    NR = vld.shape[2]
    ZQ = Z * Q
    NCZ = c_hi.shape[0]
    NC0 = c_hi.shape[1]
    NF = NC0 // NCF
    NFZ = NF // Z
    RR = SLOTS * NCF * CG // LANES
    ndev = Q * Z
    me = q * Z + z
    nxt = lax.rem(me + 1, ndev)
    prv = lax.rem(me + ndev - 1, ndev)
    nxt_id = (nxt // Z, lax.rem(nxt, Z))
    prv_id = (prv // Z, lax.rem(prv, Z))

    def q_peer(k):
        return lax.rem(q + k, Q)

    def z_peer(k):
        return lax.rem(z + k, Z)

    owed = {}

    def owe(key, ref, sem):
        owed[key] = lambda: pltpu.make_async_copy(ref, ref, sem).wait()

    def settle(*key):
        owed.pop(key)()

    load_copy = pltpu.make_async_copy(load, vld, in_sem)
    load_copy.start()

    def stager(src, rows, stage, sem):
        def copy(i, slot):
            return pltpu.make_async_copy(
                src.at[pl.ds(pl.multiple_of(i * rows, rows), rows), :], stage.at[slot], sem.at[slot]
            )
        return copy

    s_rows = s_stage.shape[1]
    c_rows = c_stage.shape[1]
    sinv_copy = stager(sinv, s_rows, s_stage, st_sem)
    schur_copy = stager(schur, s_rows, s_stage, st_sem)
    c_copy = stager(coarse, c_rows, c_stage, ct_sem)

    def first(copy):
        copy(0, 0).start()
        copy(1, 1).start()
        owed[copy] = lambda: (copy(0, 0).wait(), copy(1, 1).wait())

    def convert(copy, stage, n, rows, hi_ref, lo_ref):
        def body(i, carry):
            slot = lax.rem(i, 2)
            copy(i, slot).wait()
            hi, lo = split(stage[slot])
            at = pl.ds(pl.multiple_of(i * rows, rows), rows)
            hi_ref[at, :] = hi
            lo_ref[at, :] = lo

            @pl.when(i + 2 < n)
            def _():
                copy(i + 2, slot).start()
            return carry
        lax.fori_loop(0, n, body, 0)
        owed.pop(copy)

    first(sinv_copy)
    first(c_copy)
    tables = [
        pltpu.make_async_copy(src, dst, tab_sem.at[i])
        for i, (src, dst) in enumerate(((sp_in, sp), (spt_in, spt), (fold4_in, fold4)))
    ]
    for copy in tables:
        copy.start()

    barrier = pltpu.get_barrier_semaphore()

    def greet(device):
        pl.semaphore_signal(barrier, inc=1, device_id=device, device_id_type=MESH)

    lax.fori_loop(1, Q, lambda k, c: (greet((q_peer(k), z)), c)[1], 0)
    for k in range(1, Z):
        greet((q, z_peer(k)))
    greet(nxt_id)
    greet(prv_id)

    lane8 = lax.broadcasted_iota(jnp.int32, (8, LANES), 1)

    def q_start(ph, src, dst, shared=False):
        def body(i, carry):
            p = q_peer(1 + lax.rem(i + Q // 2 - 1, Q - 1))
            block = src.at[pl.ds(0 if shared else pl.multiple_of(p * 8, 8), USED), :]
            pltpu.make_async_remote_copy(
                src_ref=block,
                dst_ref=dst.at[pl.ds(pl.multiple_of(q * 8, 8), USED), :],
                send_sem=q_send.at[ph], recv_sem=q_recv.at[ph],
                device_id=(p, z), device_id_type=MESH,
            ).start()
            return carry
        lax.fori_loop(0, Q - 1, body, 0)
        mine = pl.ds(pl.multiple_of(q * 8, 8), USED)
        dst[mine, :] = src[0:USED, :] if shared else src[mine, :]
        every = dst.at[pl.ds(0, (Q - 1) * USED), :]
        owe((ph, "in"), every, q_recv.at[ph])
        owe((ph, "out"), every, q_send.at[ph])

    def z_start(ph, src_of, dst, three):
        for k in sorted(range(1, Z), key=lambda k: -min(k, Z - k)):
            t = z_peer(k)
            pltpu.make_async_remote_copy(
                src_ref=src_of(t), dst_ref=dst,
                send_sem=q_send.at[ph], recv_sem=q_recv.at[ph],
                device_id=(q, t), device_id_type=MESH,
            ).start()
        owe((ph, "in"), three, q_recv.at[ph])
        owe((ph, "out"), three, q_send.at[ph])

    def rel_of(k):
        p = ps[k // FACES, lax.rem(k, FACES)]
        rel = p - me * SLOTS
        rel = jnp.where(rel < -SLOTS, rel + ndev * SLOTS, rel)
        rel = jnp.where(rel >= 2 * SLOTS, rel - ndev * SLOTS, rel)
        return p, rel

    def weight_of(k):
        return jnp.where(ps[k // FACES, lax.rem(k, FACES)] >= 0, jnp.float32(0.5), jnp.float32(1.0))

    ups, downs = [], []
    for s in range(SUBS):
        up = jnp.int32(0)
        down = jnp.int32(0)
        for f in range(FACES):
            p, rel = rel_of(s * FACES + f)
            here = p >= 0
            up = jnp.where(here & (rel >= SLOTS), s * FACES + f, up)
            down = jnp.where(here & (rel < 0), s * FACES + f, down)
        ups.append(up)
        downs.append(down)

    def pair_start(h, send, recv, count):
        for way, device in ((0, nxt_id), (1, prv_id)):
            part = pl.ds(way * count, count)
            pltpu.make_async_remote_copy(
                src_ref=send.at[part], dst_ref=recv.at[part],
                send_sem=h_send.at[h, way], recv_sem=h_recv.at[h, way],
                device_id=device, device_id_type=MESH,
            ).start()
            owe((h, way, "halo in"), recv.at[part], h_recv.at[h, way])
            owe((h, way, "halo out"), recv.at[part], h_send.at[h, way])

    def halo_start(h, v, send, recv):
        for s in range(SUBS):
            send[s] = v[ups[s]]
            send[SUBS + s] = v[downs[s]]
        pair_start(h, send, recv, SUBS)

    def half_start(h, s, v, send, recv):
        for way, slot, device in ((0, ups[s], nxt_id), (1, downs[s], prv_id)):
            place = way * SUBS + s
            send[place] = v[slot]
            part = pl.ds(place, 1)
            pltpu.make_async_remote_copy(
                src_ref=send.at[part], dst_ref=recv.at[part],
                send_sem=h_send.at[h, way], recv_sem=h_recv.at[h, way],
                device_id=device, device_id_type=MESH,
            ).start()
            owe((h, way, "halo in"), recv.at[part], h_recv.at[h, way])
            owe((h, way, "halo out"), recv.at[part], h_send.at[h, way])

    def halo_wait(h):
        settle(h, 0, "halo in")
        settle(h, 1, "halo in")

    def place_of(k):
        p, rel = rel_of(k)
        local = (rel >= 0) & (rel < SLOTS)
        inside = jnp.clip(rel, 0, SLOTS - 1)
        below = (rel + SLOTS >= FACES).astype(jnp.int32)
        above = SUBS + (rel - SLOTS >= FACES).astype(jnp.int32)
        return local, inside, jnp.clip(jnp.where(rel < 0, below, above), 0, 2 * SUBS - 1)

    def permute(k, val):
        hi, lo = split(val)
        return dot(perm[k], jnp.concatenate([hi, lo], axis=0))

    def partner(k, v, recv):
        local, inside, outside = place_of(k)
        return permute(k, jnp.where(local, v[inside], recv[outside]))

    def partner_here(k, v):
        local, inside, outside = place_of(k)
        return permute(k, jnp.where(local, v[inside], jnp.float32(0.0)))

    rows_e = lax.broadcasted_iota(jnp.int32, (E, E), 0)
    for k in range(SLOTS):
        line = em[k % FACES, pl.ds(k // FACES, 1), :]
        one = jnp.where(rows_e == line, jnp.float32(1.0), jnp.float32(0.0)).T
        one = jnp.where(ps[k // FACES, k % FACES] >= 0, one, jnp.zeros_like(one)).astype(BF16)
        perm[k] = jnp.concatenate([one, one], axis=1)

    NI = FACES * E
    NCL = FACES * NCF
    convert(sinv_copy, s_stage, SUBS * NI // s_rows, s_rows, sinv_hi, sinv_lo)
    first(schur_copy)
    load_copy.wait()
    pl.semaphore_wait(barrier, Q + Z)
    halo_start(0, vld, hs0, hr0)

    row = jnp.zeros((8, LANES), F32)
    for k in range(SLOTS):
        row = jnp.where(lane8 == k, cn[k // FACES, k % FACES].astype(F32), row)
    arb[0] = row
    q_start(0, arb.at[0], arr.at[0], shared=True)

    for s in range(SUBS):
        for place, slot in ((s, ups[s]), (SUBS + s, downs[s])):
            face = jnp.zeros((NCL, E), F32)
            for f in range(FACES):
                face = jnp.where(slot == s * FACES + f, basis_t[s, :, f * E:(f + 1) * E], face)
            bs[place] = face
    pair_start(4, bs, br, SUBS)

    zrow = jnp.zeros((32 - NCL, NI), F32)
    for s in range(SUBS):
        b = basis_t[s]
        bh = b.astype(BF16).astype(F32)
        bl = b - bh
        bh = jnp.concatenate([bh, zrow], axis=0)
        bl = jnp.concatenate([bl, zrow], axis=0)
        bt_hi[s] = bh.astype(BF16)
        bt_lo[s] = bl.astype(BF16)
        bcol[s] = jnp.concatenate([bh, bh, bl, jnp.zeros_like(bl)], axis=0).T.astype(BF16)

    xbuf[...] = jnp.zeros_like(xbuf)

    convert(c_copy, c_stage, NCZ // c_rows, c_rows, c_hi, c_lo)
    for copy in tables:
        copy.wait()

    settle(0, "in")
    zmine = pl.ds(pl.multiple_of(z * Q, Q), Q)
    arz0[...] = arr[0, pl.ds(0, Q, stride=8), :]
    cnz[zmine, :] = arz0[...]
    z_start(1, lambda t: arz0, cnz.at[zmine, :], cnz.at[pl.ds(0, (Z - 1) * Q), :])

    def number_tables():
        settle(1, "in")
        cns = cnz[...]
        cnt = cns.T if ZQ == LANES else jnp.concatenate([cns, jnp.zeros((LANES - ZQ, LANES), F32)], axis=0).T
        face0 = lax.broadcasted_iota(jnp.int32, (NF, ZQ), 0).astype(F32)
        face1 = lax.broadcasted_iota(jnp.int32, (ZQ, NFZ), 1).astype(F32) + (z * NFZ).astype(F32)
        for k in range(SLOTS):
            scat[:, k * ZQ:(k + 1) * ZQ] = jnp.where(
                face0 == cnt[k:k + 1, :ZQ], jnp.float32(1.0), jnp.float32(0.0)
            ).astype(BF16)
            gath[k] = jnp.where(
                cns[:, k:k + 1] == face1, jnp.float32(1.0), jnp.float32(0.0)
            ).astype(BF16)

    def face_tables():
        settle(4, 0, "halo in")
        settle(4, 1, "halo in")
        pad = jnp.zeros((32 - NCL, E), F32)
        for c in range(2 * SUBS):
            b = jnp.concatenate([br[c], pad], axis=0)
            bh = b.astype(BF16).astype(F32)
            bface[c] = jnp.concatenate([bh, bh, b - bh, jnp.zeros_like(bh)], axis=0).T.astype(BF16)
        for s in range(SUBS):
            for place, slot in ((s, ups[s]), (SUBS + s, downs[s])):
                local, inside, outside = place_of(slot)
                b = jnp.concatenate([br[outside], pad], axis=0)
                bh = b.astype(BF16).astype(F32)
                both = jnp.concatenate([bh, b - bh], axis=0).astype(BF16)
                bpart[place] = lax.dot_general(
                    both, perm[slot][:, :E], (((1,), (1,)), ((), ())), preferred_element_type=F32
                ).astype(BF16)

    def put(k, x):
        hi, lo = split(x)
        at = pl.ds(pl.multiple_of(k * E, E), E)
        hh[at, :] = hi
        hl[at, :] = lo

    def local_mul(a_hi, a_lo, out, scale, subs=range(SUBS)):
        def body(s, carry):
            at = pl.ds(pl.multiple_of(s * NI, NI), NI)
            top = hh[at, :]
            acc = dot(a_hi[at, :], top) + dot(a_hi[at, :], hl[at, :]) + dot(a_lo[at, :], top)
            for f in range(FACES):
                k = s * FACES + f
                out[k] = scale(k) * acc[f * E:(f + 1) * E]
            return carry
        lax.fori_loop(subs[0], subs[-1] + 1, body, 0)

    def coarse_load(s):
        sub = pl.ds(s * NI, NI)
        top = hh[sub, :]
        x = dot(bt_hi[s], top) + dot(bt_hi[s], hl[sub, :]) + dot(bt_lo[s], top)
        return x[:NCL]

    def forward_start(n, loads, sums=()):
        for s in range(SUBS):
            xbuf[s * NCL:(s + 1) * NCL, :] = loads[s]
        for i, part in enumerate(sums):
            xbuf[pl.ds(SUBS * NCL + i, 1), :] = part.sum(axis=0, keepdims=True)
        xt[...] = xbuf[...].T
        acc = jnp.zeros((2 * Q, (RR + 1) * LANES), F32)
        for c in range(CG):
            part = xt[pl.ds(c, Q, stride=CG), :]
            hi = part.astype(BF16).astype(F32)
            both = jnp.concatenate([hi, part - hi], axis=0).astype(BF16)
            acc += dot(both, spt[c * LANES:(c + 1) * LANES, :])
        acc = acc[:Q] + acc[Q:]
        b = qb.at[n]
        for r in range(RR + 1):
            b[pl.ds(r, Q, stride=8), :] = acc[:, r * LANES:(r + 1) * LANES]
        q_start(2 + 4 * n, b, qr.at[n])

    def gather_start(n):
        settle(2 + 4 * n, "in")
        for r in range(RR + n):
            part = qr[n, pl.ds(r, Q, stride=8), :]
            zb[n, r] = part
            zr[n, r, zmine, :] = part
        used = pl.ds(0, RR + n)
        z_start(
            3 + 4 * n, lambda t: zb.at[n, used], zr.at[n, used, zmine, :],
            zr.at[n, used, pl.ds(0, (Z - 1) * Q), :],
        )

    def gather_wait(n):
        settle(3 + 4 * n, "in")

    def own_step(n):
        tot = jnp.broadcast_to(zr[n, RR].sum(axis=0, keepdims=True), (8, LANES))
        below = pltpu.roll(tot, LANES - CG, 1)
        row = jnp.where(lane8 < CG, tot / below, jnp.float32(0.0))
        for shift in (8, 16, 32, 64):
            row = row + pltpu.roll(row, shift, 1)
        return row[0:1]

    def coarse_product(n, step=None):
        la = lax.broadcasted_iota(jnp.int32, (ZQ, LANES), 1) >> 5
        pieces = []
        for r in range(RR):
            part = zr[n, r]
            for a in range(NCF):
                hi, lo = split(jnp.where(la == a, part, jnp.float32(0.0)))
                pieces.append(jnp.concatenate([hi, lo], axis=1))
        slots = jnp.concatenate(pieces, axis=0)
        fa = lax.broadcasted_iota(jnp.int32, (NF, LANES), 1)
        acc = dot(scat[...], slots)
        x = acc[:, :LANES] + acc[:, LANES:]
        x = x + pltpu.roll(x, 64, 1)
        x = x + pltpu.roll(x, 32, 1)
        if step is not None:
            x = xf0[...] - step() * x
        xf0[...] = x
        hi = x.astype(BF16).astype(F32)
        v = jnp.where((fa >> 5) == 0, hi, jnp.where((fa >> 5) == 1, x - hi, jnp.float32(0.0)))
        for j in range(NCF):
            xm[pl.ds(j, NF, stride=NCF), :] = jnp.where(((fa >> 3) & 3) == j, v, jnp.float32(0.0))
        xb[...] = xm[...].astype(BF16)
        kc = NC0 // 7
        acc = jnp.zeros((NCZ, LANES), F32)
        for k in range(7):
            cols = slice(k * kc, (k + 1) * kc)
            acc += dot(c_hi[:, cols], xb[cols, :]) + dot(c_lo[:, cols], xb[cols, :])
        y2[...] = acc
        pieces = []
        for j in range(NCF):
            pieces.extend(split(y2[pl.ds(j, NFZ, stride=NCF), :]))
        y = dot(jnp.concatenate(pieces, axis=1), fold4[...])
        hi, lo = split(y)
        both = jnp.concatenate([hi, lo], axis=1)
        for r in range(RR):
            o = jnp.zeros((ZQ, LANES), F32)
            for a in range(NCF):
                g = dot(gath[NCF * r + a], both)
                o = jnp.where(la == a, g[:, :LANES] + g[:, LANES:], o)
            ob[n, r] = o
        if n == 1:
            mine = xf0[pl.ds(pl.multiple_of(z * NFZ, 8) if NFZ % 8 == 0 else z * NFZ, NFZ), :]
            energy = (mine * y).sum(axis=0, keepdims=True)
            ob[n, RR] = jnp.where(la == 0, energy, jnp.float32(0.0))
        used = pl.ds(0, RR + n)
        zs = (zs0, zs1)[n]
        zs[z, used] = ob[n, used, zmine, :]
        z_start(
            4 + 4 * n,
            lambda t: ob.at[n, used, pl.ds(pl.multiple_of(t * Q, Q), Q), :],
            zs.at[z, used],
            zs.at[pl.ds(0, Z - 1), used],
        )

    def backward_start(n):
        zs = (zs0, zs1)[n]
        settle(4 + 4 * n, "in")
        b = qb.at[2 + n]
        for r in range(RR + n):
            tot = zs[0, r]
            for t in range(1, Z):
                tot = tot + zs[t, r]
            b[pl.ds(r, Q, stride=8), :] = tot
        for r in range(RR + n, RR + 1):
            b[pl.ds(r, Q, stride=8), :] = jnp.zeros((Q, LANES), F32)
        q_start(5 + 4 * n, b, qr.at[2 + n])

    def backward_finish(n):
        settle(5 + 4 * n, "in")
        acc = jnp.zeros((2 * Q, CG * LANES), F32)
        for r in range(RR + n):
            part = qr[2 + n, pl.ds(r, Q, stride=8), :]
            hi = part.astype(BF16).astype(F32)
            both = jnp.concatenate([hi, part - hi], axis=0).astype(BF16)
            acc += dot(both, sp[r * LANES:(r + 1) * LANES, :])
        for c in range(CG):
            cols = slice(c * LANES, (c + 1) * LANES)
            yt[pl.ds(c, Q, stride=CG), :] = acc[:Q, cols] + acc[Q:, cols]
        return yt[...].T

    def columns(ys):
        ys = jnp.concatenate([ys, jnp.zeros((32 - NCL, NR), F32)], axis=0)
        hi = ys.astype(BF16).astype(F32)
        return jnp.concatenate([hi, ys - hi, hi, jnp.zeros_like(hi)], axis=0).astype(BF16)

    def share_coarse(n, y):
        for way in range(2):
            ys[n, way] = y[:SUBS * NCL]
        pair_start(6 + n, ys.at[n], yr.at[n], 1)

    def add_coarse(n, y, recv):
        for s in range(SUBS):
            cols = columns(y[s * NCL:(s + 1) * NCL])

            def body(i, carry):
                for j in range(3):
                    f = 3 * i + j
                    k = s * FACES + f
                    at = pl.ds(pl.multiple_of(f * E, E), E)
                    loc[k] = loc[k] + weight_of(k) * dot(bcol[s, at, :], cols)
                return carry
            lax.fori_loop(0, FACES // 3, body, 0)
        halo_wait(6 + n)
        halo_wait(1 + 2 * n)
        halo_wait(8 + n)
        for c in range(2 * SUBS):
            first_row = (c % SUBS) * NCL
            cols = columns(yr[n, c // SUBS, first_row:first_row + NCL, :])
            recv[c] = recv[c] + 0.5 * dot(bface[c], cols)

    def fold(x):
        return x.reshape(E // 8, 8, NR).sum(axis=0)

    nh = max(1, NR // LANES)
    lw = min(NR, LANES)

    def sums_start(n, parts):
        b = arb.at[1 + n]
        b[...] = jnp.zeros((8, LANES), F32)
        for i, part in enumerate(parts):
            line = part.sum(axis=0, keepdims=True)
            for h in range(nh):
                b[pl.ds(i * nh + h, 1), 0:lw] = line[:, h * lw:(h + 1) * lw]
        q_start(10 + 2 * n, b, arr.at[1 + n], shared=True)

    def sums_pass(n):
        settle(10 + 2 * n, "in")
        tot = arr[1 + n].reshape(Q, 8, LANES).sum(axis=0)
        tot = jnp.where(lax.broadcasted_iota(jnp.int32, (8, LANES), 0) < USED, tot, jnp.float32(0.0))
        arb[3 + n] = tot
        arz1[n, z] = tot
        z_start(11 + 2 * n, lambda t: arb.at[3 + n], arz1.at[n, z], arz1.at[n, pl.ds(0, Z - 1)])

    def sums_finish(n):
        settle(11 + 2 * n, "in")
        tot = arz1[n, 0]
        for t in range(1, Z):
            tot = tot + arz1[n, t]
        return tot

    def cases(tile, i):
        return jnp.concatenate([tile[i * nh + h:i * nh + h + 1, :lw] for h in range(nh)], axis=1)

    def over_slots(body, carry):
        def some(i, carry):
            for k in range(STEP):
                carry = body(STEP * i + k, carry)
            return carry
        return lax.fori_loop(0, SLOTS // STEP, some, carry)

    zero8 = jnp.zeros((8, NR), F32)

    halo_wait(0)

    def residual(k, carry):
        r = vld[k] + partner(k, vld, hr0)
        res[k] = r
        put(k, weight_of(k) * r)
        return carry
    over_slots(residual, 0)

    def unscaled(k):
        return jnp.float32(1.0)

    forward_start(0, [coarse_load(s) for s in range(SUBS)])
    local_mul(sinv_hi, sinv_lo, loc, weight_of, (0,))
    half_start(1, 0, loc, hs1, hr1)
    local_mul(sinv_hi, sinv_lo, loc, weight_of, (1,))
    gather_start(0)
    number_tables()
    gather_wait(0)
    half_start(8, 1, loc, hs1, hr1)
    coarse_product(0)
    face_tables()
    convert(schur_copy, s_stage, SUBS * NI // s_rows, s_rows, schur_hi, schur_lo)
    backward_start(0)
    y = backward_finish(0)
    share_coarse(0, y)
    add_coarse(0, y, hr1)

    def direction(k, acc):
        d = loc[k] + partner(k, loc, hr1)
        dirn[k] = d
        put(k, d)
        return acc + fold(weight_of(k) * res[k] * d)
    rz_part = over_slots(direction, zero8)

    local_mul(schur_hi, schur_lo, prod, unscaled)
    for s in range(SUBS):
        for place, slot in ((s, ups[s]), (SUBS + s, downs[s])):
            hi, lo = split(prod[slot])
            b = bpart[place]
            x = dot(b, hi)
            gs[place] = 0.5 * (x[:NCL] + x[32:32 + NCL] + dot(b[:32], lo)[:NCL])
    pair_start(5, gs, gr, SUBS)
    halo_start(2, prod, hs2, hr2)

    def image_here(k, acc):
        m = prod[k]
        put(k, weight_of(k) * (m + partner_here(k, prod)))
        return acc + fold(dirn[k] * m)
    da_part = over_slots(image_here, zero8)

    loads = [coarse_load(s) for s in range(SUBS)]
    halo_wait(5)
    for s in range(SUBS):
        loads[s] = loads[s] + gr[place_of(downs[s])[2]] + gr[place_of(ups[s])[2]]
    forward_start(1, loads, [rz_part, da_part])
    sums_start(0, [rz_part, da_part])
    gather_start(1)
    sums_pass(0)
    gather_wait(1)
    coarse_product(1, lambda: own_step(1))
    tot = sums_finish(0)
    rz = cases(tot, 0)
    alpha = rz / cases(tot, 1)
    halo_wait(2)

    def advance(k, carry):
        m = prod[k] + partner(k, prod, hr2)
        img[k] = m
        r = res[k] - alpha * m
        vld[k] = r
        put(k, weight_of(k) * r)
        return carry
    over_slots(advance, 0)

    local_mul(sinv_hi, sinv_lo, loc, weight_of, (0,))
    half_start(3, 0, loc, hs3, hr3)
    local_mul(sinv_hi, sinv_lo, loc, weight_of, (1,))
    backward_start(1)
    half_start(9, 1, loc, hs3, hr3)

    def energies(k, acc):
        return acc + fold(vld[k] * loc[k])
    sums_start(1, [over_slots(energies, zero8)])
    y = backward_finish(1)
    share_coarse(1, y)
    coarse_energy = y[SUBS * NCL:SUBS * NCL + NCF].sum(axis=0, keepdims=True)
    sums_pass(1)
    add_coarse(1, y, hr3)

    def second(k, carry):
        pre[k] = loc[k] + partner(k, loc, hr3)
        return carry
    over_slots(second, 0)
    out_alpha[...] = alpha
    out_beta[...] = (cases(sums_finish(1), 0) + coarse_energy) / rz

    for wait in list(owed.values()):
        wait()


def one_hot_tables():
    rows = (SLOTS * NCF * CG // LANES + 1) * LANES
    i0 = np.arange(rows)[:, None]
    i1 = np.arange(CG * LANES)[None, :]
    table = i1 == (i0 % CG) * LANES + (i0 // LANES) * (LANES // CG) + i0 % LANES // CG
    m0 = np.arange(2 * NCF * LANES)[:, None]
    m1 = np.arange(LANES)[None, :]
    fold = (m0 % CG == m1 % CG) & (m0 // (2 * LANES) == m1 // CG % NCF)
    return [jnp.asarray(t.astype(np.float32), BF16) for t in (table, table.T, fold)]


def shards(Q, Z, load, schur, schur_inverse, basis, coarse_inverse, partner_slot, edge_map, coarse_number):
    E, NR = load.shape[2], load.shape[3]
    NI = FACES * E
    NCZ, NC0 = coarse_inverse.shape
    NF = NC0 // NCF
    ZQ = Z * Q
    RR = SLOTS * NCF * CG // LANES
    vec = pltpu.VMEM((SLOTS, E, NR), F32)
    halo = pltpu.VMEM((2 * SUBS, E, NR), F32)
    mat = pltpu.VMEM((SUBS * NI, NI), BF16)
    out = pltpu.VMEM((SLOTS, E, NR), F32)
    ratio = pltpu.VMEM((1, NR), F32)
    NCL = FACES * NCF
    anywhere = pl.BlockSpec(memory_space=pl.ANY)
    vmem = pl.BlockSpec(memory_space=pltpu.VMEM)
    smem = pl.BlockSpec(memory_space=pltpu.SMEM)
    direction, residual, image, preconditioned, alpha, beta = pl.pallas_call(
        functools.partial(kernel, Q, Z),
        out_shape=(out, out, out, out, ratio, ratio),
        in_specs=[anywhere, anywhere, anywhere, vmem, anywhere, smem, vmem, smem] + [anywhere] * 3,
        out_specs=(vmem,) * 6,
        scratch_shapes=[vec] * 3 + [halo] * 8 + [mat] * 4 + [
            pltpu.VMEM((NCZ, NC0), BF16),
            pltpu.VMEM((NCZ, NC0), BF16),
            pltpu.VMEM((2, 2 * E, NI), F32),
            pltpu.VMEM((2, NCZ // 7, NC0), F32),
            pltpu.VMEM((SUBS * NI, NR), BF16),
            pltpu.VMEM((SUBS * NI, NR), BF16),
            pltpu.VMEM((SLOTS, E, 2 * E), BF16),
            pltpu.VMEM((SUBS, 32, NI), BF16),
            pltpu.VMEM((SUBS, 32, NI), BF16),
            pltpu.VMEM((SUBS, NI, LANES), BF16),
            pltpu.VMEM((2 * SUBS, E, LANES), BF16),
            pltpu.VMEM((2 * SUBS, 64, E), BF16),
            pltpu.VMEM((2 * SUBS, NCL, E), F32),
            pltpu.VMEM((2 * SUBS, NCL, E), F32),
            pltpu.VMEM((2 * SUBS, NCL, NR), F32),
            pltpu.VMEM((2 * SUBS, NCL, NR), F32),
            pltpu.VMEM((2, 2, SUBS * NCL, NR), F32),
            pltpu.VMEM((2, 2, SUBS * NCL, NR), F32),
            pltpu.VMEM(((RR + 1) * LANES, CG * LANES), BF16),
            pltpu.VMEM((CG * LANES, (RR + 1) * LANES), BF16),
            pltpu.VMEM((2 * NCF * LANES, LANES), BF16),
            pltpu.VMEM((NF, SLOTS * ZQ), BF16),
            pltpu.VMEM((SLOTS, ZQ, NF // Z), BF16),
            pltpu.VMEM((LANES, NR), F32),
            pltpu.VMEM((NR, LANES), F32),
            pltpu.VMEM((NR, LANES), F32),
            pltpu.VMEM((NC0, LANES), F32),
            pltpu.VMEM((NC0, LANES), BF16),
            pltpu.VMEM((NF, LANES), F32),
            pltpu.VMEM((NCZ, LANES), F32),
            pltpu.VMEM((4, Q * 8, LANES), F32),
            pltpu.VMEM((4, Q * 8, LANES), F32),
            pltpu.VMEM((2, RR + 1, Q, LANES), F32),
            pltpu.VMEM((2, RR + 1, ZQ, LANES), F32),
            pltpu.VMEM((2, RR + 1, ZQ, LANES), F32),
            pltpu.VMEM((Z, RR + 1, Q, LANES), F32),
            pltpu.VMEM((Z, RR + 1, Q, LANES), F32),
            pltpu.VMEM((5, 8, LANES), F32),
            pltpu.VMEM((3, Q * 8, LANES), F32),
            pltpu.VMEM((Q, LANES), F32),
            pltpu.VMEM((2, Z, 8, LANES), F32),
            pltpu.VMEM((ZQ, LANES), F32),
            pltpu.SemaphoreType.DMA,
            pltpu.SemaphoreType.DMA((3,)),
            pltpu.SemaphoreType.DMA((2,)),
            pltpu.SemaphoreType.DMA((2,)),
            pltpu.SemaphoreType.DMA((14,)),
            pltpu.SemaphoreType.DMA((14,)),
            pltpu.SemaphoreType.DMA((10, 2)),
            pltpu.SemaphoreType.DMA((10, 2)),
        ],
        compiler_params=pltpu.CompilerParams(
            collective_id=0, has_side_effects=True, vmem_limit_bytes=56 * 1024 * 1024
        ),
    )(
        load.reshape(SLOTS, E, NR),
        schur.reshape(SUBS * NI, NI),
        schur_inverse.reshape(SUBS * NI, NI),
        jnp.swapaxes(basis, 1, 2),
        coarse_inverse,
        partner_slot,
        jnp.swapaxes(edge_map, 0, 1),
        coarse_number,
        *one_hot_tables(),
    )
    return tuple(
        o.reshape(load.shape)
        for o in (alpha * direction, residual - alpha * image, preconditioned + beta * direction)
    )


def solution(mesh):
    both = ("sub", "coarse")
    placed = (
        P(both, None, None, None),
        P(both, None, None),
        P(both, None, None),
        P(both, None, None),
        P("coarse", None),
        P(both, None),
        P(both, None, None),
        P(both, None),
    )
    return jax.shard_map(
        functools.partial(shards, mesh.shape["sub"], mesh.shape["coarse"]),
        mesh=mesh,
        in_specs=placed,
        out_specs=(P(both, None, None, None),) * 3,
        check_vma=False,
    )
```

```python
import functools

import jax
import jax.numpy as jnp
import numpy as np
from jax import lax
from jax.experimental import pallas as pl
from jax.experimental.pallas import tpu as pltpu
from jax.sharding import PartitionSpec as P

MESH = pl.DeviceIdType.MESH
F32 = jnp.float32
BF16 = jnp.bfloat16
FACES = 6
SUBS = 2
SLOTS = FACES * SUBS
NCF = 4
LANES = 128
STEP = 6
USED = 4
CG = 8


def split(x):
    hi = x.astype(BF16)
    return hi, (x - hi.astype(F32)).astype(BF16)


def dot(a, b):
    return jnp.dot(a, b, preferred_element_type=F32)


def kernel(
    Q, Z, load, schur, sinv, basis_t, coarse, ps, em, cn, sp_in, spt_in, fold4_in,
    dirn, res, img, pre, out_alpha, out_beta,
    vld, loc, prod,
    hs0, hs1, hs2, hs3, hr0, hr1, hr2, hr3,
    sinv_hi, sinv_lo, schur_hi, schur_lo, c_hi, c_lo, s_stage, c_stage,
    hh, hl, perm, bt_hi, bt_lo, bcol, bface, bpart, bs, br, gs, gr, ys, yr, sp, spt,
    fold4, scat, gath, xbuf, xt, yt, xm, xb, xf0, y2,
    qb, qr, zb, zr, ob, zs0, zs1, arb, arr, arz0, arz1, cnz,
    in_sem, tab_sem, st_sem, ct_sem, q_send, q_recv, h_send, h_recv, eb, er,
):
    q = lax.axis_index("sub")
    z = lax.axis_index("coarse")
    E = vld.shape[1]
    NR = vld.shape[2]
    ZQ = Z * Q
    NCZ = c_hi.shape[0]
    NC0 = c_hi.shape[1]
    NF = NC0 // NCF
    NFZ = NF // Z
    RR = SLOTS * NCF * CG // LANES
    ndev = Q * Z
    me = q * Z + z
    nxt = lax.rem(me + 1, ndev)
    prv = lax.rem(me + ndev - 1, ndev)
    nxt_id = (nxt // Z, lax.rem(nxt, Z))
    prv_id = (prv // Z, lax.rem(prv, Z))

    def q_peer(k):
        return lax.rem(q + k, Q)

    def z_peer(k):
        return lax.rem(z + k, Z)

    owed = {}

    def owe(key, ref, sem):
        owed[key] = lambda: pltpu.make_async_copy(ref, ref, sem).wait()

    def settle(*key):
        owed.pop(key)()

    load_copy = pltpu.make_async_copy(load, vld, in_sem)
    load_copy.start()

    def stager(src, rows, stage, sem):
        def copy(i, slot):
            return pltpu.make_async_copy(
                src.at[pl.ds(pl.multiple_of(i * rows, rows), rows), :], stage.at[slot], sem.at[slot]
            )
        return copy

    s_rows = s_stage.shape[1]
    c_rows = c_stage.shape[1]
    sinv_copy = stager(sinv, s_rows, s_stage, st_sem)
    schur_copy = stager(schur, s_rows, s_stage, st_sem)
    c_copy = stager(coarse, c_rows, c_stage, ct_sem)

    def first(copy):
        copy(0, 0).start()
        copy(1, 1).start()
        owed[copy] = lambda: (copy(0, 0).wait(), copy(1, 1).wait())

    def convert(copy, stage, n, rows, hi_ref, lo_ref):
        def body(i, carry):
            slot = lax.rem(i, 2)
            copy(i, slot).wait()
            hi, lo = split(stage[slot])
            at = pl.ds(pl.multiple_of(i * rows, rows), rows)
            hi_ref[at, :] = hi
            lo_ref[at, :] = lo

            @pl.when(i + 2 < n)
            def _():
                copy(i + 2, slot).start()
            return carry
        lax.fori_loop(0, n, body, 0)
        owed.pop(copy)

    first(sinv_copy)
    first(c_copy)
    tables = [
        pltpu.make_async_copy(src, dst, tab_sem.at[i])
        for i, (src, dst) in enumerate(((sp_in, sp), (spt_in, spt), (fold4_in, fold4)))
    ]
    for copy in tables:
        copy.start()

    barrier = pltpu.get_barrier_semaphore()

    def greet(device):
        pl.semaphore_signal(barrier, inc=1, device_id=device, device_id_type=MESH)

    lax.fori_loop(1, Q, lambda k, c: (greet((q_peer(k), z)), c)[1], 0)
    for k in range(1, Z):
        greet((q, z_peer(k)))
    greet(nxt_id)
    greet(prv_id)

    lane8 = lax.broadcasted_iota(jnp.int32, (8, LANES), 1)

    def far(k):
        x, y = k // 8, k // 2 % 4
        return min(x, 4 - x) + min(y, 4 - y)

    def q_start(ph, src, dst, shared=False):
        def body(k, carry):
            p = q_peer(k)
            block = src.at[pl.ds(0 if shared else pl.multiple_of(p * 8, 8), USED), :]
            pltpu.make_async_remote_copy(
                src_ref=block,
                dst_ref=dst.at[pl.ds(pl.multiple_of(q * 8, 8), USED), :],
                send_sem=q_send.at[ph], recv_sem=q_recv.at[ph],
                device_id=(p, z), device_id_type=MESH,
            ).start()
            return carry
        if shared:
            lax.fori_loop(1, Q, body, 0)
        else:
            for k in sorted(range(1, Q), key=lambda k: -far(k)):
                body(k, 0)
        mine = pl.ds(pl.multiple_of(q * 8, 8), USED)
        dst[mine, :] = src[0:USED, :] if shared else src[mine, :]
        every = dst.at[pl.ds(0, (Q - 1) * USED), :]
        owe((ph, "in"), every, q_recv.at[ph])
        owe((ph, "out"), every, q_send.at[ph])

    def z_start(ph, src_of, dst, three):
        for k in sorted(range(1, Z), key=lambda k: -min(k, Z - k)):
            t = z_peer(k)
            pltpu.make_async_remote_copy(
                src_ref=src_of(t), dst_ref=dst,
                send_sem=q_send.at[ph], recv_sem=q_recv.at[ph],
                device_id=(q, t), device_id_type=MESH,
            ).start()
        owe((ph, "in"), three, q_recv.at[ph])
        owe((ph, "out"), three, q_send.at[ph])

    def rel_of(k):
        p = ps[k // FACES, lax.rem(k, FACES)]
        rel = p - me * SLOTS
        rel = jnp.where(rel < -SLOTS, rel + ndev * SLOTS, rel)
        rel = jnp.where(rel >= 2 * SLOTS, rel - ndev * SLOTS, rel)
        return p, rel

    def weight_of(k):
        return jnp.where(ps[k // FACES, lax.rem(k, FACES)] >= 0, jnp.float32(0.5), jnp.float32(1.0))

    ups, downs = [], []
    for s in range(SUBS):
        up = jnp.int32(0)
        down = jnp.int32(0)
        for f in range(FACES):
            p, rel = rel_of(s * FACES + f)
            here = p >= 0
            up = jnp.where(here & (rel >= SLOTS), s * FACES + f, up)
            down = jnp.where(here & (rel < 0), s * FACES + f, down)
        ups.append(up)
        downs.append(down)

    def pair_start(h, send, recv, count):
        for way, device in ((0, nxt_id), (1, prv_id)):
            part = pl.ds(way * count, count)
            pltpu.make_async_remote_copy(
                src_ref=send.at[part], dst_ref=recv.at[part],
                send_sem=h_send.at[h, way], recv_sem=h_recv.at[h, way],
                device_id=device, device_id_type=MESH,
            ).start()
            owe((h, way, "halo in"), recv.at[part], h_recv.at[h, way])
            owe((h, way, "halo out"), recv.at[part], h_send.at[h, way])

    def halo_start(h, v, send, recv):
        for s in range(SUBS):
            send[s] = v[ups[s]]
            send[SUBS + s] = v[downs[s]]
        pair_start(h, send, recv, SUBS)

    def half_start(h, s, v, send, recv):
        for way, slot, device in ((0, ups[s], nxt_id), (1, downs[s], prv_id)):
            place = way * SUBS + s
            send[place] = v[slot]
            part = pl.ds(place, 1)
            pltpu.make_async_remote_copy(
                src_ref=send.at[part], dst_ref=recv.at[part],
                send_sem=h_send.at[h, way], recv_sem=h_recv.at[h, way],
                device_id=device, device_id_type=MESH,
            ).start()
            owe((h, way, "halo in"), recv.at[part], h_recv.at[h, way])
            owe((h, way, "halo out"), recv.at[part], h_send.at[h, way])

    def halo_wait(h):
        settle(h, 0, "halo in")
        settle(h, 1, "halo in")

    def place_of(k):
        p, rel = rel_of(k)
        local = (rel >= 0) & (rel < SLOTS)
        inside = jnp.clip(rel, 0, SLOTS - 1)
        below = (rel + SLOTS >= FACES).astype(jnp.int32)
        above = SUBS + (rel - SLOTS >= FACES).astype(jnp.int32)
        return local, inside, jnp.clip(jnp.where(rel < 0, below, above), 0, 2 * SUBS - 1)

    def permute(k, val):
        hi, lo = split(val)
        return dot(perm[k], jnp.concatenate([hi, lo], axis=0))

    def partner(k, v, recv):
        local, inside, outside = place_of(k)
        return permute(k, jnp.where(local, v[inside], recv[outside]))

    def partner_here(k, v):
        local, inside, outside = place_of(k)
        return permute(k, jnp.where(local, v[inside], jnp.float32(0.0)))

    rows_e = lax.broadcasted_iota(jnp.int32, (E, E), 0)
    for k in range(SLOTS):
        line = em[k % FACES, pl.ds(k // FACES, 1), :]
        one = jnp.where(rows_e == line, jnp.float32(1.0), jnp.float32(0.0)).T
        one = jnp.where(ps[k // FACES, k % FACES] >= 0, one, jnp.zeros_like(one)).astype(BF16)
        perm[k] = jnp.concatenate([one, one], axis=1)

    NI = FACES * E
    NCL = FACES * NCF
    convert(sinv_copy, s_stage, SUBS * NI // s_rows, s_rows, sinv_hi, sinv_lo)
    first(schur_copy)
    load_copy.wait()
    pl.semaphore_wait(barrier, Q + Z)
    halo_start(0, vld, hs0, hr0)

    row = jnp.zeros((8, LANES), F32)
    for k in range(SLOTS):
        row = jnp.where(lane8 == k, cn[k // FACES, k % FACES].astype(F32), row)
    arb[0] = row
    q_start(0, arb.at[0], arr.at[0], shared=True)

    for s in range(SUBS):
        for place, slot in ((s, ups[s]), (SUBS + s, downs[s])):
            face = jnp.zeros((NCL, E), F32)
            for f in range(FACES):
                face = jnp.where(slot == s * FACES + f, basis_t[s, :, f * E:(f + 1) * E], face)
            bs[place] = face
    pair_start(4, bs, br, SUBS)

    zrow = jnp.zeros((32 - NCL, NI), F32)
    for s in range(SUBS):
        b = basis_t[s]
        bh = b.astype(BF16).astype(F32)
        bl = b - bh
        bh = jnp.concatenate([bh, zrow], axis=0)
        bl = jnp.concatenate([bl, zrow], axis=0)
        bt_hi[s] = bh.astype(BF16)
        bt_lo[s] = bl.astype(BF16)
        bcol[s] = jnp.concatenate([bh, bh, bl, jnp.zeros_like(bl)], axis=0).T.astype(BF16)

    xbuf[...] = jnp.zeros_like(xbuf)

    convert(c_copy, c_stage, NCZ // c_rows, c_rows, c_hi, c_lo)
    for copy in tables:
        copy.wait()

    settle(0, "in")
    zmine = pl.ds(pl.multiple_of(z * Q, Q), Q)
    arz0[...] = arr[0, pl.ds(0, Q, stride=8), :]
    cnz[zmine, :] = arz0[...]
    z_start(1, lambda t: arz0, cnz.at[zmine, :], cnz.at[pl.ds(0, (Z - 1) * Q), :])

    def number_tables():
        settle(1, "in")
        cns = cnz[...]
        cnt = cns.T if ZQ == LANES else jnp.concatenate([cns, jnp.zeros((LANES - ZQ, LANES), F32)], axis=0).T
        face0 = lax.broadcasted_iota(jnp.int32, (NF, ZQ), 0).astype(F32)
        face1 = lax.broadcasted_iota(jnp.int32, (ZQ, NFZ), 1).astype(F32) + (z * NFZ).astype(F32)
        for k in range(SLOTS):
            scat[:, k * ZQ:(k + 1) * ZQ] = jnp.where(
                face0 == cnt[k:k + 1, :ZQ], jnp.float32(1.0), jnp.float32(0.0)
            ).astype(BF16)
            gath[k] = jnp.where(
                cns[:, k:k + 1] == face1, jnp.float32(1.0), jnp.float32(0.0)
            ).astype(BF16)

    def face_tables():
        settle(4, 0, "halo in")
        settle(4, 1, "halo in")
        pad = jnp.zeros((32 - NCL, E), F32)
        for c in range(2 * SUBS):
            b = jnp.concatenate([br[c], pad], axis=0)
            bh = b.astype(BF16).astype(F32)
            bface[c] = jnp.concatenate([bh, bh, b - bh, jnp.zeros_like(bh)], axis=0).T.astype(BF16)
        for s in range(SUBS):
            for place, slot in ((s, ups[s]), (SUBS + s, downs[s])):
                local, inside, outside = place_of(slot)
                b = jnp.concatenate([br[outside], pad], axis=0)
                bh = b.astype(BF16).astype(F32)
                both = jnp.concatenate([bh, b - bh], axis=0).astype(BF16)
                bpart[place] = lax.dot_general(
                    both, perm[slot][:, :E], (((1,), (1,)), ((), ())), preferred_element_type=F32
                ).astype(BF16)

    def put(k, x):
        hi, lo = split(x)
        at = pl.ds(pl.multiple_of(k * E, E), E)
        hh[at, :] = hi
        hl[at, :] = lo

    def local_mul(a_hi, a_lo, out, scale, subs=range(SUBS)):
        def body(s, carry):
            at = pl.ds(pl.multiple_of(s * NI, NI), NI)
            top = hh[at, :]
            acc = dot(a_hi[at, :], top) + dot(a_hi[at, :], hl[at, :]) + dot(a_lo[at, :], top)
            for f in range(FACES):
                k = s * FACES + f
                out[k] = scale(k) * acc[f * E:(f + 1) * E]
            return carry
        lax.fori_loop(subs[0], subs[-1] + 1, body, 0)

    def coarse_load(s):
        sub = pl.ds(s * NI, NI)
        top = hh[sub, :]
        x = dot(bt_hi[s], top) + dot(bt_hi[s], hl[sub, :]) + dot(bt_lo[s], top)
        return x[:NCL]

    def forward_start(n, loads, sums=()):
        for s in range(SUBS):
            xbuf[s * NCL:(s + 1) * NCL, :] = loads[s]
        for i, part in enumerate(sums):
            xbuf[pl.ds(SUBS * NCL + i, 1), :] = part.sum(axis=0, keepdims=True)
        xt[...] = xbuf[...].T
        acc = jnp.zeros((2 * Q, (RR + 1) * LANES), F32)
        for c in range(CG):
            part = xt[pl.ds(c, Q, stride=CG), :]
            hi = part.astype(BF16).astype(F32)
            both = jnp.concatenate([hi, part - hi], axis=0).astype(BF16)
            acc += dot(both, spt[c * LANES:(c + 1) * LANES, :])
        acc = acc[:Q] + acc[Q:]
        b = qb.at[n]
        for r in range(RR + 1):
            b[pl.ds(r, Q, stride=8), :] = acc[:, r * LANES:(r + 1) * LANES]
        q_start(2 + 4 * n, b, qr.at[n])

    def gather_start(n):
        settle(2 + 4 * n, "in")
        for r in range(RR):
            part = qr[n, pl.ds(r, Q, stride=8), :]
            zb[n, r] = part
            zr[n, r, zmine, :] = part
        z_start(
            3 + 4 * n, lambda t: zb.at[n], zr.at[n, :, zmine, :],
            zr.at[n, :, pl.ds(0, (Z - 1) * Q), :],
        )
        if n == 1:
            row = qr[n, pl.ds(RR, Q, stride=8), :].sum(axis=0, keepdims=True)
            row_start(0, row)

    def row_start(i, row):
        row = jnp.broadcast_to(row, (8, LANES))
        eb[i] = row
        er[i, z] = row
        z_start(14 + i, lambda t: eb.at[i], er.at[i, z], er.at[i, pl.ds(0, Z - 1)])

    def row_finish(i):
        settle(14 + i, "in")
        tot = er[i, 0]
        for t in range(1, Z):
            tot = tot + er[i, t]
        return tot

    def gather_wait(n):
        settle(3 + 4 * n, "in")

    def own_step(n):
        tot = row_finish(0)
        below = pltpu.roll(tot, LANES - CG, 1)
        row = jnp.where(lane8 < CG, tot / below, jnp.float32(0.0))
        for shift in (8, 16, 32, 64):
            row = row + pltpu.roll(row, shift, 1)
        return row[0:1]

    def coarse_product(n, step=None):
        la = lax.broadcasted_iota(jnp.int32, (ZQ, LANES), 1) >> 5
        pieces = []
        for r in range(RR):
            part = zr[n, r]
            for a in range(NCF):
                hi, lo = split(jnp.where(la == a, part, jnp.float32(0.0)))
                pieces.append(jnp.concatenate([hi, lo], axis=1))
        slots = jnp.concatenate(pieces, axis=0)
        fa = lax.broadcasted_iota(jnp.int32, (NF, LANES), 1)
        acc = dot(scat[...], slots)
        x = acc[:, :LANES] + acc[:, LANES:]
        x = x + pltpu.roll(x, 64, 1)
        x = x + pltpu.roll(x, 32, 1)
        if step is not None:
            x = xf0[...] - step() * x
        xf0[...] = x
        hi = x.astype(BF16).astype(F32)
        v = jnp.where((fa >> 5) == 0, hi, jnp.where((fa >> 5) == 1, x - hi, jnp.float32(0.0)))
        for j in range(NCF):
            xm[pl.ds(j, NF, stride=NCF), :] = jnp.where(((fa >> 3) & 3) == j, v, jnp.float32(0.0))
        xb[...] = xm[...].astype(BF16)
        kc = NC0 // 7
        acc = jnp.zeros((NCZ, LANES), F32)
        for k in range(7):
            cols = slice(k * kc, (k + 1) * kc)
            acc += dot(c_hi[:, cols], xb[cols, :]) + dot(c_lo[:, cols], xb[cols, :])
        y2[...] = acc
        pieces = []
        for j in range(NCF):
            pieces.extend(split(y2[pl.ds(j, NFZ, stride=NCF), :]))
        y = dot(jnp.concatenate(pieces, axis=1), fold4[...])
        hi, lo = split(y)
        both = jnp.concatenate([hi, lo], axis=1)
        for r in range(RR):
            o = jnp.zeros((ZQ, LANES), F32)
            for a in range(NCF):
                g = dot(gath[NCF * r + a], both)
                o = jnp.where(la == a, g[:, :LANES] + g[:, LANES:], o)
            ob[n, r] = o
        if n == 1:
            mine = xf0[pl.ds(pl.multiple_of(z * NFZ, 8) if NFZ % 8 == 0 else z * NFZ, NFZ), :]
            energy = (mine * y).sum(axis=0, keepdims=True)
            energy = jnp.where(la[0:1] == 0, energy, jnp.float32(0.0))
        zs = (zs0, zs1)[n]
        zs[z] = ob[n, :, zmine, :]
        z_start(
            4 + 4 * n,
            lambda t: ob.at[n, :, pl.ds(pl.multiple_of(t * Q, Q), Q), :],
            zs.at[z],
            zs.at[pl.ds(0, Z - 1)],
        )
        if n == 1:
            row_start(1, energy)

    def backward_start(n):
        zs = (zs0, zs1)[n]
        settle(4 + 4 * n, "in")
        b = qb.at[2 + n]
        for r in range(RR):
            tot = zs[0, r]
            for t in range(1, Z):
                tot = tot + zs[t, r]
            b[pl.ds(r, Q, stride=8), :] = tot
        last = row_finish(1)[0:1] if n == 1 else jnp.zeros((1, LANES), F32)
        b[pl.ds(RR, Q, stride=8), :] = jnp.broadcast_to(last, (Q, LANES))
        q_start(5 + 4 * n, b, qr.at[2 + n])

    def backward_finish(n):
        settle(5 + 4 * n, "in")
        acc = jnp.zeros((2 * Q, CG * LANES), F32)
        for r in range(RR + n):
            part = qr[2 + n, pl.ds(r, Q, stride=8), :]
            hi = part.astype(BF16).astype(F32)
            both = jnp.concatenate([hi, part - hi], axis=0).astype(BF16)
            acc += dot(both, sp[r * LANES:(r + 1) * LANES, :])
        for c in range(CG):
            cols = slice(c * LANES, (c + 1) * LANES)
            yt[pl.ds(c, Q, stride=CG), :] = acc[:Q, cols] + acc[Q:, cols]
        return yt[...].T

    def columns(ys):
        ys = jnp.concatenate([ys, jnp.zeros((32 - NCL, NR), F32)], axis=0)
        hi = ys.astype(BF16).astype(F32)
        return jnp.concatenate([hi, ys - hi, hi, jnp.zeros_like(hi)], axis=0).astype(BF16)

    def share_coarse(n, y):
        for way in range(2):
            ys[n, way] = y[:SUBS * NCL]
        pair_start(6 + n, ys.at[n], yr.at[n], 1)

    def add_coarse(n, y, recv):
        for s in range(SUBS):
            cols = columns(y[s * NCL:(s + 1) * NCL])

            def body(i, carry):
                for j in range(3):
                    f = 3 * i + j
                    k = s * FACES + f
                    at = pl.ds(pl.multiple_of(f * E, E), E)
                    loc[k] = loc[k] + weight_of(k) * dot(bcol[s, at, :], cols)
                return carry
            lax.fori_loop(0, FACES // 3, body, 0)
        halo_wait(6 + n)
        halo_wait(1 + 2 * n)
        halo_wait(8 + n)
        for c in range(2 * SUBS):
            first_row = (c % SUBS) * NCL
            cols = columns(yr[n, c // SUBS, first_row:first_row + NCL, :])
            recv[c] = recv[c] + 0.5 * dot(bface[c], cols)

    def fold(x):
        return x.reshape(E // 8, 8, NR).sum(axis=0)

    nh = max(1, NR // LANES)
    lw = min(NR, LANES)

    def sums_start(n, parts):
        b = arb.at[1 + n]
        b[...] = jnp.zeros((8, LANES), F32)
        for i, part in enumerate(parts):
            line = part.sum(axis=0, keepdims=True)
            for h in range(nh):
                b[pl.ds(i * nh + h, 1), 0:lw] = line[:, h * lw:(h + 1) * lw]
        q_start(10 + 2 * n, b, arr.at[1 + n], shared=True)

    def sums_pass(n):
        settle(10 + 2 * n, "in")
        tot = arr[1 + n].reshape(Q, 8, LANES).sum(axis=0)
        tot = jnp.where(lax.broadcasted_iota(jnp.int32, (8, LANES), 0) < USED, tot, jnp.float32(0.0))
        arb[3 + n] = tot
        arz1[n, z] = tot
        z_start(11 + 2 * n, lambda t: arb.at[3 + n], arz1.at[n, z], arz1.at[n, pl.ds(0, Z - 1)])

    def sums_finish(n):
        settle(11 + 2 * n, "in")
        tot = arz1[n, 0]
        for t in range(1, Z):
            tot = tot + arz1[n, t]
        return tot

    def cases(tile, i):
        return jnp.concatenate([tile[i * nh + h:i * nh + h + 1, :lw] for h in range(nh)], axis=1)

    def over_slots(body, carry):
        def some(i, carry):
            for k in range(STEP):
                carry = body(STEP * i + k, carry)
            return carry
        return lax.fori_loop(0, SLOTS // STEP, some, carry)

    zero8 = jnp.zeros((8, NR), F32)

    halo_wait(0)

    def residual(k, carry):
        r = vld[k] + partner(k, vld, hr0)
        res[k] = r
        put(k, weight_of(k) * r)
        return carry
    over_slots(residual, 0)

    def unscaled(k):
        return jnp.float32(1.0)

    forward_start(0, [coarse_load(s) for s in range(SUBS)])
    local_mul(sinv_hi, sinv_lo, loc, weight_of, (0,))
    half_start(1, 0, loc, hs1, hr1)
    local_mul(sinv_hi, sinv_lo, loc, weight_of, (1,))
    gather_start(0)
    number_tables()
    gather_wait(0)
    half_start(8, 1, loc, hs1, hr1)
    coarse_product(0)
    face_tables()
    convert(schur_copy, s_stage, SUBS * NI // s_rows, s_rows, schur_hi, schur_lo)
    backward_start(0)
    y = backward_finish(0)
    share_coarse(0, y)
    add_coarse(0, y, hr1)

    def direction(k, acc):
        d = loc[k] + partner(k, loc, hr1)
        dirn[k] = d
        put(k, d)
        return acc + fold(weight_of(k) * res[k] * d)
    rz_part = over_slots(direction, zero8)

    local_mul(schur_hi, schur_lo, prod, unscaled)
    for s in range(SUBS):
        for place, slot in ((s, ups[s]), (SUBS + s, downs[s])):
            hi, lo = split(prod[slot])
            b = bpart[place]
            x = dot(b, hi)
            gs[place] = 0.5 * (x[:NCL] + x[32:32 + NCL] + dot(b[:32], lo)[:NCL])
    pair_start(5, gs, gr, SUBS)
    halo_start(2, prod, hs2, hr2)

    def image_here(k, acc):
        m = prod[k]
        put(k, weight_of(k) * (m + partner_here(k, prod)))
        return acc + fold(dirn[k] * m)
    da_part = over_slots(image_here, zero8)

    loads = [coarse_load(s) for s in range(SUBS)]
    halo_wait(5)
    for s in range(SUBS):
        loads[s] = loads[s] + gr[place_of(downs[s])[2]] + gr[place_of(ups[s])[2]]
    forward_start(1, loads, [rz_part, da_part])
    sums_start(0, [rz_part, da_part])
    gather_start(1)
    sums_pass(0)
    gather_wait(1)
    coarse_product(1, lambda: own_step(1))
    tot = sums_finish(0)
    rz = cases(tot, 0)
    alpha = rz / cases(tot, 1)
    halo_wait(2)

    def advance(k, carry):
        m = prod[k] + partner(k, prod, hr2)
        img[k] = m
        r = res[k] - alpha * m
        vld[k] = r
        put(k, weight_of(k) * r)
        return carry
    over_slots(advance, 0)

    local_mul(sinv_hi, sinv_lo, loc, weight_of, (0,))
    half_start(3, 0, loc, hs3, hr3)
    local_mul(sinv_hi, sinv_lo, loc, weight_of, (1,))
    backward_start(1)
    half_start(9, 1, loc, hs3, hr3)

    def energies(k, acc):
        return acc + fold(vld[k] * loc[k])
    sums_start(1, [over_slots(energies, zero8)])
    y = backward_finish(1)
    share_coarse(1, y)
    coarse_energy = y[SUBS * NCL:SUBS * NCL + NCF].sum(axis=0, keepdims=True)
    sums_pass(1)
    add_coarse(1, y, hr3)

    def second(k, carry):
        pre[k] = loc[k] + partner(k, loc, hr3)
        return carry
    over_slots(second, 0)
    out_alpha[...] = alpha
    out_beta[...] = (cases(sums_finish(1), 0) + coarse_energy) / rz

    for wait in list(owed.values()):
        wait()


def one_hot_tables():
    rows = (SLOTS * NCF * CG // LANES + 1) * LANES
    i0 = np.arange(rows)[:, None]
    i1 = np.arange(CG * LANES)[None, :]
    table = i1 == (i0 % CG) * LANES + (i0 // LANES) * (LANES // CG) + i0 % LANES // CG
    m0 = np.arange(2 * NCF * LANES)[:, None]
    m1 = np.arange(LANES)[None, :]
    fold = (m0 % CG == m1 % CG) & (m0 // (2 * LANES) == m1 // CG % NCF)
    return [jnp.asarray(t.astype(np.float32), BF16) for t in (table, table.T, fold)]


def shards(Q, Z, load, schur, schur_inverse, basis, coarse_inverse, partner_slot, edge_map, coarse_number):
    E, NR = load.shape[2], load.shape[3]
    NI = FACES * E
    NCZ, NC0 = coarse_inverse.shape
    NF = NC0 // NCF
    ZQ = Z * Q
    RR = SLOTS * NCF * CG // LANES
    vec = pltpu.VMEM((SLOTS, E, NR), F32)
    halo = pltpu.VMEM((2 * SUBS, E, NR), F32)
    mat = pltpu.VMEM((SUBS * NI, NI), BF16)
    out = pltpu.VMEM((SLOTS, E, NR), F32)
    ratio = pltpu.VMEM((1, NR), F32)
    NCL = FACES * NCF
    anywhere = pl.BlockSpec(memory_space=pl.ANY)
    vmem = pl.BlockSpec(memory_space=pltpu.VMEM)
    smem = pl.BlockSpec(memory_space=pltpu.SMEM)
    direction, residual, image, preconditioned, alpha, beta = pl.pallas_call(
        functools.partial(kernel, Q, Z),
        out_shape=(out, out, out, out, ratio, ratio),
        in_specs=[anywhere, anywhere, anywhere, vmem, anywhere, smem, vmem, smem] + [anywhere] * 3,
        out_specs=(vmem,) * 6,
        scratch_shapes=[vec] * 3 + [halo] * 8 + [mat] * 4 + [
            pltpu.VMEM((NCZ, NC0), BF16),
            pltpu.VMEM((NCZ, NC0), BF16),
            pltpu.VMEM((2, 2 * E, NI), F32),
            pltpu.VMEM((2, NCZ // 7, NC0), F32),
            pltpu.VMEM((SUBS * NI, NR), BF16),
            pltpu.VMEM((SUBS * NI, NR), BF16),
            pltpu.VMEM((SLOTS, E, 2 * E), BF16),
            pltpu.VMEM((SUBS, 32, NI), BF16),
            pltpu.VMEM((SUBS, 32, NI), BF16),
            pltpu.VMEM((SUBS, NI, LANES), BF16),
            pltpu.VMEM((2 * SUBS, E, LANES), BF16),
            pltpu.VMEM((2 * SUBS, 64, E), BF16),
            pltpu.VMEM((2 * SUBS, NCL, E), F32),
            pltpu.VMEM((2 * SUBS, NCL, E), F32),
            pltpu.VMEM((2 * SUBS, NCL, NR), F32),
            pltpu.VMEM((2 * SUBS, NCL, NR), F32),
            pltpu.VMEM((2, 2, SUBS * NCL, NR), F32),
            pltpu.VMEM((2, 2, SUBS * NCL, NR), F32),
            pltpu.VMEM(((RR + 1) * LANES, CG * LANES), BF16),
            pltpu.VMEM((CG * LANES, (RR + 1) * LANES), BF16),
            pltpu.VMEM((2 * NCF * LANES, LANES), BF16),
            pltpu.VMEM((NF, SLOTS * ZQ), BF16),
            pltpu.VMEM((SLOTS, ZQ, NF // Z), BF16),
            pltpu.VMEM((LANES, NR), F32),
            pltpu.VMEM((NR, LANES), F32),
            pltpu.VMEM((NR, LANES), F32),
            pltpu.VMEM((NC0, LANES), F32),
            pltpu.VMEM((NC0, LANES), BF16),
            pltpu.VMEM((NF, LANES), F32),
            pltpu.VMEM((NCZ, LANES), F32),
            pltpu.VMEM((4, Q * 8, LANES), F32),
            pltpu.VMEM((4, Q * 8, LANES), F32),
            pltpu.VMEM((2, RR, Q, LANES), F32),
            pltpu.VMEM((2, RR, ZQ, LANES), F32),
            pltpu.VMEM((2, RR, ZQ, LANES), F32),
            pltpu.VMEM((Z, RR, Q, LANES), F32),
            pltpu.VMEM((Z, RR, Q, LANES), F32),
            pltpu.VMEM((5, 8, LANES), F32),
            pltpu.VMEM((3, Q * 8, LANES), F32),
            pltpu.VMEM((Q, LANES), F32),
            pltpu.VMEM((2, Z, 8, LANES), F32),
            pltpu.VMEM((ZQ, LANES), F32),
            pltpu.SemaphoreType.DMA,
            pltpu.SemaphoreType.DMA((3,)),
            pltpu.SemaphoreType.DMA((2,)),
            pltpu.SemaphoreType.DMA((2,)),
            pltpu.SemaphoreType.DMA((16,)),
            pltpu.SemaphoreType.DMA((16,)),
            pltpu.SemaphoreType.DMA((10, 2)),
            pltpu.SemaphoreType.DMA((10, 2)),
            pltpu.VMEM((2, 8, LANES), F32),
            pltpu.VMEM((2, Z, 8, LANES), F32),
        ],
        compiler_params=pltpu.CompilerParams(
            collective_id=0, has_side_effects=True, vmem_limit_bytes=56 * 1024 * 1024
        ),
    )(
        load.reshape(SLOTS, E, NR),
        schur.reshape(SUBS * NI, NI),
        schur_inverse.reshape(SUBS * NI, NI),
        jnp.swapaxes(basis, 1, 2),
        coarse_inverse,
        partner_slot,
        jnp.swapaxes(edge_map, 0, 1),
        coarse_number,
        *one_hot_tables(),
    )
    return tuple(
        o.reshape(load.shape)
        for o in (alpha * direction, residual - alpha * image, preconditioned + beta * direction)
    )


def solution(mesh):
    both = ("sub", "coarse")
    placed = (
        P(both, None, None, None),
        P(both, None, None),
        P(both, None, None),
        P(both, None, None),
        P("coarse", None),
        P(both, None),
        P(both, None, None),
        P(both, None),
    )
    return jax.shard_map(
        functools.partial(shards, mesh.shape["sub"], mesh.shape["coarse"]),
        mesh=mesh,
        in_specs=placed,
        out_specs=(P(both, None, None, None),) * 3,
        check_vma=False,
    )
```

```python
import functools

import jax
import jax.numpy as jnp
import numpy as np
from jax import lax
from jax.experimental import pallas as pl
from jax.experimental.pallas import tpu as pltpu
from jax.sharding import PartitionSpec as P

MESH = pl.DeviceIdType.MESH
F32 = jnp.float32
BF16 = jnp.bfloat16
FACES = 6
SUBS = 2
SLOTS = FACES * SUBS
NCF = 4
LANES = 128
STEP = 6
USED = 4
CG = 8


def split(x):
    hi = x.astype(BF16)
    return hi, (x - hi.astype(F32)).astype(BF16)


def dot(a, b):
    return jnp.dot(a, b, preferred_element_type=F32)


def kernel(
    Q, Z, load, schur, sinv, basis_t, coarse, ps, em, cn, sp_in, spt_in, fold4_in,
    dirn, res, img, pre, out_alpha, out_beta,
    vld, loc, prod,
    hs0, hs1, hs2, hs3, hr0, hr1, hr2, hr3,
    sinv_hi, sinv_lo, schur_hi, schur_lo, c_hi, c_lo, s_stage, c_stage,
    hh, hl, perm, bt_hi, bt_lo, bcol, bface, bpart, bs, br, gs, gr, ys, yr, sp, spt,
    fold4, scat, gath, xbuf, xt, yt, xm, xb, xf0, y2,
    qb, qr, zb, zr, ob, zs0, zs1, arb, arr, arz0, arz1, cnz,
    in_sem, tab_sem, st_sem, ct_sem, q_send, q_recv, h_send, h_recv, eb, er,
):
    q = lax.axis_index("sub")
    z = lax.axis_index("coarse")
    E = vld.shape[1]
    NR = vld.shape[2]
    ZQ = Z * Q
    NCZ = c_hi.shape[0]
    NC0 = c_hi.shape[1]
    NF = NC0 // NCF
    NFZ = NF // Z
    RR = SLOTS * NCF * CG // LANES
    ndev = Q * Z
    me = q * Z + z
    nxt = lax.rem(me + 1, ndev)
    prv = lax.rem(me + ndev - 1, ndev)
    nxt_id = (nxt // Z, lax.rem(nxt, Z))
    prv_id = (prv // Z, lax.rem(prv, Z))

    def q_peer(k):
        return lax.rem(q + k, Q)

    def z_peer(k):
        return lax.rem(z + k, Z)

    owed = {}

    def owe(key, ref, sem):
        owed[key] = lambda: pltpu.make_async_copy(ref, ref, sem).wait()

    def settle(*key):
        owed.pop(key)()

    load_copy = pltpu.make_async_copy(load, vld, in_sem)
    load_copy.start()

    def stager(src, rows, stage, sem):
        def copy(i, slot):
            return pltpu.make_async_copy(
                src.at[pl.ds(pl.multiple_of(i * rows, rows), rows), :], stage.at[slot], sem.at[slot]
            )
        return copy

    s_rows = s_stage.shape[1]
    c_rows = c_stage.shape[1]
    sinv_copy = stager(sinv, s_rows, s_stage, st_sem)
    schur_copy = stager(schur, s_rows, s_stage, st_sem)
    c_copy = stager(coarse, c_rows, c_stage, ct_sem)

    def first(copy):
        copy(0, 0).start()
        copy(1, 1).start()
        owed[copy] = lambda: (copy(0, 0).wait(), copy(1, 1).wait())

    def convert(copy, stage, n, rows, hi_ref, lo_ref):
        def body(i, carry):
            slot = lax.rem(i, 2)
            copy(i, slot).wait()
            hi, lo = split(stage[slot])
            at = pl.ds(pl.multiple_of(i * rows, rows), rows)
            hi_ref[at, :] = hi
            lo_ref[at, :] = lo

            @pl.when(i + 2 < n)
            def _():
                copy(i + 2, slot).start()
            return carry
        lax.fori_loop(0, n, body, 0)
        owed.pop(copy)

    first(sinv_copy)
    first(c_copy)
    tables = [
        pltpu.make_async_copy(src, dst, tab_sem.at[i])
        for i, (src, dst) in enumerate(((sp_in, sp), (spt_in, spt), (fold4_in, fold4)))
    ]
    for copy in tables:
        copy.start()

    barrier = pltpu.get_barrier_semaphore()

    def greet(device):
        pl.semaphore_signal(barrier, inc=1, device_id=device, device_id_type=MESH)

    lax.fori_loop(1, Q, lambda k, c: (greet((q_peer(k), z)), c)[1], 0)
    for k in range(1, Z):
        greet((q, z_peer(k)))
    greet(nxt_id)
    greet(prv_id)

    lane8 = lax.broadcasted_iota(jnp.int32, (8, LANES), 1)

    def far(k):
        x, y = k // 8, k // 2 % 4
        return min(x, 4 - x) + min(y, 4 - y)

    def q_start(ph, src, dst, shared=False):
        def body(k, carry):
            p = q_peer(k)
            block = src.at[pl.ds(0 if shared else pl.multiple_of(p * 8, 8), USED), :]
            pltpu.make_async_remote_copy(
                src_ref=block,
                dst_ref=dst.at[pl.ds(pl.multiple_of(q * 8, 8), USED), :],
                send_sem=q_send.at[ph], recv_sem=q_recv.at[ph],
                device_id=(p, z), device_id_type=MESH,
            ).start()
            return carry
        if shared:
            lax.fori_loop(1, Q, body, 0)
        else:
            for k in sorted(range(1, Q), key=lambda k: -far(k)):
                body(k, 0)
        mine = pl.ds(pl.multiple_of(q * 8, 8), USED)
        dst[mine, :] = src[0:USED, :] if shared else src[mine, :]
        every = dst.at[pl.ds(0, (Q - 1) * USED), :]
        owe((ph, "in"), every, q_recv.at[ph])
        owe((ph, "out"), every, q_send.at[ph])

    def z_start(ph, src_of, dst, three):
        for k in sorted(range(1, Z), key=lambda k: -min(k, Z - k)):
            t = z_peer(k)
            pltpu.make_async_remote_copy(
                src_ref=src_of(t), dst_ref=dst,
                send_sem=q_send.at[ph], recv_sem=q_recv.at[ph],
                device_id=(q, t), device_id_type=MESH,
            ).start()
        owe((ph, "in"), three, q_recv.at[ph])
        owe((ph, "out"), three, q_send.at[ph])

    def rel_of(k):
        p = ps[k // FACES, lax.rem(k, FACES)]
        rel = p - me * SLOTS
        rel = jnp.where(rel < -SLOTS, rel + ndev * SLOTS, rel)
        rel = jnp.where(rel >= 2 * SLOTS, rel - ndev * SLOTS, rel)
        return p, rel

    def weight_of(k):
        return jnp.where(ps[k // FACES, lax.rem(k, FACES)] >= 0, jnp.float32(0.5), jnp.float32(1.0))

    ups, downs = [], []
    for s in range(SUBS):
        up = jnp.int32(0)
        down = jnp.int32(0)
        for f in range(FACES):
            p, rel = rel_of(s * FACES + f)
            here = p >= 0
            up = jnp.where(here & (rel >= SLOTS), s * FACES + f, up)
            down = jnp.where(here & (rel < 0), s * FACES + f, down)
        ups.append(up)
        downs.append(down)

    def pair_start(h, send, recv, count):
        for way, device in ((0, nxt_id), (1, prv_id)):
            part = pl.ds(way * count, count)
            pltpu.make_async_remote_copy(
                src_ref=send.at[part], dst_ref=recv.at[part],
                send_sem=h_send.at[h, way], recv_sem=h_recv.at[h, way],
                device_id=device, device_id_type=MESH,
            ).start()
            owe((h, way, "halo in"), recv.at[part], h_recv.at[h, way])
            owe((h, way, "halo out"), recv.at[part], h_send.at[h, way])

    def halo_start(h, v, send, recv):
        for s in range(SUBS):
            send[s] = v[ups[s]]
            send[SUBS + s] = v[downs[s]]
        pair_start(h, send, recv, SUBS)

    def half_start(h, s, v, send, recv):
        for way, slot, device in ((0, ups[s], nxt_id), (1, downs[s], prv_id)):
            place = way * SUBS + s
            send[place] = v[slot]
            part = pl.ds(place, 1)
            pltpu.make_async_remote_copy(
                src_ref=send.at[part], dst_ref=recv.at[part],
                send_sem=h_send.at[h, way], recv_sem=h_recv.at[h, way],
                device_id=device, device_id_type=MESH,
            ).start()
            owe((h, way, "halo in"), recv.at[part], h_recv.at[h, way])
            owe((h, way, "halo out"), recv.at[part], h_send.at[h, way])

    def halo_wait(h):
        settle(h, 0, "halo in")
        settle(h, 1, "halo in")

    def place_of(k):
        p, rel = rel_of(k)
        local = (rel >= 0) & (rel < SLOTS)
        inside = jnp.clip(rel, 0, SLOTS - 1)
        below = (rel + SLOTS >= FACES).astype(jnp.int32)
        above = SUBS + (rel - SLOTS >= FACES).astype(jnp.int32)
        return local, inside, jnp.clip(jnp.where(rel < 0, below, above), 0, 2 * SUBS - 1)

    def permute(k, val):
        hi, lo = split(val)
        return dot(perm[k], jnp.concatenate([hi, lo], axis=0))

    def partner(k, v, recv):
        local, inside, outside = place_of(k)
        return permute(k, jnp.where(local, v[inside], recv[outside]))

    def partner_here(k, v):
        local, inside, outside = place_of(k)
        return permute(k, jnp.where(local, v[inside], jnp.float32(0.0)))

    rows_e = lax.broadcasted_iota(jnp.int32, (E, E), 0)
    for k in range(SLOTS):
        line = em[k % FACES, pl.ds(k // FACES, 1), :]
        one = jnp.where(rows_e == line, jnp.float32(1.0), jnp.float32(0.0)).T
        one = jnp.where(ps[k // FACES, k % FACES] >= 0, one, jnp.zeros_like(one)).astype(BF16)
        perm[k] = jnp.concatenate([one, one], axis=1)

    NI = FACES * E
    NCL = FACES * NCF
    convert(sinv_copy, s_stage, SUBS * NI // s_rows, s_rows, sinv_hi, sinv_lo)
    first(schur_copy)
    load_copy.wait()
    pl.semaphore_wait(barrier, Q + Z)
    halo_start(0, vld, hs0, hr0)

    row = jnp.zeros((8, LANES), F32)
    for k in range(SLOTS):
        row = jnp.where(lane8 == k, cn[k // FACES, k % FACES].astype(F32), row)
    arb[0] = row
    q_start(0, arb.at[0], arr.at[0], shared=True)

    for s in range(SUBS):
        for place, slot in ((s, ups[s]), (SUBS + s, downs[s])):
            face = jnp.zeros((NCL, E), F32)
            for f in range(FACES):
                face = jnp.where(slot == s * FACES + f, basis_t[s, :, f * E:(f + 1) * E], face)
            bs[place] = face
    pair_start(4, bs, br, SUBS)

    zrow = jnp.zeros((32 - NCL, NI), F32)
    for s in range(SUBS):
        b = basis_t[s]
        bh = b.astype(BF16).astype(F32)
        bl = b - bh
        bh = jnp.concatenate([bh, zrow], axis=0)
        bl = jnp.concatenate([bl, zrow], axis=0)
        bt_hi[s] = bh.astype(BF16)
        bt_lo[s] = bl.astype(BF16)
        bcol[s] = jnp.concatenate([bh, bh, bl, jnp.zeros_like(bl)], axis=0).T.astype(BF16)

    xbuf[...] = jnp.zeros_like(xbuf)

    convert(c_copy, c_stage, NCZ // c_rows, c_rows, c_hi, c_lo)
    for copy in tables:
        copy.wait()

    settle(0, "in")
    zmine = pl.ds(pl.multiple_of(z * Q, Q), Q)
    arz0[...] = arr[0, pl.ds(0, Q, stride=8), :]
    cnz[zmine, :] = arz0[...]
    z_start(1, lambda t: arz0, cnz.at[zmine, :], cnz.at[pl.ds(0, (Z - 1) * Q), :])

    def number_tables():
        settle(1, "in")
        cns = cnz[...]
        cnt = cns.T if ZQ == LANES else jnp.concatenate([cns, jnp.zeros((LANES - ZQ, LANES), F32)], axis=0).T
        face0 = lax.broadcasted_iota(jnp.int32, (NF, ZQ), 0).astype(F32)
        face1 = lax.broadcasted_iota(jnp.int32, (ZQ, NFZ), 1).astype(F32) + (z * NFZ).astype(F32)
        for k in range(SLOTS):
            scat[:, k * ZQ:(k + 1) * ZQ] = jnp.where(
                face0 == cnt[k:k + 1, :ZQ], jnp.float32(1.0), jnp.float32(0.0)
            ).astype(BF16)
            gath[k] = jnp.where(
                cns[:, k:k + 1] == face1, jnp.float32(1.0), jnp.float32(0.0)
            ).astype(BF16)

    def face_tables():
        settle(4, 0, "halo in")
        settle(4, 1, "halo in")
        pad = jnp.zeros((32 - NCL, E), F32)
        for c in range(2 * SUBS):
            b = jnp.concatenate([br[c], pad], axis=0)
            bh = b.astype(BF16).astype(F32)
            bface[c] = jnp.concatenate([bh, bh, b - bh, jnp.zeros_like(bh)], axis=0).T.astype(BF16)
        for s in range(SUBS):
            for place, slot in ((s, ups[s]), (SUBS + s, downs[s])):
                local, inside, outside = place_of(slot)
                b = jnp.concatenate([br[outside], pad], axis=0)
                bh = b.astype(BF16).astype(F32)
                both = jnp.concatenate([bh, b - bh], axis=0).astype(BF16)
                bpart[place] = lax.dot_general(
                    both, perm[slot][:, :E], (((1,), (1,)), ((), ())), preferred_element_type=F32
                ).astype(BF16)

    def put(k, x):
        hi, lo = split(x)
        at = pl.ds(pl.multiple_of(k * E, E), E)
        hh[at, :] = hi
        hl[at, :] = lo

    def local_mul(a_hi, a_lo, out, scale, subs=range(SUBS)):
        def body(s, carry):
            at = pl.ds(pl.multiple_of(s * NI, NI), NI)
            top = hh[at, :]
            acc = dot(a_hi[at, :], top) + dot(a_hi[at, :], hl[at, :]) + dot(a_lo[at, :], top)
            for f in range(FACES):
                k = s * FACES + f
                out[k] = scale(k) * acc[f * E:(f + 1) * E]
            return carry
        lax.fori_loop(subs[0], subs[-1] + 1, body, 0)

    def coarse_load(s):
        sub = pl.ds(s * NI, NI)
        top = hh[sub, :]
        x = dot(bt_hi[s], top) + dot(bt_hi[s], hl[sub, :]) + dot(bt_lo[s], top)
        return x[:NCL]

    def forward_start(n, loads, sums=()):
        for s in range(SUBS):
            xbuf[s * NCL:(s + 1) * NCL, :] = loads[s]
        for i, part in enumerate(sums):
            xbuf[pl.ds(SUBS * NCL + i, 1), :] = part.sum(axis=0, keepdims=True)
        xt[...] = xbuf[...].T
        acc = jnp.zeros((2 * Q, (RR + 1) * LANES), F32)
        for c in range(CG):
            part = xt[pl.ds(c, Q, stride=CG), :]
            hi = part.astype(BF16).astype(F32)
            both = jnp.concatenate([hi, part - hi], axis=0).astype(BF16)
            acc += dot(both, spt[c * LANES:(c + 1) * LANES, :])
        acc = acc[:Q] + acc[Q:]
        b = qb.at[n]
        for r in range(RR + 1):
            b[pl.ds(r, Q, stride=8), :] = acc[:, r * LANES:(r + 1) * LANES]
        q_start(2 + 4 * n, b, qr.at[n])

    def gather_start(n):
        settle(2 + 4 * n, "in")
        for r in range(RR):
            part = qr[n, pl.ds(r, Q, stride=8), :]
            zb[n, r] = part
            zr[n, r, zmine, :] = part
        z_start(
            3 + 4 * n, lambda t: zb.at[n], zr.at[n, :, zmine, :],
            zr.at[n, :, pl.ds(0, (Z - 1) * Q), :],
        )
        if n == 1:
            row = qr[n, pl.ds(RR, Q, stride=8), :].sum(axis=0, keepdims=True)
            row_start(0, row)

    def row_start(i, row):
        row = jnp.broadcast_to(row, (8, LANES))
        eb[i] = row
        er[i, z] = row
        z_start(14 + i, lambda t: eb.at[i], er.at[i, z], er.at[i, pl.ds(0, Z - 1)])

    def row_finish(i):
        settle(14 + i, "in")
        tot = er[i, 0]
        for t in range(1, Z):
            tot = tot + er[i, t]
        return tot

    def gather_wait(n):
        settle(3 + 4 * n, "in")

    def own_step(n):
        tot = row_finish(0)
        below = pltpu.roll(tot, LANES - CG, 1)
        row = jnp.where(lane8 < CG, tot / below, jnp.float32(0.0))
        for shift in (8, 16, 32, 64):
            row = row + pltpu.roll(row, shift, 1)
        return row[0:1]

    def coarse_product(n, step=None):
        la = lax.broadcasted_iota(jnp.int32, (ZQ, LANES), 1) >> 5
        pieces = []
        for r in range(RR):
            part = zr[n, r]
            for a in range(NCF):
                hi, lo = split(jnp.where(la == a, part, jnp.float32(0.0)))
                pieces.append(jnp.concatenate([hi, lo], axis=1))
        slots = jnp.concatenate(pieces, axis=0)
        fa = lax.broadcasted_iota(jnp.int32, (NF, LANES), 1)
        acc = dot(scat[...], slots)
        x = acc[:, :LANES] + acc[:, LANES:]
        x = x + pltpu.roll(x, 64, 1)
        x = x + pltpu.roll(x, 32, 1)
        if step is not None:
            x = xf0[...] - step() * x
        xf0[...] = x
        hi = x.astype(BF16).astype(F32)
        v = jnp.where((fa >> 5) == 0, hi, jnp.where((fa >> 5) == 1, x - hi, jnp.float32(0.0)))
        for j in range(NCF):
            xm[pl.ds(j, NF, stride=NCF), :] = jnp.where(((fa >> 3) & 3) == j, v, jnp.float32(0.0))
        xb[...] = xm[...].astype(BF16)
        kc = NC0 // 7
        acc = jnp.zeros((NCZ, LANES), F32)
        for k in range(7):
            cols = slice(k * kc, (k + 1) * kc)
            acc += dot(c_hi[:, cols], xb[cols, :]) + dot(c_lo[:, cols], xb[cols, :])
        y2[...] = acc
        pieces = []
        for j in range(NCF):
            pieces.extend(split(y2[pl.ds(j, NFZ, stride=NCF), :]))
        y = dot(jnp.concatenate(pieces, axis=1), fold4[...])
        hi, lo = split(y)
        both = jnp.concatenate([hi, lo], axis=1)
        for r in range(RR):
            o = jnp.zeros((ZQ, LANES), F32)
            for a in range(NCF):
                g = dot(gath[NCF * r + a], both)
                o = jnp.where(la == a, g[:, :LANES] + g[:, LANES:], o)
            ob[n, r] = o
        if n == 1:
            mine = xf0[pl.ds(pl.multiple_of(z * NFZ, 8) if NFZ % 8 == 0 else z * NFZ, NFZ), :]
            energy = (mine * y).sum(axis=0, keepdims=True)
            energy = jnp.where(la[0:1] == 0, energy, jnp.float32(0.0))
        zs = (zs0, zs1)[n]
        zs[z] = ob[n, :, zmine, :]
        z_start(
            4 + 4 * n,
            lambda t: ob.at[n, :, pl.ds(pl.multiple_of(t * Q, Q), Q), :],
            zs.at[z],
            zs.at[pl.ds(0, Z - 1)],
        )
        if n == 1:
            row_start(1, energy)

    def backward_start(n):
        zs = (zs0, zs1)[n]
        settle(4 + 4 * n, "in")
        b = qb.at[2 + n]
        for r in range(RR):
            tot = zs[0, r]
            for t in range(1, Z):
                tot = tot + zs[t, r]
            b[pl.ds(r, Q, stride=8), :] = tot
        last = row_finish(1)[0:1] if n == 1 else jnp.zeros((1, LANES), F32)
        b[pl.ds(RR, Q, stride=8), :] = jnp.broadcast_to(last, (Q, LANES))
        q_start(5 + 4 * n, b, qr.at[2 + n])

    def backward_finish(n):
        settle(5 + 4 * n, "in")
        acc = jnp.zeros((2 * Q, CG * LANES), F32)
        for r in range(RR + n):
            part = qr[2 + n, pl.ds(r, Q, stride=8), :]
            hi = part.astype(BF16).astype(F32)
            both = jnp.concatenate([hi, part - hi], axis=0).astype(BF16)
            acc += dot(both, sp[r * LANES:(r + 1) * LANES, :])
        for c in range(CG):
            cols = slice(c * LANES, (c + 1) * LANES)
            yt[pl.ds(c, Q, stride=CG), :] = acc[:Q, cols] + acc[Q:, cols]
        return yt[...].T

    def columns(ys):
        ys = jnp.concatenate([ys, jnp.zeros((32 - NCL, NR), F32)], axis=0)
        hi = ys.astype(BF16).astype(F32)
        return jnp.concatenate([hi, ys - hi, hi, jnp.zeros_like(hi)], axis=0).astype(BF16)

    def share_coarse(n, y):
        for way in range(2):
            ys[n, way] = y[:SUBS * NCL]
        pair_start(6 + n, ys.at[n], yr.at[n], 1)

    def add_coarse(n, y, recv):
        for s in range(SUBS):
            cols = columns(y[s * NCL:(s + 1) * NCL])

            def body(i, carry):
                for j in range(3):
                    f = 3 * i + j
                    k = s * FACES + f
                    at = pl.ds(pl.multiple_of(f * E, E), E)
                    loc[k] = loc[k] + weight_of(k) * dot(bcol[s, at, :], cols)
                return carry
            lax.fori_loop(0, FACES // 3, body, 0)
        halo_wait(6 + n)
        halo_wait(1 + 2 * n)
        halo_wait(8 + n)
        for c in range(2 * SUBS):
            first_row = (c % SUBS) * NCL
            cols = columns(yr[n, c // SUBS, first_row:first_row + NCL, :])
            recv[c] = recv[c] + 0.5 * dot(bface[c], cols)

    def fold(x):
        return x.reshape(E // 8, 8, NR).sum(axis=0)

    nh = max(1, NR // LANES)
    lw = min(NR, LANES)

    def sums_start(n, parts):
        b = arb.at[1 + n]
        b[...] = jnp.zeros((8, LANES), F32)
        for i, part in enumerate(parts):
            line = part.sum(axis=0, keepdims=True)
            for h in range(nh):
                b[pl.ds(i * nh + h, 1), 0:lw] = line[:, h * lw:(h + 1) * lw]
        q_start(10 + 2 * n, b, arr.at[1 + n], shared=True)

    def sums_pass(n):
        settle(10 + 2 * n, "in")
        tot = arr[1 + n].reshape(Q, 8, LANES).sum(axis=0)
        tot = jnp.where(lax.broadcasted_iota(jnp.int32, (8, LANES), 0) < USED, tot, jnp.float32(0.0))
        arb[3 + n] = tot
        arz1[n, z] = tot
        z_start(11 + 2 * n, lambda t: arb.at[3 + n], arz1.at[n, z], arz1.at[n, pl.ds(0, Z - 1)])

    def sums_finish(n):
        settle(11 + 2 * n, "in")
        tot = arz1[n, 0]
        for t in range(1, Z):
            tot = tot + arz1[n, t]
        return tot

    def cases(tile, i):
        return jnp.concatenate([tile[i * nh + h:i * nh + h + 1, :lw] for h in range(nh)], axis=1)

    def over_slots(body, carry):
        def some(i, carry):
            for k in range(STEP):
                carry = body(STEP * i + k, carry)
            return carry
        return lax.fori_loop(0, SLOTS // STEP, some, carry)

    zero8 = jnp.zeros((8, NR), F32)

    halo_wait(0)

    def residual(k, carry):
        r = vld[k] + partner(k, vld, hr0)
        res[k] = r
        put(k, weight_of(k) * r)
        return carry
    over_slots(residual, 0)

    def unscaled(k):
        return jnp.float32(1.0)

    forward_start(0, [coarse_load(s) for s in range(SUBS)])
    local_mul(sinv_hi, sinv_lo, loc, weight_of, (0,))
    half_start(1, 0, loc, hs1, hr1)
    local_mul(sinv_hi, sinv_lo, loc, weight_of, (1,))
    gather_start(0)
    number_tables()
    gather_wait(0)
    half_start(8, 1, loc, hs1, hr1)
    coarse_product(0)
    face_tables()
    convert(schur_copy, s_stage, SUBS * NI // s_rows, s_rows, schur_hi, schur_lo)
    backward_start(0)
    y = backward_finish(0)
    share_coarse(0, y)
    add_coarse(0, y, hr1)

    def direction(k, acc):
        d = loc[k] + partner(k, loc, hr1)
        dirn[k] = d
        put(k, d)
        return acc + fold(weight_of(k) * res[k] * d)
    rz_part = over_slots(direction, zero8)

    local_mul(schur_hi, schur_lo, prod, unscaled)
    for s in range(SUBS):
        for place, slot in ((s, ups[s]), (SUBS + s, downs[s])):
            hi, lo = split(prod[slot])
            b = bpart[place]
            x = dot(b, hi)
            gs[place] = 0.5 * (x[:NCL] + x[32:32 + NCL] + dot(b[:32], lo)[:NCL])
    pair_start(5, gs, gr, SUBS)

    def image_here(k, acc):
        m = prod[k]
        put(k, weight_of(k) * (m + partner_here(k, prod)))
        return acc + fold(dirn[k] * m)
    da_part = over_slots(image_here, zero8)

    loads = [coarse_load(s) for s in range(SUBS)]
    halo_wait(5)
    for s in range(SUBS):
        loads[s] = loads[s] + gr[place_of(downs[s])[2]] + gr[place_of(ups[s])[2]]
    forward_start(1, loads, [rz_part, da_part])
    halo_start(2, prod, hs2, hr2)
    sums_start(0, [rz_part, da_part])
    gather_start(1)
    sums_pass(0)
    gather_wait(1)
    coarse_product(1, lambda: own_step(1))
    tot = sums_finish(0)
    rz = cases(tot, 0)
    alpha = rz / cases(tot, 1)
    halo_wait(2)

    def advance(k, carry):
        m = prod[k] + partner(k, prod, hr2)
        img[k] = m
        r = res[k] - alpha * m
        vld[k] = r
        put(k, weight_of(k) * r)
        return carry
    over_slots(advance, 0)

    local_mul(sinv_hi, sinv_lo, loc, weight_of, (0,))
    half_start(3, 0, loc, hs3, hr3)
    local_mul(sinv_hi, sinv_lo, loc, weight_of, (1,))
    backward_start(1)
    half_start(9, 1, loc, hs3, hr3)

    def energies(k, acc):
        return acc + fold(vld[k] * loc[k])
    sums_start(1, [over_slots(energies, zero8)])
    y = backward_finish(1)
    share_coarse(1, y)
    coarse_energy = y[SUBS * NCL:SUBS * NCL + NCF].sum(axis=0, keepdims=True)
    sums_pass(1)
    add_coarse(1, y, hr3)

    def second(k, carry):
        pre[k] = loc[k] + partner(k, loc, hr3)
        return carry
    over_slots(second, 0)
    out_alpha[...] = alpha
    out_beta[...] = (cases(sums_finish(1), 0) + coarse_energy) / rz

    for wait in list(owed.values()):
        wait()


def one_hot_tables():
    rows = (SLOTS * NCF * CG // LANES + 1) * LANES
    i0 = np.arange(rows)[:, None]
    i1 = np.arange(CG * LANES)[None, :]
    table = i1 == (i0 % CG) * LANES + (i0 // LANES) * (LANES // CG) + i0 % LANES // CG
    m0 = np.arange(2 * NCF * LANES)[:, None]
    m1 = np.arange(LANES)[None, :]
    fold = (m0 % CG == m1 % CG) & (m0 // (2 * LANES) == m1 // CG % NCF)
    return [jnp.asarray(t.astype(np.float32), BF16) for t in (table, table.T, fold)]


def shards(Q, Z, load, schur, schur_inverse, basis, coarse_inverse, partner_slot, edge_map, coarse_number):
    E, NR = load.shape[2], load.shape[3]
    NI = FACES * E
    NCZ, NC0 = coarse_inverse.shape
    NF = NC0 // NCF
    ZQ = Z * Q
    RR = SLOTS * NCF * CG // LANES
    vec = pltpu.VMEM((SLOTS, E, NR), F32)
    halo = pltpu.VMEM((2 * SUBS, E, NR), F32)
    mat = pltpu.VMEM((SUBS * NI, NI), BF16)
    out = pltpu.VMEM((SLOTS, E, NR), F32)
    ratio = pltpu.VMEM((1, NR), F32)
    NCL = FACES * NCF
    anywhere = pl.BlockSpec(memory_space=pl.ANY)
    vmem = pl.BlockSpec(memory_space=pltpu.VMEM)
    smem = pl.BlockSpec(memory_space=pltpu.SMEM)
    direction, residual, image, preconditioned, alpha, beta = pl.pallas_call(
        functools.partial(kernel, Q, Z),
        out_shape=(out, out, out, out, ratio, ratio),
        in_specs=[anywhere, anywhere, anywhere, vmem, anywhere, smem, vmem, smem] + [anywhere] * 3,
        out_specs=(vmem,) * 6,
        scratch_shapes=[vec] * 3 + [halo] * 8 + [mat] * 4 + [
            pltpu.VMEM((NCZ, NC0), BF16),
            pltpu.VMEM((NCZ, NC0), BF16),
            pltpu.VMEM((2, 2 * E, NI), F32),
            pltpu.VMEM((2, NCZ // 7, NC0), F32),
            pltpu.VMEM((SUBS * NI, NR), BF16),
            pltpu.VMEM((SUBS * NI, NR), BF16),
            pltpu.VMEM((SLOTS, E, 2 * E), BF16),
            pltpu.VMEM((SUBS, 32, NI), BF16),
            pltpu.VMEM((SUBS, 32, NI), BF16),
            pltpu.VMEM((SUBS, NI, LANES), BF16),
            pltpu.VMEM((2 * SUBS, E, LANES), BF16),
            pltpu.VMEM((2 * SUBS, 64, E), BF16),
            pltpu.VMEM((2 * SUBS, NCL, E), F32),
            pltpu.VMEM((2 * SUBS, NCL, E), F32),
            pltpu.VMEM((2 * SUBS, NCL, NR), F32),
            pltpu.VMEM((2 * SUBS, NCL, NR), F32),
            pltpu.VMEM((2, 2, SUBS * NCL, NR), F32),
            pltpu.VMEM((2, 2, SUBS * NCL, NR), F32),
            pltpu.VMEM(((RR + 1) * LANES, CG * LANES), BF16),
            pltpu.VMEM((CG * LANES, (RR + 1) * LANES), BF16),
            pltpu.VMEM((2 * NCF * LANES, LANES), BF16),
            pltpu.VMEM((NF, SLOTS * ZQ), BF16),
            pltpu.VMEM((SLOTS, ZQ, NF // Z), BF16),
            pltpu.VMEM((LANES, NR), F32),
            pltpu.VMEM((NR, LANES), F32),
            pltpu.VMEM((NR, LANES), F32),
            pltpu.VMEM((NC0, LANES), F32),
            pltpu.VMEM((NC0, LANES), BF16),
            pltpu.VMEM((NF, LANES), F32),
            pltpu.VMEM((NCZ, LANES), F32),
            pltpu.VMEM((4, Q * 8, LANES), F32),
            pltpu.VMEM((4, Q * 8, LANES), F32),
            pltpu.VMEM((2, RR, Q, LANES), F32),
            pltpu.VMEM((2, RR, ZQ, LANES), F32),
            pltpu.VMEM((2, RR, ZQ, LANES), F32),
            pltpu.VMEM((Z, RR, Q, LANES), F32),
            pltpu.VMEM((Z, RR, Q, LANES), F32),
            pltpu.VMEM((5, 8, LANES), F32),
            pltpu.VMEM((3, Q * 8, LANES), F32),
            pltpu.VMEM((Q, LANES), F32),
            pltpu.VMEM((2, Z, 8, LANES), F32),
            pltpu.VMEM((ZQ, LANES), F32),
            pltpu.SemaphoreType.DMA,
            pltpu.SemaphoreType.DMA((3,)),
            pltpu.SemaphoreType.DMA((2,)),
            pltpu.SemaphoreType.DMA((2,)),
            pltpu.SemaphoreType.DMA((16,)),
            pltpu.SemaphoreType.DMA((16,)),
            pltpu.SemaphoreType.DMA((10, 2)),
            pltpu.SemaphoreType.DMA((10, 2)),
            pltpu.VMEM((2, 8, LANES), F32),
            pltpu.VMEM((2, Z, 8, LANES), F32),
        ],
        compiler_params=pltpu.CompilerParams(
            collective_id=0, has_side_effects=True, vmem_limit_bytes=56 * 1024 * 1024
        ),
    )(
        load.reshape(SLOTS, E, NR),
        schur.reshape(SUBS * NI, NI),
        schur_inverse.reshape(SUBS * NI, NI),
        jnp.swapaxes(basis, 1, 2),
        coarse_inverse,
        partner_slot,
        jnp.swapaxes(edge_map, 0, 1),
        coarse_number,
        *one_hot_tables(),
    )
    return tuple(
        o.reshape(load.shape)
        for o in (alpha * direction, residual - alpha * image, preconditioned + beta * direction)
    )


def solution(mesh):
    both = ("sub", "coarse")
    placed = (
        P(both, None, None, None),
        P(both, None, None),
        P(both, None, None),
        P(both, None, None),
        P("coarse", None),
        P(both, None),
        P(both, None, None),
        P(both, None),
    )
    return jax.shard_map(
        functools.partial(shards, mesh.shape["sub"], mesh.shape["coarse"]),
        mesh=mesh,
        in_specs=placed,
        out_specs=(P(both, None, None, None),) * 3,
        check_vma=False,
    )
```
